128 devices in a mesh: dp: 16 (over z, x_hi, core), tensor: 8 (over x_lo, y).
Axes of the slice: x: 4 (x_hi: 2, x_lo: 2; x = x_hi * 2 + x_lo), y: 4, z: 4, core: 2. Of those that a mesh axis runs over, the one named last changes fastest.
Arguments:
- inputs: float32 [32768, 1024], P(('dp', 'tensor')), may hold values from -6 to 6
- lengths: int32 [16, 4], P('dp'), may hold values from 1 to 1024, 2048 in all within a row
- ln1_gain: float32 [1024], replicated, may hold values from 0.1 to 1.9
- ln1_bias: float32 [1024], replicated, may hold values from -1.75 to 1.75
- ln2_gain: float32 [1024], replicated, may hold values from 0.1 to 1.9
- ln2_bias: float32 [1024], replicated, may hold values from -1.75 to 1.75
- w_query: float32 [1024, 1024], P('dp', 'tensor'), may hold values from -0.1875 to 0.1875
- w_key: float32 [1024, 1024], P('dp', 'tensor'), may hold values from -0.1875 to 0.1875
- w_value: float32 [1024, 1024], P('dp', 'tensor'), may hold values from -0.1875 to 0.1875
- w_out: float32 [1024, 1024], P('tensor', 'dp'), may hold values from -1.5 to 1.5
- w_up: float32 [1024, 4096], P('dp', 'tensor'), may hold values from -0.1875 to 0.1875
- w_down: float32 [4096, 1024], P('tensor', 'dp'), may hold values from -0.09375 to 0.09375
- cotangent: float32 [32768, 1024], P(('dp', 'tensor')), may hold values from -6 to 6
Outputs:
- result: float32 [32768, 1024], P(('dp', 'tensor'))
- grad_inputs: float32 [32768, 1024], P(('dp', 'tensor'))
- grad_ln1_gain: float32 [1024], replicated
- grad_ln1_bias: float32 [1024], replicated
- grad_ln2_gain: float32 [1024], replicated
- grad_ln2_bias: float32 [1024], replicated
- grad_w_query: float32 [1024, 1024], P('dp', 'tensor')
- grad_w_key: float32 [1024, 1024], P('dp', 'tensor')
- grad_w_value: float32 [1024, 1024], P('dp', 'tensor')
- grad_w_out: float32 [1024, 1024], P('tensor', 'dp')
- grad_w_up: float32 [1024, 4096], P('dp', 'tensor')
- grad_w_down: float32 [4096, 1024], P('tensor', 'dp')
The draws below stay inside these ranges and needn't reach their ends.
Inputs may be any that keep to these rules, and one draw needn't show every extreme that they name: The 4 lengths of a row sum to 2048; one of them is 1024.
All inputs are finite; a program needn't handle non-finite values.
Results may differ from the reference program's by a relative error of at most 0.025.
Values may be sent and summed in bfloat16 or wider, within the bound.
No kernel may reach another device: no remote copies, remote signals or barrier semaphores. Data moves between devices by JAX's collectives and lax.ppermute only.
A program may use at most 128 MiB of HBM per device.

```python
import math
import jax
import jax.numpy as jnp
import numpy as np
from jax import lax

D = 1024
HEADS = 16
HEAD_DIM = 64
FF = 4096
SEQ = 2048
ITEMS = 4
GROUPS = 16
TOKENS = 32768


def block_scale(own_key, dims, cuts, smallest, top_value):
    gain, own = 1.0, jax.random.fold_in(own_key, 6)
    for dim, blocks in cuts:
        draws = jnp.exp(jax.random.uniform(jax.random.fold_in(own, dim), (blocks,), jnp.float32, smallest / len(cuts), top_value / len(cuts)))
        gain = gain * jnp.repeat(draws, dims[dim] // blocks).reshape([-1 if axis == dim else 1 for axis in range(len(dims))])
    return gain


def profile(number_of, total, reach, lean):
    weights = [(1 << 20) // math.isqrt(rank ** lean) + 1 for rank in range(2, number_of + 1)]
    spare, given = total - reach - (number_of - 1), [1] * (number_of - 1)
    while spare > 0:
        movable = [i for i in range(number_of - 1) if given[i] < reach]
        pool, budget = sum([weights[i] for i in movable]), spare
        for i in movable:
            extra = min(reach - given[i], max(1, budget * weights[i] // pool), spare)
            given[i] = given[i] + extra
            spare = spare - extra
    return np.array([reach] + given)


def ragged_sizes(own_key, number_of, total, limit, slope):
    if number_of == 2:
        one = jax.random.randint(own_key, (), max(1, total - limit), min(limit, total - 1) + 1)
        return jnp.stack([one, total - one])
    sizes = jnp.asarray(profile(number_of, total, limit, slope), jnp.int32)
    twos = (number_of - 1) // 2
    giver, taker = sizes[1:1 + 2 * twos:2], sizes[2:2 + 2 * twos:2]
    margin = jnp.minimum(giver - 1, limit - taker)
    passed = jax.random.randint(jax.random.fold_in(own_key, 1), (twos,), 0, 1 << 20) % (margin + 1)
    sizes = sizes.at[1:1 + 2 * twos:2].set(giver - passed).at[2:2 + 2 * twos:2].set(taker + passed)
    return sizes[jax.random.permutation(jax.random.fold_in(own_key, 2), number_of)]


def scatter_about(rng, dims, deviation, most, cuts=(), kind=jnp.bfloat16):
    entries = deviation * jax.random.normal(rng, dims, jnp.float32)
    if cuts:
        entries = entries * block_scale(rng, dims, cuts, -0.22, 0.18)
    return jnp.clip(entries, -most, most).astype(kind)


def setup_inputs(seed: int = 0) -> dict:
    key_of = jax.random.split(jax.random.key(seed), 14)
    inputs = scatter_about(key_of[0], (TOKENS, D), 1.0, 6.0, ((0, 128),), jnp.float32)
    lengths = jax.vmap(lambda own: ragged_sizes(own, ITEMS, SEQ, SEQ // 2, 2))(jax.random.split(key_of[1], GROUPS)).reshape((GROUPS, ITEMS)).astype(jnp.int32)
    ln1_gain = jnp.clip(1.0 + 0.18 * jax.random.normal(key_of[2], (D,), jnp.float32), 0.1, 1.9)
    ln1_bias = scatter_about(key_of[3], (D,), 0.3, 1.75, (), jnp.float32)
    ln2_gain = jnp.clip(1.0 + 0.18 * jax.random.normal(key_of[4], (D,), jnp.float32), 0.1, 1.9)
    ln2_bias = scatter_about(key_of[5], (D,), 0.3, 1.75, (), jnp.float32)
    w_query = scatter_about(key_of[6], (D, D), D ** -0.5, 0.1875, ((0, 16), (1, 8)), jnp.float32)
    w_key = scatter_about(key_of[7], (D, D), D ** -0.5, 0.1875, ((0, 16), (1, 8)), jnp.float32)
    w_value = scatter_about(key_of[8], (D, D), D ** -0.5, 0.1875, ((0, 16), (1, 8)), jnp.float32)
    w_out = scatter_about(key_of[9], (D, D), (max(1, D // 64)) ** -0.5, 1.5, ((0, 8), (1, 16)), jnp.float32)
    w_up = scatter_about(key_of[10], (D, FF), D ** -0.5, 0.1875, ((0, 16), (1, 8)), jnp.float32)
    w_down = scatter_about(key_of[11], (FF, D), FF ** -0.5, 0.09375, ((0, 8), (1, 16)), jnp.float32)
    cotangent = scatter_about(key_of[12], (TOKENS, D), 1.0, 6.0, ((0, 128),), jnp.float32)
    return dict(inputs=inputs, lengths=lengths, ln1_gain=ln1_gain, ln1_bias=ln1_bias, ln2_gain=ln2_gain, ln2_bias=ln2_bias, w_query=w_query, w_key=w_key, w_value=w_value, w_out=w_out, w_up=w_up, w_down=w_down, cotangent=cotangent)


@jax.custom_vjp
def low(v):
    return lax.optimization_barrier(v.astype(jnp.bfloat16)).astype(jnp.float32)

@jax.custom_vjp
def low_back(v):
    return v

def low_keep(v):
    return (low(v), None)

def low_pass(kept, grad):
    return (grad,)

def back_keep(v):
    return (v, None)

def back_low(kept, grad):
    return (low(grad),)
low.defvjp(low_keep, low_pass)
low_back.defvjp(back_keep, back_low)
precise = lax.Precision.HIGHEST
norm_eps = 1e-05

def layer_norm(values, norm_gain, norm_shift):
    center = lax.optimization_barrier(jnp.mean(values, axis=-1, keepdims=True))
    centred = values - center
    spread = lax.optimization_barrier(jnp.mean(centred * centred, axis=-1, keepdims=True))
    return centred * lax.rsqrt(spread + norm_eps) * norm_gain + norm_shift

def feature(values):
    return jax.nn.elu(values) + 1.0

def segment_ids(lengths, positions):
    item_ends = jnp.cumsum(lengths).astype(jnp.int32)
    places = jnp.arange(positions, dtype=jnp.int32)
    return lax.optimization_barrier(jnp.sum((places[:, None] >= item_ends[None, :]).astype(jnp.int32), axis=1)).astype(jnp.int32)

def block_step(carry, block):
    memory, totals, previous = carry
    queries, keys_in, values_in, segments = block
    block_len = segments.shape[0]
    places = jnp.arange(block_len, dtype=jnp.int32)
    allowed = ((places[:, None] >= places[None, :]) & (segments[:, None] == segments[None, :])).astype(jnp.float32)
    scores = jnp.einsum('ihe,jhe->hij', queries, keys_in, precision=precise) * allowed[None]
    carried = (segments == previous).astype(jnp.float32)
    numerator = jnp.einsum('hij,jhe->ihe', scores, values_in, precision=precise)
    numerator = numerator + carried[:, None, None] * jnp.einsum('ihe,hef->ihf', queries, memory, precision=precise)
    denominator = lax.optimization_barrier(jnp.sum(scores, axis=2)).T + carried[:, None] * jnp.einsum('ihe,he->ih', queries, totals, precision=precise)
    attended = numerator / denominator[:, :, None]
    last_seg = segments[-1]
    survive = (last_seg == previous).astype(jnp.float32)
    in_last = (segments == last_seg).astype(jnp.float32)[:, None, None]
    memory = survive * memory + jnp.einsum('jhe,jhf->hef', keys_in * in_last, values_in, precision=precise)
    totals = survive * totals + lax.optimization_barrier(jnp.sum(keys_in * in_last, axis=0))
    return ((memory, totals, last_seg), attended)

def group_forward(weights, inputs, lengths):
    gain_one, bias_one, gain_two, bias_two, w_query, w_key, w_value, w_out, w_up, w_down = weights
    segments = segment_ids(lengths, SEQ)
    first_in = low(layer_norm(inputs, gain_one, bias_one))
    queries = low_back(jnp.dot(first_in, w_query, precision=precise))
    key_proj = low_back(jnp.dot(first_in, w_key, precision=precise))
    values_low = low(low_back(jnp.dot(first_in, w_value, precision=precise)))
    feat_query = low(feature(queries))
    feat_key = low(feature(key_proj))
    block_len = min(512, SEQ)
    blocks = SEQ // block_len

    def to_blocks(values):
        return values.reshape(blocks, block_len, HEADS, HEAD_DIM)
    initial = (jnp.zeros((HEADS, HEAD_DIM, HEAD_DIM), jnp.float32), jnp.zeros((HEADS, HEAD_DIM), jnp.float32), jnp.array(-1, jnp.int32))
    unused, attended = lax.scan(jax.checkpoint(block_step), initial, (to_blocks(feat_query), to_blocks(feat_key), to_blocks(values_low), segments.reshape(blocks, block_len)))
    attended_low = low(low_back(attended.reshape(SEQ, D)))
    hidden = inputs + low_back(jnp.dot(attended_low, w_out, precision=precise))
    second_in = low(layer_norm(hidden, gain_two, bias_two))
    up_proj = low_back(jnp.dot(second_in, w_up, precision=precise))
    activated = low(jax.nn.gelu(up_proj, approximate=False))
    return hidden + low_back(jnp.dot(activated, w_down, precision=precise))

def reference(inputs, lengths, ln1_gain, ln1_bias, ln2_gain, ln2_bias, w_query, w_key, w_value, w_out, w_up, w_down, cotangent):

    def forward(inputs, gain_one, bias_one, gain_two, bias_two, query_w, key_w, value_w, out_w, up_w, down_w):
        weights = (gain_one, bias_one, gain_two, bias_two, low(query_w), low(key_w), low(value_w), low(out_w), low(up_w), low(down_w))

        def one_group(group_pair):
            return group_forward(weights, group_pair[0], group_pair[1])
        outputs = lax.map(jax.checkpoint(one_group), (inputs.reshape(GROUPS, SEQ, D), lengths))
        return outputs.reshape(TOKENS, D)
    result, pullback = jax.vjp(forward, inputs, ln1_gain, ln1_bias, ln2_gain, ln2_bias, w_query, w_key, w_value, w_out, w_up, w_down)
    grads = pullback(cotangent)
    return (result, grads[0], grads[1], grads[2], grads[3], grads[4], grads[5], grads[6], grads[7], grads[8], grads[9], grads[10])
```

```python
import jax
import jax.numpy as jnp
from jax import lax
from jax.experimental import pallas as pl
from jax.experimental.pallas import tpu as pltpu
from jax.sharding import Mesh, PartitionSpec as P

BF = jnp.bfloat16
F32 = jnp.float32
EPS = 1e-05
BLOCK = 256
WIDTH = 1024
HALF = 512
FF_HALF = 2048
PAIRS = 4
STATE_ROWS = 80
X = ("xh", "xl")
REACH = 4


def dot(left, right, left_dim=1, right_dim=0):
    return lax.dot_general(
        left, right, (((left_dim,), (right_dim,)), ((), ())), preferred_element_type=F32
    )


def ring_shift(value, axis, step):
    return lax.ppermute(value, axis, [(i, (i + step) % 4) for i in range(4)])


def core_swap(value):
    return lax.ppermute(value, "core", [(0, 1), (1, 0)])


def turn(value, step):
    pairs = []
    for c in range(2):
        for xl in range(2):
            for y in range(4):
                pairs.append(((c * 2 + xl) * 4 + y, (xl * 2 + c) * 4 + (y + step) % 4))
    return lax.ppermute(value, ("core", "xl", "y"), pairs)


def place(pieces, index, axis=0):
    shape = list(pieces[0].shape)
    shape.insert(axis, 4)
    out = jnp.zeros(shape, pieces[0].dtype)
    for k, piece in enumerate(pieces):
        out = lax.dynamic_update_index_in_dim(out, piece, lax.rem(index - k + 4, 4), axis)
    return out


def gather_ring(value, axis, index, new_axis=0):
    return place([value] + [ring_shift(value, axis, k) for k in (1, 2, 3)], index, new_axis)


def split_pair(value):
    high = lax.reduce_precision(value, 8, 7)
    return jnp.concatenate([high, value - high], axis=0).astype(BF)


def join_pair(value):
    value = value.astype(F32)
    return value[:4] + value[4:8]


def sum_in_order(packed, index):
    return jnp.sum(place([join_pair(p) for p in packed], index), axis=0)


def scatter_ring(blocks, axis, index, block_axis=0, extra=None):
    def pick(k):
        return lax.dynamic_index_in_dim(
            blocks, lax.rem(index + k, 4), block_axis, keepdims=False
        )

    own = pick(0)
    shape, rows = own.shape, own.size // WIDTH
    total = own.astype(F32)
    if extra is not None:
        packed = jnp.concatenate([split_pair(extra), jnp.zeros((8, WIDTH), BF)], axis=0)
        extras = [packed]
    for k in (1, 2, 3):
        piece = pick(k)
        if extra is None:
            total = total + ring_shift(piece, axis, k).astype(F32)
        else:
            both = jnp.concatenate([piece.reshape(rows, WIDTH), packed], axis=0)
            both = ring_shift(both, axis, k)
            total = total + both[:rows].reshape(shape).astype(F32)
            extras.append(both[rows:])
    return total.astype(BF), None if extra is None else sum_in_order(extras, index)


def scatter_turn(blocks, index, extra=None):
    total, extras = 0.0, []
    shape, rows = blocks.shape[1:], blocks[0].size // WIDTH
    if extra is not None:
        packed = jnp.concatenate([split_pair(extra), jnp.zeros((8, WIDTH), BF)], axis=0)
    for k in range(4):
        piece = lax.dynamic_index_in_dim(blocks, lax.rem(index + k, 4), 0, keepdims=False)
        if extra is None:
            total = total + turn(piece, k).astype(F32)
        else:
            both = turn(jnp.concatenate([piece.reshape(rows, WIDTH), packed], axis=0), k)
            total = total + both[:rows].reshape(shape).astype(F32)
            extras.append(both[rows:])
    return total, None if extra is None else sum_in_order(extras, index)


def lanes(shape):
    return lax.broadcasted_iota(jnp.int32, shape, 1)


def head_sums(values):
    left = lanes(values.shape) < 64
    first = jnp.sum(jnp.where(left, values, 0.0), axis=1, keepdims=True)
    second = jnp.sum(jnp.where(left, 0.0, values), axis=1, keepdims=True)
    return jnp.where(left, first, second)


def segments_of(info, group, places):
    return sum((places >= info[group, k]).astype(jnp.int32) for k in range(4))


def column_segments(info, group):
    base = info[group, 4]
    return segments_of(info, group, base + lax.broadcasted_iota(jnp.int32, (BLOCK, 1), 0))


def pair_mask(info, group):
    base = info[group, 4]
    rows = lax.broadcasted_iota(jnp.int32, (BLOCK, 1), 0)
    cols = lax.broadcasted_iota(jnp.int32, (1, BLOCK), 1)
    row_seg = segments_of(info, group, base + rows)
    col_seg = segments_of(info, group, base + cols)
    return (rows >= cols) & (row_seg == col_seg)


def carried_of(info, group):
    return column_segments(info, group) == info[group, 5]


def in_last_of(info, group):
    return column_segments(info, group) == info[group, 6]


def pack_state(matrix, row, out):
    left = lanes((64, 128)) < 64
    out[0, 0, :64, :] = jnp.where(left, matrix[:64], matrix[64:]).astype(BF)
    out[0, 0, 64:, :] = jnp.broadcast_to(row, (STATE_ROWS - 64, 128)).astype(BF)


def unpack_state(state):
    memory = state[0, 0, :64, :].astype(F32)
    left = lanes((64, 128)) < 64
    full = jnp.concatenate(
        [jnp.where(left, memory, 0.0), jnp.where(left, 0.0, memory)], axis=0
    )
    return full.astype(BF), state[0, 0, 64:65, :].astype(F32)


def state_kernel(info, key, value, out):
    group = pl.program_id(0)
    kept = jnp.where(in_last_of(info, group), key[...].astype(F32), 0.0)
    matrix = dot(kept.astype(BF), value[...], 0, 0)
    pack_state(matrix, jnp.sum(kept, axis=0, keepdims=True), out)


def inner_kernel(info, query, key, value, numer, denom):
    group = pl.program_id(0)
    allowed = pair_mask(info, group)
    left = lanes((BLOCK, 128)) < 64
    q, k, v = query[...], key[...], value[...]
    zero = jnp.zeros_like(q)
    parts = []
    for side in (left, jnp.logical_not(left)):
        scores = jnp.where(allowed, dot(jnp.where(side, q, zero), k, 1, 1), 0.0)
        parts.append((dot(scores.astype(BF), v), jnp.sum(scores, axis=1, keepdims=True)))
    numer[...] = jnp.where(left, parts[0][0], parts[1][0])
    denom[...] = jnp.where(left, parts[0][1], parts[1][1])


def join_kernel(info, query, state, numer, denom, attended, inverse):
    group = pl.program_id(0)
    memory, totals = unpack_state(state)
    carried = carried_of(info, group)
    q = query[...]
    num = numer[...] + jnp.where(carried, dot(q, memory), 0.0)
    den = denom[...] + jnp.where(carried, head_sums(q.astype(F32) * totals), 0.0)
    inv = 1.0 / den
    attended[...] = (num * inv).astype(BF)
    inverse[...] = inv


def back_state_kernel(info, grad, attended, inverse, query, out, scaled, shift):
    group = pl.program_id(0)
    inv = inverse[...]
    d = grad[...].astype(F32)
    g = (d * inv).astype(BF)
    e = -head_sums(d * attended[...].astype(F32)) * inv
    scaled[...] = g
    shift[...] = e
    kept = jnp.where(carried_of(info, group), query[...].astype(F32), 0.0)
    pack_state(dot(kept.astype(BF), g, 0, 0), jnp.sum(kept * e, axis=0, keepdims=True), out)


def back_inner_kernel(
    info, query, key, value, scaled, shift, state, d_query, d_key, d_value
):
    group = pl.program_id(0)
    allowed = pair_mask(info, group)
    left = lanes((BLOCK, 128)) < 64
    q, k, v, g, e = query[...], key[...], value[...], scaled[...], shift[...]
    zero = jnp.zeros_like(q)
    parts = []
    for head, side in enumerate((left, jnp.logical_not(left))):
        scores = jnp.where(allowed, dot(jnp.where(side, q, zero), k, 1, 1), 0.0).astype(BF)
        d_scores = dot(jnp.where(side, g, zero), v, 1, 1) + e[:, 64 * head : 64 * head + 1]
        d_scores = jnp.where(allowed, d_scores, 0.0).astype(BF)
        parts.append((dot(d_scores, k), dot(d_scores, q, 0, 0), dot(scores, g, 0, 0)))
    dq, dk, dv = [jnp.where(left, a, b) for a, b in zip(*parts)]
    memory, totals = unpack_state(state)
    dq = dq + jnp.where(carried_of(info, group), dot(g, memory, 1, 1) + e * totals, 0.0)
    d_query[...] = (dq * jnp.minimum(q.astype(F32), 1.0)).astype(BF)
    d_key[...] = dk
    d_value[...] = dv


def back_join_kernel(info, key, value, state, d_key, d_value, key_out, value_out):
    group = pl.program_id(0)
    memory, totals = unpack_state(state)
    last = in_last_of(info, group)
    k, v = key[...], value[...]
    dk = d_key[...] + jnp.where(last, dot(v, memory, 1, 1) + totals, 0.0)
    dv = d_value[...] + jnp.where(last, dot(k, memory), 0.0)
    key_out[...] = (dk * jnp.minimum(k.astype(F32), 1.0)).astype(BF)
    value_out[...] = dv.astype(BF)


def attention_call(kernel, info, operands, outs, flops):
    def spec(shape, offset=0):
        if len(shape) == 4:
            return pl.BlockSpec((1, 1, STATE_ROWS, 128), lambda g, p: (g, p, 0, 0))
        return pl.BlockSpec((BLOCK, 128), lambda g, p: (g, p + offset))

    arrays = [a for a, _ in operands]
    moved = sum(2 * BLOCK * HALF * 4 for _ in arrays + outs)
    return pl.pallas_call(
        kernel,
        grid=(2, PAIRS),
        in_specs=[pl.BlockSpec(memory_space=pltpu.SMEM)]
        + [spec(a.shape, offset) for a, offset in operands],
        out_specs=[spec(o.shape) for o in outs],
        out_shape=outs,
        cost_estimate=pl.CostEstimate(flops=flops, bytes_accessed=moved, transcendentals=0),
        compiler_params=pltpu.CompilerParams(vmem_limit_bytes=24 * 1024 * 1024),
    )(info, *arrays)


TOKENS2 = 2 * BLOCK
STATE = jax.ShapeDtypeStruct((2, PAIRS, STATE_ROWS, 128), BF)
WIDE32 = jax.ShapeDtypeStruct((TOKENS2, HALF), F32)
WIDE16 = jax.ShapeDtypeStruct((TOKENS2, HALF), BF)


FF_STEP = 256


def gelu_parts(u):
    density = jnp.exp(-0.5 * u * u) * 0.3989422804014327
    return 0.5 * (1.0 + lax.erf(u * 0.7071067811865476)), density


def feed_kernel(second, grad, up, down, grad_up, grad_down, d_second, result, second_t, grad_t):
    step = pl.program_id(0)

    @pl.when(step == 0)
    def _():
        second_t[...] = second[...].T
        grad_t[...] = grad[...].T

    u = dot(second[...], up[...])
    d_act = dot(grad[...], down[...])
    below, density = gelu_parts(u)
    act = (u * below).astype(BF)
    d_up = (d_act * (below + u * density)).astype(BF)
    grad_up[...] = dot(second_t[...], d_up).astype(BF)
    grad_down[...] = dot(grad_t[...], act).astype(BF)
    d_part = dot(d_up, up[...], 1, 1)
    r_part = dot(act, down[...], 1, 1)

    @pl.when(step == 0)
    def _():
        d_second[...] = d_part
        result[...] = r_part

    @pl.when(step > 0)
    def _():
        d_second[...] += d_part
        result[...] += r_part


def feed_forward(second, grad, weights):
    steps = FF_HALF // FF_STEP
    whole = pl.BlockSpec((TOKENS2, WIDTH), lambda j: (0, 0))
    columns = pl.BlockSpec((WIDTH, FF_STEP), lambda j: (0, j))
    return pl.pallas_call(
        feed_kernel,
        grid=(steps,),
        in_specs=[whole, whole, columns, pl.BlockSpec((WIDTH, FF_STEP), lambda j: (0, j + steps))],
        out_specs=[columns, columns, whole, whole],
        out_shape=[
            jax.ShapeDtypeStruct((WIDTH, FF_HALF), BF),
            jax.ShapeDtypeStruct((WIDTH, FF_HALF), BF),
            jax.ShapeDtypeStruct((TOKENS2, WIDTH), F32),
            jax.ShapeDtypeStruct((TOKENS2, WIDTH), F32),
        ],
        scratch_shapes=[pltpu.VMEM((WIDTH, TOKENS2), BF), pltpu.VMEM((WIDTH, TOKENS2), BF)],
        cost_estimate=pl.CostEstimate(
            flops=12 * TOKENS2 * WIDTH * FF_HALF,
            bytes_accessed=20 * 1024 * 1024,
            transcendentals=2 * TOKENS2 * FF_HALF,
        ),
        compiler_params=pltpu.CompilerParams(vmem_limit_bytes=40 * 1024 * 1024),
    )(second, grad, weights, weights)


def norm(values, gain, bias):
    center = jnp.mean(values, axis=-1, keepdims=True)
    centred = values - center
    scale = lax.rsqrt(jnp.mean(centred * centred, axis=-1, keepdims=True) + EPS)
    unit = centred * scale
    return (unit * gain + bias).astype(BF), unit, scale


def norm_back(d_out, unit, scale, gain):
    gh = d_out * gain
    slope = scale * (
        gh
        - jnp.mean(gh, axis=-1, keepdims=True)
        - unit * jnp.mean(gh * unit, axis=-1, keepdims=True)
    )
    return slope, jnp.sum(d_out * unit, axis=0), jnp.sum(d_out, axis=0)


def both_cores(value):
    return jnp.concatenate([value, core_swap(value)], axis=0)


def sum_cores(partial):
    return partial[:BLOCK] + core_swap(partial[BLOCK:].astype(BF)).astype(F32)


def feature(values):
    return jnp.where(values > 0.0, values + 1.0, jnp.exp(jnp.minimum(values, 0.0)))


def local(
    inputs,
    lengths,
    ln1_gain,
    ln1_bias,
    ln2_gain,
    ln2_bias,
    w_query,
    w_key,
    w_value,
    w_out,
    w_up,
    w_down,
    cotangent,
):
    z = lax.axis_index("z")
    x = lax.axis_index(X)
    y = lax.axis_index("y")
    block = lax.axis_index(("xl", "y"))

    shard = jnp.concatenate(
        [w_query, w_key, w_value, w_out.T, w_up, w_down.T], axis=1
    ).astype(BF)
    turned = place([turn(shard, k) for k in range(4)], y)

    def columns(start, size):
        return jnp.concatenate([turned[j, :, start : start + size] for j in range(4)], axis=1)

    first_half = jnp.concatenate([columns(0, 128), columns(128, 128)], axis=1)
    second_half = jnp.concatenate([columns(256, 128), columns(384, 128)], axis=1)
    feed_rows = jnp.concatenate([columns(512, 512), columns(1024, 512)], axis=1)
    feed_weights = lax.all_gather(feed_rows, ("z", "xh", "xl"), axis=0, tiled=True)
    first_half = gather_ring(first_half, X, x)
    second_half = gather_ring(second_half, "z", z)
    first_half = gather_ring(first_half, "z", z).reshape(WIDTH, WIDTH)
    second_half = gather_ring(second_half, X, x, 1).reshape(WIDTH, WIDTH)

    ends = jnp.cumsum(both_cores(lengths), axis=1)

    def segment_at(place_in_group):
        return jnp.sum((place_in_group >= ends).astype(jnp.int32), axis=1)

    def last_segment(which):
        return segment_at(which * BLOCK + BLOCK - 1)

    here = last_segment(block)
    before = jnp.where(block > 0, last_segment(block - 1), -1)
    zeros = jnp.zeros((2,), jnp.int32)
    info = jnp.concatenate(
        [ends, jnp.stack([zeros + block * BLOCK, before, here, zeros], axis=1)], axis=1
    )

    first_in, unit_one, scale_one = norm(inputs, ln1_gain, ln1_bias)
    first_all = both_cores(first_in)
    grad_all = both_cores(cotangent.astype(BF))

    feats = feature(dot(first_all, first_half)).astype(BF)
    values = dot(first_all, second_half[:, :HALF]).astype(BF)
    q_, k_, v_ = (feats, 0), (feats, PAIRS), (values, 0)

    (state,) = attention_call(state_kernel, info, [k_, v_], [STATE], 2 * 256 * 128 * 128 * 8)

    def tensor_shift(value, step):
        return lax.ppermute(
            value, ("xl", "y"), [(i, i + step) for i in range(8) if 0 <= i + step < 8]
        )

    state_in = 0.0
    for k in range(1, REACH + 1):
        joined = ((block - k >= 0) & (last_segment(block - k) == before)).astype(F32)
        state_in = state_in + joined[:, None, None, None] * tensor_shift(state, k).astype(F32)
    state_in = state_in.astype(BF)

    numer, denom = attention_call(
        inner_kernel, info, [q_, k_, v_], [WIDE32, WIDE32], 4 * 2 * 256 * 256 * 128 * 8
    )
    attended, inverse = attention_call(
        join_kernel,
        info,
        [q_, (state_in, 0), (numer, 0), (denom, 0)],
        [WIDE16, WIDE32],
        2 * 256 * 128 * 128 * 8,
    )
    out_rows = second_half[:, HALF:]
    hidden = inputs + sum_cores(dot(attended, out_rows, 1, 1))

    second_in, unit_two, scale_two = norm(hidden, ln2_gain, ln2_bias)
    second_all = both_cores(second_in)
    grad_up, grad_down, d_second, ff_out = feed_forward(second_all, grad_all, feed_weights)
    result = hidden + sum_cores(ff_out)
    slope, d_gain_two, d_bias_two = norm_back(
        sum_cores(d_second), unit_two, scale_two, ln2_gain
    )
    d_hidden = cotangent + slope
    branch_all = both_cores(d_hidden.astype(BF))
    d_attended = dot(branch_all, out_rows).astype(BF)
    grad_out = dot(branch_all, attended, 0, 0).astype(BF)

    down_part, _ = scatter_ring(grad_down.reshape(4, 4, 64, FF_HALF), "z", z)
    up_part, _ = scatter_ring(grad_up.reshape(4, 4, 64, FF_HALF), X, x, 1)
    down_part, _ = scatter_ring(down_part, X, x)
    up_part, _ = scatter_ring(up_part, "z", z)
    feed_part = jnp.stack(
        [
            jnp.concatenate(
                [up_part[:, j * 512 : j * 512 + 512], down_part[:, j * 512 : j * 512 + 512]], axis=1
            )
            for j in range(4)
        ]
    )
    feed_grad, _ = scatter_turn(feed_part, y)

    back_state, scaled, shift = attention_call(
        back_state_kernel,
        info,
        [(d_attended, 0), (attended, 0), (inverse, 0), q_],
        [STATE, WIDE16, WIDE32],
        2 * 256 * 128 * 128 * 8,
    )
    state_back = 0.0
    for k in range(1, REACH + 1):
        joined = ((block + k < 8) & (last_segment(block + k - 1) == here)).astype(F32)
        state_back = state_back + joined[:, None, None, None] * tensor_shift(
            back_state, -k
        ).astype(F32)
    state_back = state_back.astype(BF)
    d_queries, d_key, d_value = attention_call(
        back_inner_kernel,
        info,
        [q_, k_, v_, (scaled, 0), (shift, 0), (state_in, 0)],
        [WIDE16, WIDE32, WIDE32],
        10 * 2 * 256 * 256 * 128 * 8,
    )
    d_keys, d_values = attention_call(
        back_join_kernel,
        info,
        [k_, v_, (state_back, 0), (d_key, 0), (d_value, 0)],
        [WIDE16, WIDE16],
        4 * 256 * 128 * 128 * 8,
    )
    d_pair = jnp.concatenate([d_queries, d_keys], axis=1)
    d_first = sum_cores(dot(d_pair, first_half, 1, 1) + dot(d_values, second_half[:, :HALF], 1, 1))
    slope, d_gain_one, d_bias_one = norm_back(d_first, unit_one, scale_one, ln1_gain)
    grad_inputs = d_hidden + slope

    norms = jnp.stack([d_gain_one, d_bias_one, d_gain_two, d_bias_two])
    packed = split_pair(norms)
    norms = join_pair(packed) + join_pair(core_swap(packed))
    grad_one = dot(first_all, d_pair, 0, 0).astype(BF)
    grad_two = jnp.concatenate([dot(first_all, d_values, 0, 0).astype(BF), grad_out], axis=1)
    one, norms = scatter_ring(grad_one.reshape(4, 4, 64, WIDTH), X, x, 1, norms)
    two, _ = scatter_ring(grad_two.reshape(4, 4, 64, WIDTH), "z", z)
    one, norms = scatter_ring(one, "z", z, 0, norms)
    two, _ = scatter_ring(two, X, x)
    part = jnp.concatenate([one, two], axis=1)
    part = part.reshape(64, 4, 4, 128).transpose(2, 0, 1, 3).reshape(4, 64, 512)
    main_grad, norms = scatter_turn(part, y, norms)

    return (
        result,
        grad_inputs,
        norms[0],
        norms[1],
        norms[2],
        norms[3],
        main_grad[:, :128],
        main_grad[:, 128:256],
        main_grad[:, 256:384],
        main_grad[:, 384:].T,
        feed_grad[:, :512],
        feed_grad[:, 512:].T,
    )


def solution(mesh):
    axes = ("z", "xh", "core", "xl", "y")
    split = Mesh(mesh.devices.reshape(4, 2, 2, 2, 4), axes)
    dp, tensor = ("z", "xh", "core"), ("xl", "y")
    tokens, rows, cols = P(axes, None), P(dp, tensor), P(tensor, dp)
    in_specs = (tokens, P(dp, None), P(), P(), P(), P(), rows, rows, rows, cols, rows, cols, tokens)
    out_specs = (tokens, tokens, P(), P(), P(), P(), rows, rows, rows, cols, rows, cols)
    return jax.shard_map(
        local, mesh=split, in_specs=in_specs, out_specs=out_specs, check_vma=False
    )
```

```python
import math

import jax
import jax.numpy as jnp
from jax import lax
from jax.experimental import pallas as pl
from jax.experimental.pallas import tpu as pltpu
from jax.sharding import Mesh, PartitionSpec as P

BF = jnp.bfloat16
F32 = jnp.float32
EPS = 1e-05
BLOCK = 256
WIDTH = 1024
HALF = 512
FF_HALF = 2048
PAIRS = 4
STATE_ROWS = 80
X = ("xh", "xl")
REACH = 4


def dot(left, right, left_dim=1, right_dim=0):
    return lax.dot_general(
        left, right, (((left_dim,), (right_dim,)), ((), ())), preferred_element_type=F32
    )


def ring_shift(value, axis, step):
    return lax.ppermute(value, axis, [(i, (i + step) % 4) for i in range(4)])


def core_swap(value):
    return lax.ppermute(value, "core", [(0, 1), (1, 0)])


def tensor_shift(value, step):
    return lax.ppermute(
        value, ("xl", "y"), [(i, i + step) for i in range(8) if 0 <= i + step < 8]
    )


def turn_y(value, step):
    pairs = []
    for c in range(2):
        for xl in range(2):
            for y in range(4):
                pairs.append(((c * 2 + xl) * 4 + y, (xl * 2 + c) * 4 + (y + step) % 4))
    return lax.ppermute(value, ("core", "xl", "y"), pairs)


def turn_x(value, step, back=False):
    high, low = step // 2, step % 2
    pairs = []
    for xh in range(2):
        for c in range(2):
            for xl in range(2):
                core, x_low = (xl ^ low, c) if back else (xl, c ^ low)
                pairs.append(((xh * 2 + c) * 2 + xl, ((xh ^ high) * 2 + core) * 2 + x_low))
    return lax.ppermute(value, ("xh", "core", "xl"), pairs)


def after(values, earlier):
    return lax.optimization_barrier((values, earlier))[0]


def place(pieces, positions):
    out = jnp.zeros((4,) + pieces[0].shape, pieces[0].dtype)
    for piece, position in zip(pieces, positions):
        out = lax.dynamic_update_index_in_dim(out, piece, position, 0)
    return out


ORDER = (1, 3, 2)


def stay(*values):
    return [pltpu.with_memory_space_constraint(v, pltpu.HBM) for v in values]


def away(shape):
    return pltpu.HBM(shape.shape, shape.dtype)


def bytes_of(values):
    return sum(math.prod(v.shape) * jnp.dtype(v.dtype).itemsize for v in values)


def call(kernel, operands, outs, scalars=(), limit=24, flops=0, scratch=()):
    moved = bytes_of(list(operands) + list(outs))

    def whole(value):
        return pl.BlockSpec(value.shape, lambda i: (0,) * len(value.shape))

    return pl.pallas_call(
        kernel,
        grid=(1,),
        in_specs=[pl.BlockSpec(memory_space=pltpu.SMEM)] * len(scalars)
        + [whole(o) for o in operands],
        out_specs=[whole(o) for o in outs],
        out_shape=list(outs),
        scratch_shapes=list(scratch),
        cost_estimate=pl.CostEstimate(flops=flops, bytes_accessed=moved, transcendentals=0),
        compiler_params=pltpu.CompilerParams(vmem_limit_bytes=limit * 1024 * 1024),
    )(*scalars, *operands)


def f32(*shape):
    return jax.ShapeDtypeStruct(shape, F32)


def bf16(*shape):
    return jax.ShapeDtypeStruct(shape, BF)


def lanes(shape):
    return lax.broadcasted_iota(jnp.int32, shape, 1)


def head_sums(values):
    left = lanes(values.shape) < 64
    first = jnp.sum(jnp.where(left, values, 0.0), axis=1, keepdims=True)
    second = jnp.sum(jnp.where(left, 0.0, values), axis=1, keepdims=True)
    return jnp.where(left, first, second)


def segments_of(info, group, places):
    return sum((places >= info[group, k]).astype(jnp.int32) for k in range(4))


def column_segments(info, group):
    base = info[group, 4]
    return segments_of(info, group, base + lax.broadcasted_iota(jnp.int32, (BLOCK, 1), 0))


def pair_mask(info, group):
    base = info[group, 4]
    rows = lax.broadcasted_iota(jnp.int32, (BLOCK, 1), 0)
    cols = lax.broadcasted_iota(jnp.int32, (1, BLOCK), 1)
    row_seg = segments_of(info, group, base + rows)
    col_seg = segments_of(info, group, base + cols)
    return (rows >= cols) & (row_seg == col_seg)


def carried_of(info, group):
    return column_segments(info, group) == info[group, 5]


def in_last_of(info, group):
    return column_segments(info, group) == info[group, 6]


def masked_mean(values, keep):
    count = jnp.maximum(jnp.sum(keep.astype(F32), axis=0, keepdims=True), 1.0)
    mean = jnp.sum(jnp.where(keep, values, 0.0), axis=0, keepdims=True) / count
    return mean.astype(BF).astype(F32)


def pack_state(matrix, row, center, out, group, pair):
    left = lanes((64, 128)) < 64
    out[group, pair, :64, :] = jnp.where(left, matrix[:64], matrix[64:]).astype(BF)
    high = row.astype(BF).astype(F32)
    place = lax.broadcasted_iota(jnp.int32, (STATE_ROWS - 64, 128), 0)
    rest = jnp.where(place == 0, high, jnp.where(place == 1, row - high, 0.0))
    out[group, pair, 64:, :] = jnp.where(place == 2, center, rest).astype(BF)


def unpack_states(info, group, states, pair, flags, step):
    left = lanes((64, 128)) < 64
    parts, rows, centers = [], [], []
    for k, state in enumerate(states, 1):
        keep = info[group, flags + k - 1].astype(F32)
        slot = (pair + step * k) % 4
        packed = state[0, slot].astype(F32) * keep
        memory = packed[:64]
        parts.append(
            jnp.concatenate([jnp.where(left, memory, 0.0), jnp.where(left, 0.0, memory)], axis=0)
        )
        rows.append(packed[64:65] + packed[65:66])
        centers.append(packed[66:67])
    return parts, rows, centers


def pair_columns(ref, pair, offset=0):
    start = offset + pair * 128
    return ref[:, start : start + 128]


def enter_kernel(info, own, other, w0, w1, w2, w3, feats, values, out):
    tokens = jnp.concatenate([own[...], other[...]], axis=0)
    all_weights = (w0, w1, w2, w3)
    for pair, weights in enumerate(all_weights):
        feat = dot(tokens, weights[:, :256])
        feat = jnp.where(feat > 0.0, feat + 1.0, jnp.exp(jnp.minimum(feat, 0.0))).astype(BF)
        feats[:, pair * 128 : pair * 128 + 128] = feat[:, :128]
        feats[:, HALF + pair * 128 : HALF + pair * 128 + 128] = feat[:, 128:]
    for two in range(2):
        both = [w[:, 256:] for w in all_weights[2 * two : 2 * two + 2]]
        value = dot(tokens, jnp.concatenate(both, axis=1)).astype(BF)
        values[:, two * 256 : two * 256 + 256] = value
    for group in range(2):
        last = in_last_of(info, group)
        rows = slice(group * BLOCK, group * BLOCK + BLOCK)
        for pair in range(PAIRS):
            span = slice(pair * 128, pair * 128 + 128)
            v = values[rows, span].astype(F32)
            keys = feats[rows, HALF + pair * 128 : HALF + pair * 128 + 128]
            kept = jnp.where(last, keys.astype(F32), 0.0)
            center = masked_mean(v, last)
            matrix = dot(kept.astype(BF), (v - center).astype(BF), 0, 0)
            row = jnp.sum(kept, axis=0, keepdims=True)
            pack_state(matrix, row, center, out, group, pair)


def inner_kernel(info, feats, values, numer, denom):
    group = pl.program_id(0)
    allowed = pair_mask(info, group)
    left = lanes((BLOCK, 128)) < 64
    for pair in range(PAIRS):
        q, k = pair_columns(feats, pair), pair_columns(feats, pair, HALF)
        v = pair_columns(values, pair)
        zero = jnp.zeros_like(q)
        parts = []
        for side in (left, jnp.logical_not(left)):
            scores = jnp.where(allowed, dot(jnp.where(side, q, zero), k, 1, 1), 0.0)
            parts.append((dot(scores.astype(BF), v), jnp.sum(scores, axis=1, keepdims=True)))
        span = slice(pair * 128, pair * 128 + 128)
        numer[:, span] = jnp.where(left, parts[0][0], parts[1][0])
        denom[:, span] = jnp.where(left, parts[0][1], parts[1][1])


def store_halves(group, partial, own, send):
    @pl.when(group == 0)
    def _():
        own[...] = partial

    @pl.when(group == 1)
    def _():
        send[...] = partial.astype(BF)


def join_kernel(
    info, feats, numer, denom, s1, s2, s3, s4, out_rows, wide, low, inverse, own, send
):
    group = pl.program_id(0)
    carried = carried_of(info, group)
    outs = []
    for pair in range(PAIRS):
        q = pair_columns(feats, pair)
        parts, rows, centers = unpack_states(info, group, (s1, s2, s3, s4), pair, 8, -1)
        num, den = dot(q, sum(parts).astype(BF)), 0.0
        for row, center in zip(rows, centers):
            weight = head_sums(q.astype(F32) * row)
            num, den = num + weight * center, den + weight
        inv = 1.0 / (pair_columns(denom, pair) + jnp.where(carried, den, 0.0))
        out = (pair_columns(numer, pair) + jnp.where(carried, num, 0.0)) * inv
        span = slice(pair * 128, pair * 128 + 128)
        wide[:, span] = out
        inverse[:, span] = inv
        outs.append(out.astype(BF))
        low[:, span] = outs[-1]
    partial = dot(jnp.concatenate(outs, axis=1), out_rows[...], 1, 1)
    store_halves(group, partial, own, send)


def back_state_kernel(
    info, feats, values, attended, inverse, b_own, b_other, out_rows, out, scaled, shift
):
    group = pl.program_id(0)
    carried = carried_of(info, group)
    branch = jnp.where(group == 0, b_own[...], b_other[...])
    grad = dot(branch, out_rows[...]).astype(BF).astype(F32)
    for pair in range(PAIRS):
        span = slice(pair * 128, pair * 128 + 128)
        g = (grad[:, span] * pair_columns(inverse, pair)).astype(BF)
        wide = g.astype(F32)
        e = -head_sums(wide * pair_columns(attended, pair))
        scaled[:, span] = g
        shift[:, span] = e
        center = masked_mean(pair_columns(values, pair).astype(F32), carried)
        kept = jnp.where(carried, pair_columns(feats, pair).astype(F32), 0.0)
        row = jnp.sum(kept * (e + head_sums(wide * center)), axis=0, keepdims=True)
        pack_state(dot(kept.astype(BF), g, 0, 0), row, center, out, 0, pair)


def back_inner_kernel(
    info, feats, values, scaled, shift, s1, s2, s3, s4, d_query, d_key, d_value
):
    group = pl.program_id(0)
    allowed = pair_mask(info, group)
    carried = carried_of(info, group)
    left = lanes((BLOCK, 128)) < 64
    for pair in range(PAIRS):
        q, k = pair_columns(feats, pair), pair_columns(feats, pair, HALF)
        v, g, e = [pair_columns(r, pair) for r in (values, scaled, shift)]
        zero = jnp.zeros_like(q)
        parts = []
        for head, side in enumerate((left, jnp.logical_not(left))):
            scores = jnp.where(allowed, dot(jnp.where(side, q, zero), k, 1, 1), 0.0).astype(BF)
            d_scores = dot(jnp.where(side, g, zero), v, 1, 1) + e[:, 64 * head : 64 * head + 1]
            d_scores = jnp.where(allowed, d_scores, 0.0).astype(BF)
            parts.append((dot(d_scores, k), dot(d_scores, q, 0, 0), dot(scores, g, 0, 0)))
        dq, dk, dv = [jnp.where(left, a, b) for a, b in zip(*parts)]
        memories, rows, centers = unpack_states(info, group, (s1, s2, s3, s4), pair, 8, -1)
        more = dot(g, sum(memories).astype(BF), 1, 1)
        for row, center in zip(rows, centers):
            more = more + row * (e + head_sums(g.astype(F32) * center))
        dq = dq + jnp.where(carried, more, 0.0)
        span = slice(pair * 128, pair * 128 + 128)
        d_query[:, span] = (dq * jnp.minimum(q.astype(F32), 1.0)).astype(BF)
        d_key[:, span] = dk
        d_value[:, span] = dv


def back_join_kernel(
    info, feats, values, d_query, d_key, d_value, s1, s2, s3, s4, w0, w1, w2, w3,
    key_out, value_out, own, send,
):
    group = pl.program_id(0)
    last = in_last_of(info, group)
    partial = 0.0
    for pair, weights in enumerate((w0, w1, w2, w3)):
        k, v = pair_columns(feats, pair, HALF), pair_columns(values, pair)
        memories, rows, centers = unpack_states(info, group, (s1, s2, s3, s4), pair, 12, 1)
        memory = sum(memories).astype(BF)
        center, row = centers[0], rows[0]
        for m, r, c in zip(memories[1:], rows[1:], centers[1:]):
            away = jnp.broadcast_to(center - c, (16, 128)).astype(BF)
            row = row + r + dot(away, m.astype(BF), 1, 1)[:1]
        more = dot((v.astype(F32) - center).astype(BF), memory, 1, 1) + row
        dk = pair_columns(d_key, pair) + jnp.where(last, more, 0.0)
        dv = pair_columns(d_value, pair) + jnp.where(last, dot(k, memory), 0.0)
        span = slice(pair * 128, pair * 128 + 128)
        dk = (dk * jnp.minimum(k.astype(F32), 1.0)).astype(BF)
        dv = dv.astype(BF)
        key_out[:, span] = dk
        value_out[:, span] = dv
        partial = partial + dot(
            jnp.concatenate([pair_columns(d_query, pair), dk, dv], axis=1), weights[...], 1, 1
        )
    store_halves(group, partial, own, send)


def attention_call(kernel, info, operands, outs, flops):
    def spec(shape):
        if len(shape) == 4:
            return pl.BlockSpec((1,) + shape[1:], lambda g: (g, 0, 0, 0))
        if shape[0] == TOKENS2:
            return pl.BlockSpec((BLOCK, shape[1]), lambda g: (g, 0))
        return pl.BlockSpec(shape, lambda g: (0, 0))

    moved = bytes_of(operands + outs)
    return pl.pallas_call(
        kernel,
        grid=(2,),
        in_specs=[pl.BlockSpec(memory_space=pltpu.SMEM)] + [spec(a.shape) for a in operands],
        out_specs=[spec(o.shape) for o in outs],
        out_shape=list(outs),
        cost_estimate=pl.CostEstimate(flops=flops, bytes_accessed=moved, transcendentals=0),
        compiler_params=pltpu.CompilerParams(vmem_limit_bytes=32 * 1024 * 1024),
    )(info, *operands)


TOKENS2 = 2 * BLOCK
STATE = bf16(2, PAIRS, STATE_ROWS, 128)
WIDE32 = f32(TOKENS2, HALF)
WIDE16 = bf16(TOKENS2, HALF)
OWN = f32(BLOCK, WIDTH)
SEND = bf16(BLOCK, WIDTH)


def prepare_kernel(w_query, w_key, w_value, w_out, w_up, w_down, main, feed):
    main[:, :128] = w_query[...].astype(BF)
    main[:, 128:256] = w_key[...].astype(BF)
    main[:, 256:] = w_value[...].astype(BF)
    feed[:, :512] = w_up[...].astype(BF)
    feed[:, 512:1024] = w_down[...].astype(BF)
    feed[:, 1024:] = w_out[...].astype(BF)


def unit_of(values):
    centred = values - jnp.mean(values, axis=-1, keepdims=True)
    scale = lax.rsqrt(jnp.mean(centred * centred, axis=-1, keepdims=True) + EPS)
    return centred * scale, scale


def feed_rows_kernel(p0, p1, p2, p3, feed, out):
    for k, p in enumerate((p0, p1, p2, p3)):
        feed[:, k * 512 : k * 512 + 512] = p[:, :512]
        feed[:, FF_HALF + k * 512 : FF_HALF + k * 512 + 512] = p[:, 512:1024]
        out[:, k * 128 : k * 128 + 128] = p[:, 1024:]


def first_norm_kernel(inputs, cotangent, gain, bias, first_in, grad_low):
    unit, _ = unit_of(inputs[...])
    first_in[...] = (unit * gain[...] + bias[...]).astype(BF)
    grad_low[...] = cotangent[...].astype(BF)


def second_norm_kernel(inputs, gain, bias, own, got, hidden, second_in):
    total = inputs[...] + (own[...] + got[...].astype(F32))
    hidden[...] = total
    unit, _ = unit_of(total)
    second_in[...] = (unit * gain[...] + bias[...]).astype(BF)


def norm_slope(values, gain, own, got):
    unit, scale = unit_of(values[...])
    d_out = own[...] + got[...].astype(F32)
    gh = d_out * gain[...]
    slope = scale * (
        gh
        - jnp.mean(gh, axis=-1, keepdims=True)
        - unit * jnp.mean(gh * unit, axis=-1, keepdims=True)
    )
    gains = jnp.sum(d_out * unit, axis=0, keepdims=True)
    return slope, gains, jnp.sum(d_out, axis=0, keepdims=True)


def second_back_kernel(hidden, gain, own, got, cotangent, d_hidden, low, sums):
    slope, gains, biases = norm_slope(hidden, gain, own, got)
    total = cotangent[...] + slope
    d_hidden[...] = total
    low[...] = total.astype(BF)
    sums[...] = jnp.zeros_like(sums)
    sums[2:3, :] = gains
    sums[3:4, :] = biases


def split_pair(sums):
    high = sums.astype(BF).astype(F32)
    return jnp.concatenate([high, sums - high], axis=0).astype(BF)


def join_pair(packed):
    wide = packed.astype(F32)
    return wide[:8] + wide[8:]


def first_back_kernel(inputs, gain, own, got, d_hidden, sums, grad_inputs, packed):
    slope, gains, biases = norm_slope(inputs, gain, own, got)
    grad_inputs[...] = d_hidden[...] + slope
    place = lax.broadcasted_iota(jnp.int32, sums.shape, 0)
    total = jnp.where(place == 0, gains, jnp.where(place == 1, biases, sums[...]))
    packed[...] = split_pair(total)


def sum_in_order(pieces, position):
    total = 0.0
    for a in range(4):
        k = position(a)
        total = total + sum(jnp.where(k == i, p, 0.0) for i, p in enumerate(pieces))
    return total


FF_STEP = 256
FF_STEPS = FF_HALF // FF_STEP


def gelu_parts(u):
    density = jnp.exp(-0.5 * u * u) * 0.3989422804014327
    return 0.5 * (1.0 + lax.erf(u * 0.7071067811865476)), density


def feed_kernel(
    where, s_own, s_other, g_own, g_other, up, down, up_then, down_then,
    up0, up1, up2, up3, down_out, d_own, d_send, r_own, r_send,
    second, grad, second_t, grad_t, act_then, d_up_then, d_total, r_total,
):
    step = pl.program_id(0)

    @pl.when(step == 0)
    def _():
        second[:BLOCK] = s_own[...]
        second[BLOCK:] = s_other[...]
        grad[:BLOCK] = g_own[...]
        grad[BLOCK:] = g_other[...]
        second_t[...] = second[...].T
        grad_t[...] = grad[...].T
        act_then[...] = jnp.zeros_like(act_then)
        d_up_then[...] = jnp.zeros_like(d_up_then)
        d_total[...] = jnp.zeros_like(d_total)
        r_total[...] = jnp.zeros_like(r_total)

    act, d_up = act_then[...], d_up_then[...]
    down_out[...] = dot(grad_t[...], act).astype(BF)
    for k, out in enumerate((up0, up1, up2, up3)):
        x = lax.rem(where[1] + k, 4)
        rows = [
            second_t[pl.ds(pl.multiple_of(z * 256 + x * 64, 64), 64), :] for z in range(4)
        ]
        out[...] = dot(jnp.concatenate(rows, axis=0), d_up).astype(BF)
    d_total[...] += dot(d_up, up_then[...], 1, 1)
    r_total[...] += dot(act, down_then[...], 1, 1)

    u = dot(second[...], up[...])
    d_act = dot(grad[...], down[...])
    below, density = gelu_parts(u)
    act_then[...] = (u * below).astype(BF)
    d_up_then[...] = (d_act * (below + u * density)).astype(BF)

    @pl.when(step == FF_STEPS)
    def _():
        d_own[...] = d_total[:BLOCK]
        d_send[...] = d_total[BLOCK:].astype(BF)
        r_own[...] = r_total[:BLOCK]
        r_send[...] = r_total[BLOCK:].astype(BF)


def feed_forward(where, tokens, weights):
    def now(j):
        return jnp.minimum(j, FF_STEPS - 1)

    def then(j):
        return jnp.maximum(j - 1, 0)

    whole = pl.BlockSpec((BLOCK, WIDTH), lambda j: (0, 0))

    def columns(rows, index, offset=0):
        return pl.BlockSpec((rows, FF_STEP), lambda j: (0, index(j) + offset))

    return pl.pallas_call(
        feed_kernel,
        grid=(FF_STEPS + 1,),
        in_specs=[pl.BlockSpec(memory_space=pltpu.SMEM)]
        + [whole] * 4
        + [
            columns(WIDTH, now),
            columns(WIDTH, now, FF_STEPS),
            columns(WIDTH, then),
            columns(WIDTH, then, FF_STEPS),
        ],
        out_specs=[columns(BLOCK, then)] * 4 + [columns(WIDTH, then)] + [whole] * 4,
        out_shape=[away(bf16(BLOCK, FF_HALF))] * 4
        + [away(bf16(WIDTH, FF_HALF)), OWN, SEND, away(OWN), away(SEND)],
        scratch_shapes=[pltpu.VMEM((TOKENS2, WIDTH), BF)] * 2
        + [pltpu.VMEM((WIDTH, TOKENS2), BF)] * 2
        + [pltpu.VMEM((TOKENS2, FF_STEP), BF)] * 2
        + [pltpu.VMEM((TOKENS2, WIDTH), F32)] * 2,
        cost_estimate=pl.CostEstimate(
            flops=12 * TOKENS2 * WIDTH * FF_HALF,
            bytes_accessed=28 * 1024 * 1024,
            transcendentals=2 * TOKENS2 * FF_HALF,
        ),
        compiler_params=pltpu.CompilerParams(vmem_limit_bytes=38 * 1024 * 1024),
    )(where, *tokens, weights, weights, weights, weights)


def rows_of(ref, index, size):
    return ref[pl.ds(pl.multiple_of(index * size, size), size), :]


def out_grad_kernel(b_own, b_other, low, packed, other, g0, g1, g2, g3):
    branch = jnp.concatenate([b_own[...], b_other[...]], axis=0).T
    norms = split_pair(join_pair(packed[...]) + join_pair(other[...]))
    for pair, out in enumerate((g0, g1, g2, g3)):
        out[:WIDTH, :] = dot(branch, pair_columns(low, pair)).astype(BF)
        for k in range(8):
            out[WIDTH + 16 * k : WIDTH + 16 * k + 16, :] = norms[:, k * 128 : k * 128 + 128]


def main_grad_kernel(f_own, f_other, d_query, d_key, d_value, g0, g1, g2, g3):
    tokens = jnp.concatenate([f_own[...], f_other[...]], axis=0).T
    for pair, out in enumerate((g0, g1, g2, g3)):
        d_all = [pair_columns(d, pair) for d in (d_query, d_key, d_value)]
        out[...] = dot(tokens, jnp.concatenate(d_all, axis=1)).astype(BF)


def feed_sum_kernel(dim, where, *refs):
    for k, out in enumerate(refs[-4:]):
        place = lax.rem(where[dim] + k, 4)
        total = sum(rows_of(p, place, 64).astype(F32) for p in refs[:-4])
        out[...] = total.astype(out.dtype)


def feed_turn_kernel(u0, u1, u2, u3, d0, d1, d2, d3, *outs):
    ups = sum(r[...].astype(F32) for r in (u0, u1, u2, u3)).astype(BF)
    downs = sum(r[...].astype(F32) for r in (d0, d1, d2, d3)).astype(BF)
    for k, out in enumerate(outs):
        slot = (-k) % 4
        span = slice(slot * 512, slot * 512 + 512)
        out[:, :512] = ups[:, span]
        out[:, 512:] = downs[:, span]


def feed_end_kernel(p0, p1, p2, p3, up, down):
    total = sum(p[...].astype(F32) for p in (p0, p1, p2, p3))
    up[...] = total[:, :512]
    down[...] = total[:, 512:]


def main_cut_kernel(where, m0, m1, m2, m3, o0, o1, o2, o3, own, b1, b2, b3, norms):
    parts = []
    for p in (o0, o1, o2, o3):
        rows = [p[WIDTH + 16 * k : WIDTH + 16 * k + 16, :] for k in range(8)]
        parts.append(join_pair(jnp.concatenate(rows, axis=1)))
    total = split_pair(sum_in_order(parts, lambda a: lax.rem(where[2] - a + 4, 4)))
    norms[...] = total
    for k, out in enumerate((own, b1, b2, b3)):
        z = lax.rem(where[0] + k, 4)
        rows = sum(rows_of(p, z, 256).astype(F32) for p in (m0, m1, m2, m3))
        out[:256, :384] = rows.astype(out.dtype)
        rows = sum(rows_of(p, z, 256).astype(F32) for p in (o0, o1, o2, o3))
        out[:256, 384:] = rows.astype(out.dtype)
        if k:
            out[256:272, :] = total[:, :512]
            out[272:, :] = total[:, 512:]


def main_turn_kernel(where, own, p1, p2, p3, norms, *outs):
    pieces = [join_pair(norms[...])]
    for p in (p1, p2, p3):
        pieces.append(join_pair(jnp.concatenate([p[256:272, :], p[272:, :]], axis=1)))
    total = split_pair(sum_in_order(pieces, lambda a: lax.rem(where[0] - a + 4, 4)))
    for k, out in enumerate(outs):
        x = where[1] ^ k
        rows = rows_of(own, x, 64) + sum(rows_of(p, x, 64).astype(F32) for p in (p1, p2, p3))
        out[:64, :] = rows.astype(BF)
        out[64:80, :] = total[:, :512]
        out[80:, :] = total[:, 512:]


def main_end_kernel(where, p0, p1, p2, p3, query, key, value, out, n0, n1, n2, n3):
    pieces = (p0, p1, p2, p3)
    total = sum(p[:64, :].astype(F32) for p in pieces)
    for k, ref in enumerate((query, key, value, out)):
        ref[...] = total[:, k * 128 : k * 128 + 128]
    parts = [join_pair(jnp.concatenate([p[64:80, :], p[80:, :]], axis=1)) for p in pieces]
    norms = sum_in_order(parts, lambda a: where[3] ^ a)
    for k, ref in enumerate((n0, n1, n2, n3)):
        ref[...] = norms[k : k + 1, :]


def local(
    inputs,
    lengths,
    ln1_gain,
    ln1_bias,
    ln2_gain,
    ln2_bias,
    w_query,
    w_key,
    w_value,
    w_out,
    w_up,
    w_down,
    cotangent,
):
    z, y = lax.axis_index("z"), lax.axis_index("y")
    x = lax.axis_index(X)
    block = lax.axis_index(("xl", "y"))
    where = jnp.stack([z, x, y, lax.axis_index(("xh", "core"))]).astype(jnp.int32)
    gain_one, bias_one, gain_two, bias_two = [
        v.reshape(1, WIDTH) for v in (ln1_gain, ln1_bias, ln2_gain, ln2_bias)
    ]

    main, feed = call(
        prepare_kernel,
        stay(w_query, w_key, w_value, w_out.T, w_up, w_down.T),
        [bf16(64, 384), bf16(64, 1152)],
    )
    main = [turn_x(main, k) for k in range(4)]
    feed = after(feed, main)
    main = place(main, [x ^ k for k in range(4)])
    feed = [turn_y(feed, k) for k in range(4)]

    def gather(value, axis, index):
        got = {k: ring_shift(value, axis, k) for k in ORDER}
        places = [lax.rem(index - k + 4, 4) for k in range(4)]
        out = place([value, got[1], got[2], got[3]], places)
        return out.reshape(4 * value.shape[0], value.shape[1])

    qkv = gather(main.reshape(256, 384), "z", z)
    feed_rows, out_rows = call(
        feed_rows_kernel, after(feed, qkv), [away(bf16(64, 2 * FF_HALF)), bf16(64, HALF)]
    )
    feed_weights = lax.all_gather(feed_rows, ("z", "xh", "xl"), axis=0, tiled=True)
    got = {k: ring_shift(qkv, "y", k) for k in ORDER}
    qkv = [qkv, got[1], got[2], got[3]]
    out_rows = gather(gather(out_rows, X, x), "z", z)

    ends = jnp.cumsum(jnp.concatenate([lengths, core_swap(lengths)], axis=0), axis=1)

    def last_segment(which):
        return jnp.sum((which * BLOCK + BLOCK - 1 >= ends).astype(jnp.int32), axis=1)

    here = last_segment(block)
    before = jnp.where(block > 0, last_segment(block - 1), -1)
    zeros = jnp.zeros((2,), jnp.int32)
    flags = [(block >= k) & (last_segment(block - k) == before) for k in range(1, REACH + 1)]
    flags += [
        (block + k < 8) & (last_segment(block + k - 1) == here) for k in range(1, REACH + 1)
    ]
    rest = [zeros + block * BLOCK, before, here, zeros] + [f.astype(jnp.int32) for f in flags]
    info = jnp.concatenate([ends, jnp.stack(rest, axis=1)], axis=1)

    first_in, grad_low = call(
        first_norm_kernel, stay(inputs, cotangent, gain_one, bias_one), [SEND, SEND]
    )
    first = [first_in, core_swap(first_in)]
    grads = [grad_low, core_swap(grad_low)]

    feats, values, state = call(
        enter_kernel,
        first + qkv,
        [bf16(TOKENS2, WIDTH), WIDE16, STATE],
        [info],
        flops=2 * 512 * 1024 * 1600,
    )
    states = [tensor_shift(state, k) for k in range(1, REACH + 1)]
    numer, denom = attention_call(
        inner_kernel, info, [feats, values], [WIDE32, WIDE32], 4 * 2 * 256 * 256 * 128 * 8
    )
    attended, low, inverse, own, send = attention_call(
        join_kernel,
        info,
        [feats, numer, denom] + states + [out_rows],
        [WIDE32, WIDE16, WIDE32, OWN, SEND],
        2 * 512 * 1024 * 640,
    )
    hidden, second_in = call(
        second_norm_kernel,
        stay(inputs, gain_two, bias_two) + [own, core_swap(send)],
        [OWN, SEND],

    )
    feed_out = feed_forward(where, [second_in, core_swap(second_in)] + grads, feed_weights)
    up_blocks, down_blocks = feed_out[:4], feed_out[4]
    d_own, d_send, r_own, r_send = feed_out[5:]
    d_hidden, branch_low, sums = call(
        second_back_kernel,
        [hidden] + stay(gain_two) + [d_own, core_swap(d_send)] + stay(cotangent),
        [OWN, SEND, f32(8, WIDTH)],
    )
    branch = [branch_low, core_swap(branch_low)]

    down_part = lax.psum_scatter(down_blocks, "z", scatter_dimension=0, tiled=True)
    back_state, scaled, shift = attention_call(
        back_state_kernel,
        info,
        [feats, values, attended, inverse] + branch + [out_rows],
        [STATE, WIDE16, WIDE32],
        2 * 512 * 1024 * 640,
    )
    back_states = [tensor_shift(back_state, -k) for k in range(1, REACH + 1)]
    d_queries, d_key, d_value = attention_call(
        back_inner_kernel,
        info,
        [feats, values, scaled, shift] + states,
        [WIDE16, WIDE32, WIDE32],
        10 * 2 * 256 * 256 * 128 * 8,
    )
    late = after(up_blocks, back_states)
    up_got = {0: up_blocks[0]}
    up_got[1] = ring_shift(late[1], X, 1)
    up_got[3] = ring_shift(late[3], X, 3)
    d_keys, d_values, own, send = attention_call(
        back_join_kernel,
        info,
        [feats, values, d_queries, d_key, d_value] + back_states + qkv,
        [WIDE16, WIDE16, OWN, SEND],
        2 * 512 * 1024 * 2000,
    )
    up_got[2] = ring_shift(after(up_blocks[2], d_keys), X, 2)
    main_grad = call(
        main_grad_kernel,
        first + [d_queries, d_keys, d_values],
        [bf16(WIDTH, 384)] * 4,
        flops=2 * 512 * 1024 * 1536,
    )
    grad_inputs, packed = call(
        first_back_kernel,
        stay(inputs, gain_one) + [own, core_swap(send), d_hidden, sums],
        [away(OWN), bf16(16, WIDTH)],
    )
    result = hidden + (r_own + core_swap(after(r_send, d_keys)).astype(F32))

    main_got = [main_grad[0]] + [ring_shift(main_grad[(-k) % 4], "y", k) for k in ORDER]
    out_grad = call(
        out_grad_kernel,
        branch + [low] + [packed, core_swap(packed)],
        [bf16(WIDTH + 128, 128)] * 4,
        flops=2 * 512 * 1024 * 512,
    )
    out_got = {k: ring_shift(out_grad[(-k) % 4], "y", k) for k in ORDER}
    out_got = [out_grad[0], out_got[1], out_got[2], out_got[3]]

    def feed_sum(dim):
        def kernel(*refs):
            feed_sum_kernel(dim, *refs)

        return kernel

    outs = [f32(64, FF_HALF)] + [bf16(64, FF_HALF)] * 3
    downs = call(feed_sum(1), after([down_part], out_grad), outs, [where])
    ups = call(feed_sum(0), after([up_got[k] for k in range(4)], out_grad), outs, [where])
    downs = [downs[0]] + [ring_shift(downs[k], X, k) for k in ORDER]
    ups = [ups[0]] + [ring_shift(ups[k], "z", k) for k in ORDER]
    sent = call(feed_turn_kernel, ups + downs, [bf16(64, WIDTH)] * 4)
    grad_up, grad_down = call(
        feed_end_kernel, [turn_y(sent[k], k) for k in range(4)], [f32(64, 512), f32(64, 512)]
    )

    cut = call(
        main_cut_kernel,
        main_got + out_got,
        [f32(256, 512)] + [bf16(288, 512)] * 3 + [bf16(16, WIDTH)],
        [where],
    )
    norms = cut[4]
    got = {k: ring_shift(cut[k], "z", k) for k in ORDER}
    sent = call(
        main_turn_kernel, [cut[0], got[1], got[2], got[3], norms], [bf16(96, 512)] * 4, [where]
    )
    ends = call(
        main_end_kernel,
        [turn_x(sent[k], k, True) for k in range(4)],
        [f32(64, 128)] * 4 + [f32(1, WIDTH)] * 4,
        [where],
    )
    norms = [v.reshape(WIDTH) for v in ends[4:]]
    return (
        result,
        grad_inputs,
        norms[0],
        norms[1],
        norms[2],
        norms[3],
        ends[0],
        ends[1],
        ends[2],
        ends[3].T,
        grad_up,
        grad_down.T,
    )


def solution(mesh):
    axes = ("z", "xh", "core", "xl", "y")
    split = Mesh(mesh.devices.reshape(4, 2, 2, 2, 4), axes)
    dp, tensor = ("z", "xh", "core"), ("xl", "y")
    tokens, rows, cols = P(axes, None), P(dp, tensor), P(tensor, dp)
    in_specs = (tokens, P(dp, None), P(), P(), P(), P(), rows, rows, rows, cols, rows, cols, tokens)
    out_specs = (tokens, tokens, P(), P(), P(), P(), rows, rows, rows, cols, rows, cols)
    return jax.shard_map(
        local, mesh=split, in_specs=in_specs, out_specs=out_specs, check_vma=False
    )
```

```python
import jax
import jax.numpy as jnp
from jax import lax
from jax.experimental import pallas as pl
from jax.experimental.pallas import tpu as pltpu
from jax.sharding import Mesh, PartitionSpec as P

BF = jnp.bfloat16
F32 = jnp.float32
EPS = 1e-05
BLOCK = 256
WIDTH = 1024
HALF = 512
FF_HALF = 2048
PAIRS = 4
STATE_ROWS = 80
X = ("xh", "xl")
REACH = 4


def dot(left, right, left_dim=1, right_dim=0):
    return lax.dot_general(
        left, right, (((left_dim,), (right_dim,)), ((), ())), preferred_element_type=F32
    )


def ring_shift(value, axis, step):
    return lax.ppermute(value, axis, [(i, (i + step) % 4) for i in range(4)])


def ring_trade(blocks, axis):
    got = {k: ring_shift(blocks[k], axis, k) for k in (1, 3, 2)}
    return [blocks[0], got[1], got[2], got[3]]


def core_swap(value):
    return lax.ppermute(value, "core", [(0, 1), (1, 0)])


def tensor_shift(value, step):
    return lax.ppermute(
        value, ("xl", "y"), [(i, i + step) for i in range(8) if 0 <= i + step < 8]
    )


def turn_y(value, step):
    pairs = []
    for c in range(2):
        for xl in range(2):
            for y in range(4):
                pairs.append(((c * 2 + xl) * 4 + y, (xl * 2 + c) * 4 + (y + step) % 4))
    return lax.ppermute(value, ("core", "xl", "y"), pairs)


def turn_x(value, step, back=False):
    high, low = step // 2, step % 2
    pairs = []
    for xh in range(2):
        for c in range(2):
            for xl in range(2):
                core, x_low = (xl ^ low, c) if back else (xl, c ^ low)
                pairs.append(((xh * 2 + c) * 2 + xl, ((xh ^ high) * 2 + core) * 2 + x_low))
    return lax.ppermute(value, ("xh", "core", "xl"), pairs)


def after(values, earlier):
    return lax.optimization_barrier((values, earlier))[0]


def place(pieces, positions):
    out = jnp.zeros((4,) + pieces[0].shape, pieces[0].dtype)
    for piece, position in zip(pieces, positions):
        out = lax.dynamic_update_index_in_dim(out, piece, position, 0)
    return out


def trade(blocks, axis):
    return lax.all_to_all(blocks, axis, split_axis=0, concat_axis=0, tiled=True)


def spread(value, axis):
    return trade(jnp.broadcast_to(value, (4,) + value.shape), axis)


def stay(*values):
    return [pltpu.with_memory_space_constraint(v, pltpu.HBM) for v in values]


def away(shape):
    return pltpu.HBM(shape.shape, shape.dtype)


COST = pl.CostEstimate(flops=1000, bytes_accessed=1000, transcendentals=0)


def call(kernel, operands, outs, scalars=(), limit=24, scratch=()):
    def whole(value):
        return pl.BlockSpec(value.shape, lambda i: (0,) * len(value.shape))

    return pl.pallas_call(
        kernel,
        grid=(1,),
        in_specs=[pl.BlockSpec(memory_space=pltpu.SMEM)] * len(scalars)
        + [whole(o) for o in operands],
        out_specs=[whole(o) for o in outs],
        out_shape=list(outs),
        scratch_shapes=list(scratch),
        cost_estimate=COST,
        compiler_params=pltpu.CompilerParams(vmem_limit_bytes=limit * 1024 * 1024),
    )(*scalars, *operands)


def f32(*shape):
    return jax.ShapeDtypeStruct(shape, F32)


def bf16(*shape):
    return jax.ShapeDtypeStruct(shape, BF)


def lanes(shape):
    return lax.broadcasted_iota(jnp.int32, shape, 1)


def head_sums(values):
    left = lanes(values.shape) < 64
    first = jnp.sum(jnp.where(left, values, 0.0), axis=1, keepdims=True)
    second = jnp.sum(jnp.where(left, 0.0, values), axis=1, keepdims=True)
    return jnp.where(left, first, second)


def segments_of(info, group, places):
    return sum((places >= info[group, k]).astype(jnp.int32) for k in range(4))


def column_segments(info, group):
    base = info[group, 4]
    return segments_of(info, group, base + lax.broadcasted_iota(jnp.int32, (BLOCK, 1), 0))


def pair_mask(info, group):
    base = info[group, 4]
    rows = lax.broadcasted_iota(jnp.int32, (BLOCK, 1), 0)
    cols = lax.broadcasted_iota(jnp.int32, (1, BLOCK), 1)
    row_seg = segments_of(info, group, base + rows)
    col_seg = segments_of(info, group, base + cols)
    return (rows >= cols) & (row_seg == col_seg)


def carried_of(info, group):
    return column_segments(info, group) == info[group, 5]


def in_last_of(info, group):
    return column_segments(info, group) == info[group, 6]


def masked_mean(values, keep):
    count = jnp.maximum(jnp.sum(keep.astype(F32), axis=0, keepdims=True), 1.0)
    mean = jnp.sum(jnp.where(keep, values, 0.0), axis=0, keepdims=True) / count
    return mean.astype(BF).astype(F32)


def pack_state(matrix, row, center, out, group, pair):
    left = lanes((64, 128)) < 64
    out[group, pair, :64, :] = jnp.where(left, matrix[:64], matrix[64:]).astype(BF)
    high = row.astype(BF).astype(F32)
    place = lax.broadcasted_iota(jnp.int32, (STATE_ROWS - 64, 128), 0)
    rest = jnp.where(place == 0, high, jnp.where(place == 1, row - high, 0.0))
    out[group, pair, 64:, :] = jnp.where(place == 2, center, rest).astype(BF)


def unpack_states(info, group, states, pair, flags):
    left = lanes((64, 128)) < 64
    parts, rows, centers = [], [], []
    for k, state in enumerate(states, 1):
        keep = info[group, flags + k - 1].astype(F32)
        packed = state[0, pair].astype(F32) * keep
        memory = packed[:64]
        parts.append(
            jnp.concatenate([jnp.where(left, memory, 0.0), jnp.where(left, 0.0, memory)], axis=0)
        )
        rows.append(packed[64:65] + packed[65:66])
        centers.append(packed[66:67])
    return parts, rows, centers


def pair_columns(ref, pair):
    return ref[:, pair * 128 : pair * 128 + 128]


def enter_kernel(info, own, other, wqkv, queries, keys, values, out):
    tokens = jnp.concatenate([own[...], other[...]], axis=0)
    both = jnp.concatenate([wqkv[0, :, 256:], wqkv[1, :, 256:]], axis=1)
    values[...] = dot(tokens, both).astype(BF)
    for pair in range(2):
        feat = dot(tokens, wqkv[pair, :, :256])
        feat = jnp.where(feat > 0.0, feat + 1.0, jnp.exp(jnp.minimum(feat, 0.0))).astype(BF)
        queries[:, pair * 128 : pair * 128 + 128] = feat[:, :128]
        keys[:, pair * 128 : pair * 128 + 128] = feat[:, 128:]
    for group in range(2):
        last = in_last_of(info, group)
        rows = slice(group * BLOCK, group * BLOCK + BLOCK)
        for pair in range(2):
            span = slice(pair * 128, pair * 128 + 128)
            v = values[rows, span].astype(F32)
            kept = jnp.where(last, keys[rows, span].astype(F32), 0.0)
            center = masked_mean(v, last)
            matrix = dot(kept.astype(BF), (v - center).astype(BF), 0, 0)
            row = jnp.sum(kept, axis=0, keepdims=True)
            pack_state(matrix, row, center, out, group, pair)


def enter(info, tokens, wqkv):
    whole = pl.BlockSpec((BLOCK, WIDTH), lambda j: (0, 0))
    columns = pl.BlockSpec((TOKENS2, 256), lambda j: (0, j))
    return pl.pallas_call(
        enter_kernel,
        grid=(2,),
        in_specs=[
            pl.BlockSpec(memory_space=pltpu.SMEM),
            whole,
            whole,
            pl.BlockSpec((2, WIDTH, 384), lambda j: (j, 0, 0)),
        ],
        out_specs=[columns] * 3
        + [pl.BlockSpec((2, 2, STATE_ROWS, 128), lambda j: (0, j, 0, 0))],
        out_shape=[away(WIDE16)] * 3 + [STATE],
        cost_estimate=COST,
        compiler_params=pltpu.CompilerParams(vmem_limit_bytes=24 * 1024 * 1024),
    )(info, *tokens, *stay(wqkv))


def inner_kernel(info, queries, keys, values, numer, denom):
    group = pl.program_id(0)
    allowed = pair_mask(info, group)
    left = lanes((BLOCK, 128)) < 64
    for pair in range(PAIRS):
        q, k = pair_columns(queries, pair), pair_columns(keys, pair)
        v = pair_columns(values, pair)
        zero = jnp.zeros_like(q)
        parts = []
        for side in (left, jnp.logical_not(left)):
            scores = jnp.where(allowed, dot(jnp.where(side, q, zero), k, 1, 1), 0.0)
            parts.append((dot(scores.astype(BF), v), jnp.sum(scores, axis=1, keepdims=True)))
        span = slice(pair * 128, pair * 128 + 128)
        numer[:, span] = jnp.where(left, parts[0][0], parts[1][0])
        denom[:, span] = jnp.where(left, parts[0][1], parts[1][1])


def store_halves(group, partial, own, send):
    @pl.when(group == 0)
    def _():
        own[...] = partial

    @pl.when(group == 1)
    def _():
        send[...] = partial.astype(BF)


def join_kernel(
    info, queries, numer, denom, s1, s2, s3, s4, out_rows, wide, low, inverse, own, send
):
    group = pl.program_id(0)
    carried = carried_of(info, group)
    outs = []
    for pair in range(PAIRS):
        q = pair_columns(queries, pair)
        parts, rows, centers = unpack_states(info, group, (s1, s2, s3, s4), pair, 8)
        num, den = dot(q, sum(parts).astype(BF)), 0.0
        for row, center in zip(rows, centers):
            weight = head_sums(q.astype(F32) * row)
            num, den = num + weight * center, den + weight
        inv = 1.0 / (pair_columns(denom, pair) + jnp.where(carried, den, 0.0))
        out = (pair_columns(numer, pair) + jnp.where(carried, num, 0.0)) * inv
        span = slice(pair * 128, pair * 128 + 128)
        wide[:, span] = out
        inverse[:, span] = inv
        outs.append(out.astype(BF))
        low[:, span] = outs[-1]
    partial = dot(jnp.concatenate(outs, axis=1), out_rows[...], 1, 1)
    store_halves(group, partial, own, send)


def back_state_kernel(
    info, queries, values, attended, inverse, b_own, b_other, out_rows, out, scaled, shift
):
    group = pl.program_id(0)
    carried = carried_of(info, group)
    branch = jnp.where(group == 0, b_own[...], b_other[...])
    grad = dot(branch, out_rows[...]).astype(BF).astype(F32)
    for pair in range(PAIRS):
        span = slice(pair * 128, pair * 128 + 128)
        g = (grad[:, span] * pair_columns(inverse, pair)).astype(BF)
        wide = g.astype(F32)
        e = -head_sums(wide * pair_columns(attended, pair))
        scaled[:, span] = g
        shift[:, span] = e
        center = masked_mean(pair_columns(values, pair).astype(F32), carried)
        kept = jnp.where(carried, pair_columns(queries, pair).astype(F32), 0.0)
        row = jnp.sum(kept * (e + head_sums(wide * center)), axis=0, keepdims=True)
        pack_state(dot(kept.astype(BF), g, 0, 0), row, center, out, 0, pair)


def back_inner_kernel(
    info, queries, keys, values, scaled, shift, s1, s2, s3, s4, d_query, d_key, d_value
):
    group = pl.program_id(0)
    allowed = pair_mask(info, group)
    carried = carried_of(info, group)
    left = lanes((BLOCK, 128)) < 64
    for pair in range(PAIRS):
        q, k = pair_columns(queries, pair), pair_columns(keys, pair)
        v, g, e = [pair_columns(r, pair) for r in (values, scaled, shift)]
        zero = jnp.zeros_like(q)
        parts = []
        for head, side in enumerate((left, jnp.logical_not(left))):
            scores = jnp.where(allowed, dot(jnp.where(side, q, zero), k, 1, 1), 0.0).astype(BF)
            d_scores = dot(jnp.where(side, g, zero), v, 1, 1) + e[:, 64 * head : 64 * head + 1]
            d_scores = jnp.where(allowed, d_scores, 0.0).astype(BF)
            parts.append((dot(d_scores, k), dot(d_scores, q, 0, 0), dot(scores, g, 0, 0)))
        dq, dk, dv = [jnp.where(left, a, b) for a, b in zip(*parts)]
        memories, rows, centers = unpack_states(info, group, (s1, s2, s3, s4), pair, 8)
        more = dot(g, sum(memories).astype(BF), 1, 1)
        for row, center in zip(rows, centers):
            more = more + row * (e + head_sums(g.astype(F32) * center))
        dq = dq + jnp.where(carried, more, 0.0)
        span = slice(pair * 128, pair * 128 + 128)
        d_query[:, span] = (dq * jnp.minimum(q.astype(F32), 1.0)).astype(BF)
        d_key[:, span] = dk
        d_value[:, span] = dv


def back_join_kernel(
    info, keys, values, d_query, d_key, d_value, s1, s2, s3, s4, wqkv,
    key_out, value_out, own, send,
):
    group = pl.program_id(0)
    last = in_last_of(info, group)
    partial = 0.0
    for pair in range(PAIRS):
        k, v = pair_columns(keys, pair), pair_columns(values, pair)
        memories, rows, centers = unpack_states(info, group, (s1, s2, s3, s4), pair, 12)
        memory = sum(memories).astype(BF)
        center, row = centers[0], rows[0]
        for m, r, c in zip(memories[1:], rows[1:], centers[1:]):
            away = jnp.broadcast_to(center - c, (16, 128)).astype(BF)
            row = row + r + dot(away, m.astype(BF), 1, 1)[:1]
        more = dot((v.astype(F32) - center).astype(BF), memory, 1, 1) + row
        dk = pair_columns(d_key, pair) + jnp.where(last, more, 0.0)
        dv = pair_columns(d_value, pair) + jnp.where(last, dot(k, memory), 0.0)
        span = slice(pair * 128, pair * 128 + 128)
        dk = (dk * jnp.minimum(k.astype(F32), 1.0)).astype(BF)
        dv = dv.astype(BF)
        key_out[:, span] = dk
        value_out[:, span] = dv
        d_pair = jnp.concatenate([pair_columns(d_query, pair), dk, dv], axis=1)
        partial = partial + dot(d_pair, wqkv[pair], 1, 1)
    store_halves(group, partial, own, send)


def attention_call(kernel, info, operands, outs, weights=()):
    def spec(shape):
        if len(shape) == 4:
            return pl.BlockSpec((1,) + shape[1:], lambda g: (g, 0, 0, 0))
        if shape[0] == TOKENS2:
            return pl.BlockSpec((BLOCK, shape[1]), lambda g: (g, 0))
        return pl.BlockSpec(shape, lambda g: (0, 0))

    def fixed(shape, index):
        return pl.BlockSpec(shape, lambda g: index)

    return pl.pallas_call(
        kernel,
        grid=(2,),
        in_specs=[pl.BlockSpec(memory_space=pltpu.SMEM)]
        + [spec(a.shape) for a in operands]
        + [fixed(shape, index) for _, shape, index in weights],
        out_specs=[spec(o.shape) for o in outs],
        out_shape=outs,
        cost_estimate=COST,
        compiler_params=pltpu.CompilerParams(vmem_limit_bytes=32 * 1024 * 1024),
    )(info, *operands, *stay(*[w for w, _, _ in weights]))


TOKENS2 = 2 * BLOCK
STATE = bf16(2, PAIRS, STATE_ROWS, 128)
WIDE32 = f32(TOKENS2, HALF)
WIDE16 = bf16(TOKENS2, HALF)
OWN = f32(BLOCK, WIDTH)
SEND = bf16(BLOCK, WIDTH)


def prepare_kernel(w_query, w_key, w_value, w_out, w_up, w_down, main, feed):
    main[:, :128] = w_query[...].astype(BF)
    main[:, 128:256] = w_key[...].astype(BF)
    main[:, 256:384] = w_value[...].astype(BF)
    main[:, 384:] = w_out[...].astype(BF)
    feed[:, :512] = w_up[...].astype(BF)
    feed[:, 512:] = w_down[...].astype(BF)


def unit_of(values):
    centred = values - jnp.mean(values, axis=-1, keepdims=True)
    scale = lax.rsqrt(jnp.mean(centred * centred, axis=-1, keepdims=True) + EPS)
    return centred * scale, scale


def feed_rows_kernel(p0, p1, p2, p3, feed):
    for k, p in enumerate((p0, p1, p2, p3)):
        feed[:, k * 512 : k * 512 + 512] = p[:, :512]
        feed[:, FF_HALF + k * 512 : FF_HALF + k * 512 + 512] = p[:, 512:]


def out_rows_kernel(where, p0, p1, p2, p3, rows):
    for k, p in enumerate((p0, p1, p2, p3)):
        y = lax.rem(where[2] - k + 4, 4)
        rows[:, pl.ds(pl.multiple_of(y * 128, 128), 128)] = p[...]


def first_norm_kernel(inputs, cotangent, gain, bias, first_in, grad_low):
    unit, _ = unit_of(inputs[...])
    first_in[...] = (unit * gain[...] + bias[...]).astype(BF)
    grad_low[...] = cotangent[...].astype(BF)


def second_norm_kernel(inputs, gain, bias, own, got, hidden, second_in):
    total = inputs[...] + (own[...] + got[...].astype(F32))
    hidden[...] = total
    unit, _ = unit_of(total)
    second_in[...] = (unit * gain[...] + bias[...]).astype(BF)


def norm_slope(values, gain, own, got):
    unit, scale = unit_of(values[...])
    d_out = own[...] + got[...].astype(F32)
    gh = d_out * gain[...]
    slope = scale * (
        gh
        - jnp.mean(gh, axis=-1, keepdims=True)
        - unit * jnp.mean(gh * unit, axis=-1, keepdims=True)
    )
    gains = jnp.sum(d_out * unit, axis=0, keepdims=True)
    return slope, gains, jnp.sum(d_out, axis=0, keepdims=True)


def second_back_kernel(hidden, gain, own, got, cotangent, d_hidden, low, sums):
    slope, gains, biases = norm_slope(hidden, gain, own, got)
    total = cotangent[...] + slope
    d_hidden[...] = total
    low[...] = total.astype(BF)
    sums[...] = jnp.zeros_like(sums)
    sums[2:3, :] = gains
    sums[3:4, :] = biases


def split_pair(sums):
    high = sums.astype(BF).astype(F32)
    return jnp.concatenate([high, sums - high], axis=0).astype(BF)


def join_pair(packed):
    wide = packed.astype(F32)
    return wide[:8] + wide[8:]


def first_back_kernel(inputs, gain, d_hidden, own, got, sums, grad_inputs, packed):
    slope, gains, biases = norm_slope(inputs, gain, own, got)
    grad_inputs[...] = d_hidden[...] + slope
    place = lax.broadcasted_iota(jnp.int32, sums.shape, 0)
    total = jnp.where(place == 0, gains, jnp.where(place == 1, biases, sums[...]))
    packed[...] = split_pair(total)


def sum_in_order(pieces, position):
    total = 0.0
    for a in range(4):
        k = position(a)
        total = total + sum(jnp.where(k == i, p, 0.0) for i, p in enumerate(pieces))
    return total


FF_STEP = 512
FF_STEPS = FF_HALF // FF_STEP


def gelu_parts(u):
    density = jnp.exp(-0.5 * u * u) * 0.3989422804014327
    return 0.5 * (1.0 + lax.erf(u * 0.7071067811865476)), density


def feed_kernel(
    s_own, s_other, g_own, g_other, up, down,
    up_out, down_out, d_own, d_send, r_own, r_send,
    second, grad, second_t, grad_t, d_total, r_total,
):
    step = pl.program_id(0)

    @pl.when(step == 0)
    def _():
        second[:BLOCK] = s_own[...]
        second[BLOCK:] = s_other[...]
        grad[:BLOCK] = g_own[...]
        grad[BLOCK:] = g_other[...]
        second_t[...] = second[...].T
        grad_t[...] = grad[...].T
        d_total[...] = jnp.zeros_like(d_total)
        r_total[...] = jnp.zeros_like(r_total)

    u = dot(second[...], up[...])
    d_act = dot(grad[...], down[...])
    below, density = gelu_parts(u)
    act = (u * below).astype(BF)
    d_up = (d_act * (below + u * density)).astype(BF)
    down_out[...] = dot(grad_t[...], act).astype(BF)
    up_out[...] = dot(second_t[...], d_up).astype(BF)
    d_total[...] += dot(d_up, up[...], 1, 1)
    r_total[...] += dot(act, down[...], 1, 1)

    @pl.when(step == FF_STEPS - 1)
    def _():
        d_own[...] = d_total[:BLOCK]
        d_send[...] = d_total[BLOCK:].astype(BF)
        r_own[...] = r_total[:BLOCK]
        r_send[...] = r_total[BLOCK:].astype(BF)


def feed_forward(tokens, weights):
    whole = pl.BlockSpec((BLOCK, WIDTH), lambda j: (0, 0))

    def columns(rows, offset=0):
        return pl.BlockSpec((rows, FF_STEP), lambda j: (0, j + offset))

    (weights,) = stay(weights)
    return pl.pallas_call(
        feed_kernel,
        grid=(FF_STEPS,),
        in_specs=[whole] * 4 + [columns(WIDTH), columns(WIDTH, FF_STEPS)],
        out_specs=[columns(WIDTH)] * 2 + [whole] * 4,
        out_shape=[away(bf16(WIDTH, FF_HALF))] * 2
        + [away(v) for v in (OWN, SEND, OWN, SEND)],
        scratch_shapes=[pltpu.VMEM((TOKENS2, WIDTH), BF)] * 2
        + [pltpu.VMEM((WIDTH, TOKENS2), BF)] * 2
        + [pltpu.VMEM((TOKENS2, WIDTH), F32)] * 2,
        cost_estimate=COST,
        compiler_params=pltpu.CompilerParams(vmem_limit_bytes=40 * 1024 * 1024),
    )(*tokens, weights, weights)


def rows_of(ref, index, size):
    return ref[pl.ds(pl.multiple_of(index * size, size), size), :]


def value_grad_kernel(
    where, f_own, f_other, b_own, b_other, d_value, low, v0, v1, v2, v3, first_t, branch_t
):
    first_t[...] = jnp.concatenate([f_own[...], f_other[...]], axis=0).T
    branch_t[...] = jnp.concatenate([b_own[...], b_other[...]], axis=0).T
    for k, part in enumerate((v0, v1, v2, v3)):
        x = lax.rem(where[1] + k, 4)
        for half, (left, right) in enumerate(((first_t, d_value), (branch_t, low))):
            rows = jnp.concatenate([rows_of(left, 4 * z + x, 64) for z in range(4)], axis=0)
            part[:, half * HALF : half * HALF + HALF] = dot(rows, right[...]).astype(BF)


def query_grad_kernel(f_own, f_other, d_query, d_key, packed, other, out):
    first = jnp.concatenate([f_own[...], f_other[...]], axis=0).T
    norms = split_pair(join_pair(packed[...]) + join_pair(other[...]))
    for pair in range(PAIRS):
        d_all = [pair_columns(d, pair) for d in (d_query, d_key)]
        out[pair, :WIDTH, :] = dot(first, jnp.concatenate(d_all, axis=1)).astype(BF)
        for j in range(4):
            at = WIDTH + 16 * j
            out[pair, at : at + 16, :] = norms[:, j * 256 : j * 256 + 256]


def feed_cut_kernel(where, part, *outs):
    for k, out in enumerate(outs):
        out[...] = rows_of(part, lax.rem(where[1] + k, 4), 64)


def sum_of(pieces, *index):
    return sum(pieces[(j,) + index].astype(F32) for j in range(4))


def feed_turn_kernel(where, u0, u1, u2, u3, d0, d1, d2, d3, values, *outs):
    for k, out in enumerate(outs):
        slot = (-k) % 4
        span = slice(slot * 512, slot * 512 + 512)
        out[:, :512] = sum(p[:, span].astype(F32) for p in (u0, u1, u2, u3)).astype(BF)
        out[:, 512:1024] = sum(p[:, span].astype(F32) for p in (d0, d1, d2, d3)).astype(BF)
        y = lax.rem(where[2] + k, 4)
        for half in range(2):
            span = pl.ds(pl.multiple_of(half * HALF + y * 128, 128), 128)
            out[:, 1024 + half * 128 : 1152 + half * 128] = values[:, span]


def feed_end_kernel(p0, p1, p2, p3, up, down, value, out):
    total = sum(p[...].astype(F32) for p in (p0, p1, p2, p3))
    up[...] = total[:, :512]
    down[...] = total[:, 512:1024]
    value[...] = total[:, 1024:1152]
    out[...] = total[:, 1152:]


def main_cut_kernel(main, v0, v1, v2, v3, out):
    parts = []
    for j in range(4):
        rows = [main[j, WIDTH + 16 * i : WIDTH + 16 * i + 16, :] for i in range(4)]
        parts.append(join_pair(jnp.concatenate(rows, axis=1)))
    total = split_pair(sum(parts))
    for z in range(4):
        rows = slice(z * 256, z * 256 + 256)
        out[z, :256, :] = sum_of(main, rows, slice(None)).astype(BF)
        rows = slice(z * 64, z * 64 + 64)
        for j in range(4):
            span = slice(j * 256, j * 256 + 256)
            out[z, 256 + 16 * j : 272 + 16 * j, :] = total[:, span]
            values = sum(p[rows, span].astype(F32) for p in (v0, v1, v2, v3))
            out[z, 320 + 64 * j : 384 + 64 * j, :] = values.astype(BF)


def main_turn_kernel(where, main, o0, o1, o2, o3, values):
    pieces = []
    for j in range(4):
        rows = [main[j, 256 + 16 * i : 272 + 16 * i, :] for i in range(4)]
        pieces.append(join_pair(jnp.concatenate(rows, axis=1)))
    norms = split_pair(sum(pieces))
    for j in range(4):
        rows = slice(320 + 64 * j, 384 + 64 * j)
        values[:, j * 256 : j * 256 + 256] = sum_of(main, rows, slice(None)).astype(BF)
    for k, out in enumerate((o0, o1, o2, o3)):
        rows = pl.ds(pl.multiple_of((where[1] ^ k) * 64, 64), 64)
        out[:64, :] = sum_of(main, rows, slice(None)).astype(BF)
        for i in range(4):
            out[64 + 16 * i : 80 + 16 * i, :] = norms[:, i * 256 : i * 256 + 256]


def main_end_kernel(where, p0, p1, p2, p3, query, key, n0, n1, n2, n3):
    pieces = (p0, p1, p2, p3)
    total = sum(p[:64, :].astype(F32) for p in pieces)
    query[...] = total[:, :128]
    key[...] = total[:, 128:]
    parts = []
    for p in pieces:
        rows = [p[64 + 16 * i : 80 + 16 * i, :] for i in range(4)]
        parts.append(join_pair(jnp.concatenate(rows, axis=1)))
    norms = sum_in_order(parts, lambda a: where[3] ^ a)
    for k, ref in enumerate((n0, n1, n2, n3)):
        ref[...] = norms[k : k + 1, :]


def local(
    inputs,
    lengths,
    ln1_gain,
    ln1_bias,
    ln2_gain,
    ln2_bias,
    w_query,
    w_key,
    w_value,
    w_out,
    w_up,
    w_down,
    cotangent,
):
    x = lax.axis_index(X)
    block = lax.axis_index(("xl", "y"))
    z = lax.axis_index("z")
    where = [z, x, lax.axis_index("y"), lax.axis_index(("xh", "core"))]
    where = jnp.stack(where).astype(jnp.int32)
    gain_one, bias_one, gain_two, bias_two = [
        v.reshape(1, WIDTH) for v in (ln1_gain, ln1_bias, ln2_gain, ln2_bias)
    ]

    main, feed = call(
        prepare_kernel,
        stay(w_query, w_key, w_value, w_out.T, w_up, w_down.T),
        [bf16(64, 512), bf16(64, 1024)],
    )
    main = [turn_x(main, k) for k in range(4)]
    feed = after(feed, main)
    main = place(main, [x ^ k for k in range(4)]).reshape(256, 512)
    wo = ring_trade([main[:, 384:]] * 4, "y")
    main = spread(main[:, :384], "z").reshape(WIDTH, 384)
    main = after(main, wo)
    feed = [turn_y(feed, k) for k in range(4)]
    (feed_rows,) = call(
        feed_rows_kernel, after(feed, main), [away(bf16(64, 2 * FF_HALF))]
    )
    feed_weights = lax.all_gather(feed_rows, ("z", "xh", "xl"), axis=0, tiled=True)
    wqkv = spread(main, "y")
    (wo,) = call(out_rows_kernel, wo, [bf16(256, HALF)], [where])
    wo = ring_trade([wo] * 4, "z")
    wo = place(wo, [lax.rem(z - k + 4, 4) for k in range(4)]).reshape(WIDTH, HALF)
    wqkv = after(wqkv, wo)
    wo = (wo, (WIDTH, HALF), (0, 0))
    ends = jnp.cumsum(jnp.concatenate([lengths, core_swap(lengths)], axis=0), axis=1)

    def last_segment(which):
        return jnp.sum((which * BLOCK + BLOCK - 1 >= ends).astype(jnp.int32), axis=1)

    here = last_segment(block)
    before = jnp.where(block > 0, last_segment(block - 1), -1)
    zeros = jnp.zeros((2,), jnp.int32)
    flags = [(block >= k) & (last_segment(block - k) == before) for k in range(1, REACH + 1)]
    flags += [
        (block + k < 8) & (last_segment(block + k - 1) == here) for k in range(1, REACH + 1)
    ]
    rest = [zeros + block * BLOCK, before, here, zeros] + [f.astype(jnp.int32) for f in flags]
    info = jnp.concatenate([ends, jnp.stack(rest, axis=1)], axis=1)

    first_in, grad_low = call(
        first_norm_kernel, stay(inputs, cotangent, gain_one, bias_one), [SEND, away(SEND)]
    )
    first = [first_in, core_swap(first_in)]
    grads = [grad_low, core_swap(grad_low)]

    queries, keys, values, state = enter(info, first, wqkv)
    queries, keys, values = stay(queries, keys, values)
    states = [tensor_shift(state, k) for k in range(1, REACH + 1)]
    numer, denom = attention_call(
        inner_kernel, info, [queries, keys, values], [WIDE32, WIDE32]
    )
    attended, low, inverse, own, send = attention_call(
        join_kernel,
        info,
        [queries, numer, denom] + states,
        [away(WIDE32), away(WIDE16), away(WIDE32), OWN, SEND],
        [wo],
    )
    hidden, second_in = call(
        second_norm_kernel,
        stay(inputs, gain_two, bias_two) + [own, core_swap(send)],
        [away(OWN), SEND],
    )
    ups, downs, d_own, d_send, r_own, r_send = feed_forward(
        [second_in, core_swap(second_in)] + stay(*grads), feed_weights
    )
    d_hidden, branch_low, sums = call(
        second_back_kernel,
        stay(hidden, gain_two, d_own) + [core_swap(d_send)] + stay(cotangent),
        [away(OWN), SEND, f32(8, WIDTH)],
    )
    branch = [branch_low, core_swap(branch_low)]

    downs = lax.psum_scatter(downs, "z", scatter_dimension=0, tiled=True)
    ups = lax.psum_scatter(ups, "z", scatter_dimension=0, tiled=True)

    back_state, scaled, shift = attention_call(
        back_state_kernel,
        info,
        [queries, values] + stay(attended, inverse) + branch,
        [STATE, WIDE16, WIDE32],
        [wo],
    )
    back_states = [tensor_shift(back_state, -k) for k in range(1, REACH + 1)]
    d_queries, d_key, d_value = attention_call(
        back_inner_kernel,
        info,
        [queries, keys, values, scaled, shift] + stay(*states),
        [WIDE16, WIDE32, WIDE32],
    )
    d_keys, d_values, own, send = attention_call(
        back_join_kernel,
        info,
        [keys, values, d_queries, d_key, d_value] + back_states,
        [WIDE16, WIDE16, OWN, SEND],
        [(wqkv, (4, WIDTH, 384), (0, 0, 0))],
    )
    gvo = call(
        value_grad_kernel,
        first + branch + [d_values, low],
        [away(bf16(256, WIDTH))] * 4,
        [where],
        limit=32,
        scratch=[pltpu.VMEM((WIDTH, TOKENS2), BF)] * 2,
    )
    sums = after(sums, gvo)
    gvo = ring_trade(gvo, X)
    grad_inputs, packed = call(
        first_back_kernel,
        stay(inputs, gain_one, d_hidden) + [own, core_swap(send), sums],
        [away(OWN), bf16(16, WIDTH)],
    )
    (gqk,) = call(
        query_grad_kernel,
        first + [d_queries, d_keys, packed, core_swap(packed)],
        [away(bf16(4, WIDTH + 64, 256))],
        limit=32,
    )
    gqk = trade(gqk, "y")

    halves = [bf16(64, FF_HALF)] * 4
    downs = ring_trade(call(feed_cut_kernel, stay(downs), halves, [where]), X)

    (cut,) = call(main_cut_kernel, [gqk] + stay(*gvo), [bf16(4, 576, 256)])
    ups = call(feed_cut_kernel, stay(after(ups, cut)), halves, [where])
    cut = after(trade(cut, "z"), (ups, downs))
    ups = ring_trade(ups, X)
    sent = call(
        main_turn_kernel, [cut], [bf16(128, 256)] * 4 + [bf16(64, WIDTH)], [where]
    )
    grad_query, grad_key, *norms = call(
        main_end_kernel,
        [turn_x(sent[k], k, True) for k in range(4)],
        [f32(64, 128)] * 2 + [f32(1, WIDTH)] * 4,
        [where],
    )
    sent = call(feed_turn_kernel, ups + downs + [sent[4]], [bf16(64, 1280)] * 4, [where])
    grad_up, grad_down, grad_value, grad_out = call(
        feed_end_kernel,
        [turn_y(sent[k], k) for k in range(4)],
        [f32(64, 512)] * 2 + [f32(64, 128)] * 2,
    )
    norms = [v.reshape(WIDTH) for v in norms]
    result = hidden + (r_own + core_swap(after(r_send, gqk)).astype(F32))
    return (
        result,
        grad_inputs,
        norms[0],
        norms[1],
        norms[2],
        norms[3],
        grad_query,
        grad_key,
        grad_value,
        grad_out.T,
        grad_up,
        grad_down.T,
    )


def solution(mesh):
    axes = ("z", "xh", "core", "xl", "y")
    split = Mesh(mesh.devices.reshape(4, 2, 2, 2, 4), axes)
    dp, tensor = ("z", "xh", "core"), ("xl", "y")
    tokens, rows, cols = P(axes, None), P(dp, tensor), P(tensor, dp)
    in_specs = (tokens, P(dp, None), P(), P(), P(), P(), rows, rows, rows, cols, rows, cols, tokens)
    out_specs = (tokens, tokens, P(), P(), P(), P(), rows, rows, rows, cols, rows, cols)
    return jax.shard_map(
        local, mesh=split, in_specs=in_specs, out_specs=out_specs, check_vma=False
    )
```

```python
import jax
import jax.numpy as jnp
from jax import lax
from jax.experimental import pallas as pl
from jax.experimental.pallas import tpu as pltpu
from jax.sharding import Mesh, PartitionSpec as P

BF = jnp.bfloat16
F32 = jnp.float32
EPS = 1e-05
BLOCK = 256
WIDTH = 1024
HALF = 512
FF_HALF = 2048
PAIRS = 4
STATE_ROWS = 80
X = ("xh", "xl")
REACH = 4


def dot(left, right, left_dim=1, right_dim=0):
    return lax.dot_general(
        left, right, (((left_dim,), (right_dim,)), ((), ())), preferred_element_type=F32
    )


def ring_shift(value, axis, step):
    return lax.ppermute(value, axis, [(i, (i + step) % 4) for i in range(4)])


def ring_trade(blocks, axis):
    got = {k: ring_shift(blocks[k], axis, k) for k in (1, 3, 2)}
    return [blocks[0], got[1], got[2], got[3]]


def core_swap(value):
    return lax.ppermute(value, "core", [(0, 1), (1, 0)])


def tensor_shift(value, step):
    return lax.ppermute(
        value, ("xl", "y"), [(i, i + step) for i in range(8) if 0 <= i + step < 8]
    )


def turn_y(value, step):
    pairs = []
    for c in range(2):
        for xl in range(2):
            for y in range(4):
                pairs.append(((c * 2 + xl) * 4 + y, (xl * 2 + c) * 4 + (y + step) % 4))
    return lax.ppermute(value, ("core", "xl", "y"), pairs)


def turn_x(value, step, back=False):
    high, low = step // 2, step % 2
    pairs = []
    for xh in range(2):
        for c in range(2):
            for xl in range(2):
                core, x_low = (xl ^ low, c) if back else (xl, c ^ low)
                pairs.append(((xh * 2 + c) * 2 + xl, ((xh ^ high) * 2 + core) * 2 + x_low))
    return lax.ppermute(value, ("xh", "core", "xl"), pairs)


def after(values, earlier):
    return lax.optimization_barrier((values, earlier))[0]


def place(pieces, positions):
    out = jnp.zeros((4,) + pieces[0].shape, pieces[0].dtype)
    for piece, position in zip(pieces, positions):
        out = lax.dynamic_update_index_in_dim(out, piece, position, 0)
    return out


def trade(blocks, axis):
    return lax.all_to_all(blocks, axis, split_axis=0, concat_axis=0, tiled=True)


def spread(value, axis):
    return trade(jnp.broadcast_to(value, (4,) + value.shape), axis)


def stay(*values):
    return [pltpu.with_memory_space_constraint(v, pltpu.HBM) for v in values]


def away(shape):
    return pltpu.HBM(shape.shape, shape.dtype)


COST = pl.CostEstimate(flops=1000, bytes_accessed=1000, transcendentals=0)


def call(kernel, operands, outs, scalars=(), limit=24, scratch=()):
    def whole(value):
        return pl.BlockSpec(value.shape, lambda i: (0,) * len(value.shape))

    return pl.pallas_call(
        kernel,
        grid=(1,),
        in_specs=[pl.BlockSpec(memory_space=pltpu.SMEM)] * len(scalars)
        + [whole(o) for o in operands],
        out_specs=[whole(o) for o in outs],
        out_shape=list(outs),
        scratch_shapes=list(scratch),
        cost_estimate=COST,
        compiler_params=pltpu.CompilerParams(vmem_limit_bytes=limit * 1024 * 1024),
    )(*scalars, *operands)


def f32(*shape):
    return jax.ShapeDtypeStruct(shape, F32)


def bf16(*shape):
    return jax.ShapeDtypeStruct(shape, BF)


def lanes(shape):
    return lax.broadcasted_iota(jnp.int32, shape, 1)


def head_sums(values):
    left = lanes(values.shape) < 64
    first = jnp.sum(jnp.where(left, values, 0.0), axis=1, keepdims=True)
    second = jnp.sum(jnp.where(left, 0.0, values), axis=1, keepdims=True)
    return jnp.where(left, first, second)


def segments_of(info, group, places):
    return sum((places >= info[group, k]).astype(jnp.int32) for k in range(4))


def column_segments(info, group):
    base = info[group, 4]
    return segments_of(info, group, base + lax.broadcasted_iota(jnp.int32, (BLOCK, 1), 0))


def pair_mask(info, group):
    base = info[group, 4]
    rows = lax.broadcasted_iota(jnp.int32, (BLOCK, 1), 0)
    cols = lax.broadcasted_iota(jnp.int32, (1, BLOCK), 1)
    row_seg = segments_of(info, group, base + rows)
    col_seg = segments_of(info, group, base + cols)
    return (rows >= cols) & (row_seg == col_seg)


def carried_of(info, group):
    return column_segments(info, group) == info[group, 5]


def in_last_of(info, group):
    return column_segments(info, group) == info[group, 6]


def masked_mean(values, keep):
    count = jnp.maximum(jnp.sum(keep.astype(F32), axis=0, keepdims=True), 1.0)
    mean = jnp.sum(jnp.where(keep, values, 0.0), axis=0, keepdims=True) / count
    return mean.astype(BF).astype(F32)


def pack_state(matrix, row, center, out, group, pair):
    left = lanes((64, 128)) < 64
    out[group, pair, :64, :] = jnp.where(left, matrix[:64], matrix[64:]).astype(BF)
    high = row.astype(BF).astype(F32)
    place = lax.broadcasted_iota(jnp.int32, (STATE_ROWS - 64, 128), 0)
    rest = jnp.where(place == 0, high, jnp.where(place == 1, row - high, 0.0))
    out[group, pair, 64:, :] = jnp.where(place == 2, center, rest).astype(BF)


def unpack_states(info, group, states, pair, flags):
    left = lanes((64, 128)) < 64
    parts, rows, centers = [], [], []
    for k, state in enumerate(states, 1):
        keep = info[group, flags + k - 1].astype(F32)
        packed = state[0, pair].astype(F32) * keep
        memory = packed[:64]
        parts.append(
            jnp.concatenate([jnp.where(left, memory, 0.0), jnp.where(left, 0.0, memory)], axis=0)
        )
        rows.append(packed[64:65] + packed[65:66])
        centers.append(packed[66:67])
    return parts, rows, centers


def pair_columns(ref, pair):
    return ref[:, pair * 128 : pair * 128 + 128]


def enter_kernel(info, own, other, wqkv, queries, keys, values, out):
    tokens = jnp.concatenate([own[...], other[...]], axis=0)
    both = jnp.concatenate([wqkv[0, :, 256:], wqkv[1, :, 256:]], axis=1)
    values[...] = dot(tokens, both).astype(BF)
    for pair in range(2):
        feat = dot(tokens, wqkv[pair, :, :256])
        feat = jnp.where(feat > 0.0, feat + 1.0, jnp.exp(jnp.minimum(feat, 0.0))).astype(BF)
        queries[:, pair * 128 : pair * 128 + 128] = feat[:, :128]
        keys[:, pair * 128 : pair * 128 + 128] = feat[:, 128:]
    for group in range(2):
        last = in_last_of(info, group)
        rows = slice(group * BLOCK, group * BLOCK + BLOCK)
        for pair in range(2):
            span = slice(pair * 128, pair * 128 + 128)
            v = values[rows, span].astype(F32)
            kept = jnp.where(last, keys[rows, span].astype(F32), 0.0)
            center = masked_mean(v, last)
            matrix = dot(kept.astype(BF), (v - center).astype(BF), 0, 0)
            row = jnp.sum(kept, axis=0, keepdims=True)
            pack_state(matrix, row, center, out, group, pair)


def enter(info, tokens, wqkv):
    whole = pl.BlockSpec((BLOCK, WIDTH), lambda j: (0, 0))
    columns = pl.BlockSpec((TOKENS2, 256), lambda j: (0, j))
    return pl.pallas_call(
        enter_kernel,
        grid=(2,),
        in_specs=[
            pl.BlockSpec(memory_space=pltpu.SMEM),
            whole,
            whole,
            pl.BlockSpec((2, WIDTH, 384), lambda j: (j, 0, 0)),
        ],
        out_specs=[columns] * 3
        + [pl.BlockSpec((2, 2, STATE_ROWS, 128), lambda j: (0, j, 0, 0))],
        out_shape=[away(WIDE16)] * 3 + [STATE],
        cost_estimate=COST,
        compiler_params=pltpu.CompilerParams(vmem_limit_bytes=24 * 1024 * 1024),
    )(info, *tokens, *stay(wqkv))


def relay_kernel(where, own, far, *outs):
    for k, out in enumerate(outs, 1):
        out[...] = jnp.where(where[2] + k < 4, own[...].astype(F32), far[...].astype(F32)).astype(BF)


def inner_kernel(info, queries, keys, values, numer, denom):
    group = pl.program_id(0)
    allowed = pair_mask(info, group)
    left = lanes((BLOCK, 128)) < 64
    for pair in range(PAIRS):
        q, k = pair_columns(queries, pair), pair_columns(keys, pair)
        v = pair_columns(values, pair)
        zero = jnp.zeros_like(q)
        parts = []
        for side in (left, jnp.logical_not(left)):
            scores = jnp.where(allowed, dot(jnp.where(side, q, zero), k, 1, 1), 0.0)
            parts.append((dot(scores.astype(BF), v), jnp.sum(scores, axis=1, keepdims=True)))
        span = slice(pair * 128, pair * 128 + 128)
        numer[:, span] = jnp.where(left, parts[0][0], parts[1][0])
        denom[:, span] = jnp.where(left, parts[0][1], parts[1][1])


def store_halves(group, partial, own, send):
    @pl.when(group == 0)
    def _():
        own[...] = partial

    @pl.when(group == 1)
    def _():
        send[...] = partial.astype(BF)


def join_kernel(
    info, queries, numer, denom, s1, s2, s3, s4, out_rows, wide, low, inverse, own, send
):
    group = pl.program_id(0)
    carried = carried_of(info, group)
    outs = []
    for pair in range(PAIRS):
        q = pair_columns(queries, pair)
        parts, rows, centers = unpack_states(info, group, (s1, s2, s3, s4), pair, 8)
        num, den = dot(q, sum(parts).astype(BF)), 0.0
        for row, center in zip(rows, centers):
            weight = head_sums(q.astype(F32) * row)
            num, den = num + weight * center, den + weight
        inv = 1.0 / (pair_columns(denom, pair) + jnp.where(carried, den, 0.0))
        out = (pair_columns(numer, pair) + jnp.where(carried, num, 0.0)) * inv
        span = slice(pair * 128, pair * 128 + 128)
        wide[:, span] = out
        inverse[:, span] = inv
        outs.append(out.astype(BF))
        low[:, span] = outs[-1]
    partial = dot(jnp.concatenate(outs, axis=1), out_rows[...], 1, 1)
    store_halves(group, partial, own, send)


def back_state_kernel(
    info, queries, values, attended, inverse, b_own, b_other, out_rows, out, scaled, shift
):
    group = pl.program_id(0)
    carried = carried_of(info, group)
    branch = jnp.where(group == 0, b_own[...], b_other[...])
    grad = dot(branch, out_rows[...]).astype(BF).astype(F32)
    for pair in range(PAIRS):
        span = slice(pair * 128, pair * 128 + 128)
        g = (grad[:, span] * pair_columns(inverse, pair)).astype(BF)
        wide = g.astype(F32)
        e = -head_sums(wide * pair_columns(attended, pair))
        scaled[:, span] = g
        shift[:, span] = e
        center = masked_mean(pair_columns(values, pair).astype(F32), carried)
        kept = jnp.where(carried, pair_columns(queries, pair).astype(F32), 0.0)
        row = jnp.sum(kept * (e + head_sums(wide * center)), axis=0, keepdims=True)
        pack_state(dot(kept.astype(BF), g, 0, 0), row, center, out, 0, pair)


def back_inner_kernel(
    info, queries, keys, values, scaled, shift, s1, s2, s3, s4, d_query, d_key, d_value
):
    group = pl.program_id(0)
    allowed = pair_mask(info, group)
    carried = carried_of(info, group)
    left = lanes((BLOCK, 128)) < 64
    for pair in range(PAIRS):
        q, k = pair_columns(queries, pair), pair_columns(keys, pair)
        v, g, e = [pair_columns(r, pair) for r in (values, scaled, shift)]
        zero = jnp.zeros_like(q)
        parts = []
        for head, side in enumerate((left, jnp.logical_not(left))):
            scores = jnp.where(allowed, dot(jnp.where(side, q, zero), k, 1, 1), 0.0).astype(BF)
            d_scores = dot(jnp.where(side, g, zero), v, 1, 1) + e[:, 64 * head : 64 * head + 1]
            d_scores = jnp.where(allowed, d_scores, 0.0).astype(BF)
            parts.append((dot(d_scores, k), dot(d_scores, q, 0, 0), dot(scores, g, 0, 0)))
        dq, dk, dv = [jnp.where(left, a, b) for a, b in zip(*parts)]
        memories, rows, centers = unpack_states(info, group, (s1, s2, s3, s4), pair, 8)
        more = dot(g, sum(memories).astype(BF), 1, 1)
        for row, center in zip(rows, centers):
            more = more + row * (e + head_sums(g.astype(F32) * center))
        dq = dq + jnp.where(carried, more, 0.0)
        span = slice(pair * 128, pair * 128 + 128)
        d_query[:, span] = (dq * jnp.minimum(q.astype(F32), 1.0)).astype(BF)
        d_key[:, span] = dk
        d_value[:, span] = dv


def back_join_kernel(
    info, keys, values, d_query, d_key, d_value, s1, s2, s3, s4, wqkv,
    key_out, value_out, own, send,
):
    group = pl.program_id(0)
    last = in_last_of(info, group)
    partial = 0.0
    for pair in range(PAIRS):
        k, v = pair_columns(keys, pair), pair_columns(values, pair)
        memories, rows, centers = unpack_states(info, group, (s1, s2, s3, s4), pair, 12)
        memory = sum(memories).astype(BF)
        center, row = centers[0], rows[0]
        for m, r, c in zip(memories[1:], rows[1:], centers[1:]):
            away = jnp.broadcast_to(center - c, (16, 128)).astype(BF)
            row = row + r + dot(away, m.astype(BF), 1, 1)[:1]
        more = dot((v.astype(F32) - center).astype(BF), memory, 1, 1) + row
        dk = pair_columns(d_key, pair) + jnp.where(last, more, 0.0)
        dv = pair_columns(d_value, pair) + jnp.where(last, dot(k, memory), 0.0)
        span = slice(pair * 128, pair * 128 + 128)
        dk = (dk * jnp.minimum(k.astype(F32), 1.0)).astype(BF)
        dv = dv.astype(BF)
        key_out[:, span] = dk
        value_out[:, span] = dv
        d_pair = jnp.concatenate([pair_columns(d_query, pair), dk, dv], axis=1)
        partial = partial + dot(d_pair, wqkv[pair], 1, 1)
    store_halves(group, partial, own, send)


def attention_call(kernel, info, operands, outs, weights=()):
    def spec(shape):
        if len(shape) == 4:
            return pl.BlockSpec((1,) + shape[1:], lambda g: (g, 0, 0, 0))
        if shape[0] == TOKENS2:
            return pl.BlockSpec((BLOCK, shape[1]), lambda g: (g, 0))
        return pl.BlockSpec(shape, lambda g: (0, 0))

    def fixed(shape, index):
        return pl.BlockSpec(shape, lambda g: index)

    return pl.pallas_call(
        kernel,
        grid=(2,),
        in_specs=[pl.BlockSpec(memory_space=pltpu.SMEM)]
        + [spec(a.shape) for a in operands]
        + [fixed(shape, index) for _, shape, index in weights],
        out_specs=[spec(o.shape) for o in outs],
        out_shape=outs,
        cost_estimate=COST,
        compiler_params=pltpu.CompilerParams(vmem_limit_bytes=32 * 1024 * 1024),
    )(info, *operands, *stay(*[w for w, _, _ in weights]))


TOKENS2 = 2 * BLOCK
STATE = bf16(2, PAIRS, STATE_ROWS, 128)
WIDE32 = f32(TOKENS2, HALF)
WIDE16 = bf16(TOKENS2, HALF)
OWN = f32(BLOCK, WIDTH)
SEND = bf16(BLOCK, WIDTH)


def prepare_kernel(w_query, w_key, w_value, w_out, w_up, w_down, main, feed):
    main[:, :128] = w_query[...].astype(BF)
    main[:, 128:256] = w_key[...].astype(BF)
    main[:, 256:] = w_value[...].astype(BF)
    feed[:, :512] = w_up[...].astype(BF)
    feed[:, 512:1024] = w_down[...].astype(BF)
    feed[:, 1024:] = w_out[...].astype(BF)


def unit_of(values):
    centred = values - jnp.mean(values, axis=-1, keepdims=True)
    scale = lax.rsqrt(jnp.mean(centred * centred, axis=-1, keepdims=True) + EPS)
    return centred * scale, scale


def feed_rows_kernel(where, p0, p1, p2, p3, feed, out):
    for k, p in enumerate((p0, p1, p2, p3)):
        feed[:, k * 512 : k * 512 + 512] = p[:, :512]
        feed[:, FF_HALF + k * 512 : FF_HALF + k * 512 + 512] = p[:, 512:1024]
        y = lax.rem(where[2] - k + 4, 4)
        out[:, pl.ds(pl.multiple_of(y * 128, 128), 128)] = p[:, 1024:]


def first_norm_kernel(inputs, cotangent, gain, bias, first_in, grad_low):
    unit, _ = unit_of(inputs[...])
    first_in[...] = (unit * gain[...] + bias[...]).astype(BF)
    grad_low[...] = cotangent[...].astype(BF)


def second_norm_kernel(inputs, gain, bias, own, got, hidden, second_in):
    total = inputs[...] + (own[...] + got[...].astype(F32))
    hidden[...] = total
    unit, _ = unit_of(total)
    second_in[...] = (unit * gain[...] + bias[...]).astype(BF)


def norm_slope(values, gain, own, got):
    unit, scale = unit_of(values[...])
    d_out = own[...] + got[...].astype(F32)
    gh = d_out * gain[...]
    slope = scale * (
        gh
        - jnp.mean(gh, axis=-1, keepdims=True)
        - unit * jnp.mean(gh * unit, axis=-1, keepdims=True)
    )
    gains = jnp.sum(d_out * unit, axis=0, keepdims=True)
    return slope, gains, jnp.sum(d_out, axis=0, keepdims=True)


def second_back_kernel(hidden, gain, own, got, cotangent, d_hidden, low, sums):
    slope, gains, biases = norm_slope(hidden, gain, own, got)
    total = cotangent[...] + slope
    d_hidden[...] = total
    low[...] = total.astype(BF)
    sums[...] = jnp.zeros_like(sums)
    sums[2:3, :] = gains
    sums[3:4, :] = biases


def split_pair(sums):
    high = sums.astype(BF).astype(F32)
    return jnp.concatenate([high, sums - high], axis=0).astype(BF)


def join_pair(packed):
    wide = packed.astype(F32)
    return wide[:8] + wide[8:]


def first_back_kernel(inputs, gain, d_hidden, own, got, sums, grad_inputs, packed):
    slope, gains, biases = norm_slope(inputs, gain, own, got)
    grad_inputs[...] = d_hidden[...] + slope
    place = lax.broadcasted_iota(jnp.int32, sums.shape, 0)
    total = jnp.where(place == 0, gains, jnp.where(place == 1, biases, sums[...]))
    packed[...] = split_pair(total)


def sum_in_order(pieces, position):
    total = 0.0
    for a in range(4):
        k = position(a)
        total = total + sum(jnp.where(k == i, p, 0.0) for i, p in enumerate(pieces))
    return total


FF_STEP = 512
FF_STEPS = FF_HALF // FF_STEP


def gelu_parts(u):
    density = jnp.exp(-0.5 * u * u) * 0.3989422804014327
    return 0.5 * (1.0 + lax.erf(u * 0.7071067811865476)), density


def feed_kernel(
    s_own, s_other, g_own, g_other, up, down,
    grads, d_own, d_send, r_own, r_send,
    second, grad, second_t, grad_t, d_total, r_total,
):
    step = pl.program_id(0)

    @pl.when(step == 0)
    def _():
        second[:BLOCK] = s_own[...]
        second[BLOCK:] = s_other[...]
        grad[:BLOCK] = g_own[...]
        grad[BLOCK:] = g_other[...]
        second_t[...] = second[...].T
        grad_t[...] = grad[...].T
        d_total[...] = jnp.zeros_like(d_total)
        r_total[...] = jnp.zeros_like(r_total)

    u = dot(second[...], up[...])
    d_act = dot(grad[...], down[...])
    below, density = gelu_parts(u)
    act = (u * below).astype(BF)
    d_up = (d_act * (below + u * density)).astype(BF)
    grads[:, :FF_STEP] = dot(second_t[...], d_up).astype(BF)
    grads[:, FF_STEP:] = dot(grad_t[...], act).astype(BF)
    d_total[...] += dot(d_up, up[...], 1, 1)
    r_total[...] += dot(act, down[...], 1, 1)

    @pl.when(step == FF_STEPS - 1)
    def _():
        d_own[...] = d_total[:BLOCK]
        d_send[...] = d_total[BLOCK:].astype(BF)
        r_own[...] = r_total[:BLOCK]
        r_send[...] = r_total[BLOCK:].astype(BF)


def feed_forward(tokens, weights):
    whole = pl.BlockSpec((BLOCK, WIDTH), lambda j: (0, 0))

    def columns(rows, offset=0):
        return pl.BlockSpec((rows, FF_STEP), lambda j: (0, j + offset))

    (weights,) = stay(weights)
    return pl.pallas_call(
        feed_kernel,
        grid=(FF_STEPS,),
        in_specs=[whole] * 4 + [columns(WIDTH), columns(WIDTH, FF_STEPS)],
        out_specs=[pl.BlockSpec((WIDTH, 2 * FF_STEP), lambda j: (0, j))] + [whole] * 4,
        out_shape=[away(bf16(WIDTH, 2 * FF_HALF))]
        + [away(v) for v in (OWN, SEND, OWN, SEND)],
        scratch_shapes=[pltpu.VMEM((TOKENS2, WIDTH), BF)] * 2
        + [pltpu.VMEM((WIDTH, TOKENS2), BF)] * 2
        + [pltpu.VMEM((TOKENS2, WIDTH), F32)] * 2,
        cost_estimate=COST,
        compiler_params=pltpu.CompilerParams(vmem_limit_bytes=40 * 1024 * 1024),
    )(*tokens, weights, weights)


def rows_of(ref, index, size):
    return ref[pl.ds(pl.multiple_of(index * size, size), size), :]


def value_grad_kernel(
    where, f_own, f_other, b_own, b_other, d_value, low, v0, v1, v2, v3, first_t, branch_t
):
    first_t[...] = jnp.concatenate([f_own[...], f_other[...]], axis=0).T
    branch_t[...] = jnp.concatenate([b_own[...], b_other[...]], axis=0).T
    for k, part in enumerate((v0, v1, v2, v3)):
        x = lax.rem(where[1] + k, 4)
        for half, (left, right) in enumerate(((first_t, d_value), (branch_t, low))):
            rows = jnp.concatenate([rows_of(left, 4 * z + x, 64) for z in range(4)], axis=0)
            part[:, half * HALF : half * HALF + HALF] = dot(rows, right[...]).astype(BF)


def query_grad_kernel(f_own, f_other, d_query, d_key, out):
    first = jnp.concatenate([f_own[...], f_other[...]], axis=0).T
    for pair in range(PAIRS):
        d_all = [pair_columns(d, pair) for d in (d_query, d_key)]
        out[pair] = dot(first, jnp.concatenate(d_all, axis=1)).astype(BF)


def norm_core_kernel(packed, other, norms):
    norms[...] = split_pair(join_pair(packed[...]) + join_pair(other[...]))


def feed_cut_kernel(where, part, u0, u1, u2, u3, d0, d1, d2, d3):
    for k, (up, down) in enumerate(((u0, d0), (u1, d1), (u2, d2), (u3, d3))):
        rows = pl.ds(pl.multiple_of(lax.rem(where[1] + k, 4) * 64, 64), 64)
        for j in range(4):
            up[:, j * 512 : j * 512 + 512] = part[rows, j * WIDTH : j * WIDTH + 512]
        slot = (-k) % 4
        down[...] = part[:, slot * WIDTH + 512 : slot * WIDTH + WIDTH]


def sum_of(pieces, *index):
    return sum(pieces[(j,) + index].astype(F32) for j in range(4))


def feed_turn_kernel(where, u0, u1, u2, u3, values, *outs):
    for k, out in enumerate(outs):
        slot = (-k) % 4
        span = slice(slot * 512, slot * 512 + 512)
        out[:, :512] = sum(p[:, span].astype(F32) for p in (u0, u1, u2, u3)).astype(BF)
        y = lax.rem(where[2] + k, 4)
        for half in range(2):
            span = pl.ds(pl.multiple_of(half * HALF + y * 128, 128), 128)
            out[:, 512 + half * 128 : 640 + half * 128] = values[:, span]


def feed_end_kernel(p0, p1, p2, p3, up, value, out):
    total = sum(p[...].astype(F32) for p in (p0, p1, p2, p3))
    up[...] = total[:, :512]
    value[...] = total[:, 512:640]
    out[...] = total[:, 640:]


def main_cut_kernel(main, norms, v0, v1, v2, v3, out):
    total = split_pair(sum(join_pair(norms[j]) for j in range(4)))
    for z in range(4):
        rows = slice(z * 256, z * 256 + 256)
        out[z, :256, :] = sum_of(main, rows, slice(None)).astype(BF)
        rows = slice(z * 64, z * 64 + 64)
        for j in range(4):
            span = slice(j * 256, j * 256 + 256)
            out[z, 256 + 16 * j : 272 + 16 * j, :] = total[:, span]
            values = sum(p[rows, span].astype(F32) for p in (v0, v1, v2, v3))
            out[z, 320 + 64 * j : 384 + 64 * j, :] = values.astype(BF)


def main_turn_kernel(where, main, d0, d1, d2, d3, o0, o1, o2, o3, values):
    pieces = []
    for j in range(4):
        rows = [main[j, 256 + 16 * i : 272 + 16 * i, :] for i in range(4)]
        pieces.append(join_pair(jnp.concatenate(rows, axis=1)))
    norms = split_pair(sum(pieces))
    for j in range(4):
        rows = slice(320 + 64 * j, 384 + 64 * j)
        values[:, j * 256 : j * 256 + 256] = sum_of(main, rows, slice(None)).astype(BF)
    for k, out in enumerate((o0, o1, o2, o3)):
        rows = pl.ds(pl.multiple_of((where[1] ^ k) * 64, 64), 64)
        out[:64, :256] = sum_of(main, rows, slice(None)).astype(BF)
        out[:64, 256:] = sum(p[rows, :].astype(F32) for p in (d0, d1, d2, d3)).astype(BF)
        for i in range(2):
            out[64 + 16 * i : 80 + 16 * i, :512] = norms[:, i * 512 : i * 512 + 512]
            out[64 + 16 * i : 80 + 16 * i, 512:] = jnp.zeros((16, 256), BF)


def main_end_kernel(where, p0, p1, p2, p3, query, key, down, n0, n1, n2, n3):
    pieces = (p0, p1, p2, p3)
    total = sum(p[:64, :].astype(F32) for p in pieces)
    query[...] = total[:, :128]
    key[...] = total[:, 128:256]
    down[...] = total[:, 256:]
    parts = []
    for p in pieces:
        rows = [p[64 + 16 * i : 80 + 16 * i, :512] for i in range(2)]
        parts.append(join_pair(jnp.concatenate(rows, axis=1)))
    norms = sum_in_order(parts, lambda a: where[3] ^ a)
    for k, ref in enumerate((n0, n1, n2, n3)):
        ref[...] = norms[k : k + 1, :]


def local(
    inputs,
    lengths,
    ln1_gain,
    ln1_bias,
    ln2_gain,
    ln2_bias,
    w_query,
    w_key,
    w_value,
    w_out,
    w_up,
    w_down,
    cotangent,
):
    x = lax.axis_index(X)
    block = lax.axis_index(("xl", "y"))
    z = lax.axis_index("z")
    where = [z, x, lax.axis_index("y"), lax.axis_index(("xh", "core"))]
    where = jnp.stack(where).astype(jnp.int32)
    gain_one, bias_one, gain_two, bias_two = [
        v.reshape(1, WIDTH) for v in (ln1_gain, ln1_bias, ln2_gain, ln2_bias)
    ]

    main, feed = call(
        prepare_kernel,
        stay(w_query, w_key, w_value, w_out.T, w_up, w_down.T),
        [bf16(64, 384), bf16(64, 1152)],
    )
    main = [turn_x(main, k) for k in range(4)]
    feed = after(feed, main)
    main = place(main, [x ^ k for k in range(4)]).reshape(256, 384)
    main = spread(main, "z").reshape(WIDTH, 384)
    feed = [turn_y(feed, k) for k in range(4)]
    feed_rows, wo = call(
        feed_rows_kernel,
        after(feed, main),
        [away(bf16(64, 2 * FF_HALF)), bf16(64, HALF)],
        [where],
    )
    feed_weights = lax.all_gather(feed_rows, ("z", "xh", "xl"), axis=0, tiled=True)
    main = jnp.broadcast_to(main, (4, WIDTH, 384))
    gain_one = after(gain_one, main)
    wqkv = trade(main, "y")
    wo = place(ring_trade([wo] * 4, X), [lax.rem(x - k + 4, 4) for k in range(4)])
    wo = ring_trade([wo.reshape(256, HALF)] * 4, "z")
    wo = place(wo, [lax.rem(z - k + 4, 4) for k in range(4)]).reshape(WIDTH, HALF)
    wqkv = after(wqkv, wo)
    wo = (wo, (WIDTH, HALF), (0, 0))

    ends = jnp.cumsum(jnp.concatenate([lengths, core_swap(lengths)], axis=0), axis=1)

    def last_segment(which):
        return jnp.sum((which * BLOCK + BLOCK - 1 >= ends).astype(jnp.int32), axis=1)

    here = last_segment(block)
    before = jnp.where(block > 0, last_segment(block - 1), -1)
    zeros = jnp.zeros((2,), jnp.int32)
    flags = [(block >= k) & (last_segment(block - k) == before) for k in range(1, REACH + 1)]
    flags += [
        (block + k < 8) & (last_segment(block + k - 1) == here) for k in range(1, REACH + 1)
    ]
    rest = [zeros + block * BLOCK, before, here, zeros] + [f.astype(jnp.int32) for f in flags]
    info = jnp.concatenate([ends, jnp.stack(rest, axis=1)], axis=1)

    first_in, grad_low = call(
        first_norm_kernel, stay(inputs, cotangent, gain_one, bias_one), [SEND, away(SEND)]
    )
    first = [first_in, core_swap(first_in)]
    grads = [grad_low, core_swap(grad_low)]

    queries, keys, values, state = enter(info, first, wqkv)
    queries, keys, values = stay(queries, keys, values)
    far = tensor_shift(state, 4)
    states = call(relay_kernel, [state, far], [STATE] * 3, [where])
    states = [ring_shift(states[k - 1], "y", k) for k in (1, 2, 3)] + [far]
    numer, denom = attention_call(
        inner_kernel, info, [queries, keys, values], [WIDE32, WIDE32]
    )
    attended, low, inverse, own, send = attention_call(
        join_kernel,
        info,
        [queries, numer, denom] + states,
        [away(WIDE32), away(WIDE16), away(WIDE32), OWN, SEND],
        [wo],
    )
    hidden, second_in = call(
        second_norm_kernel,
        stay(inputs, gain_two, bias_two) + [own, core_swap(send)],
        [away(OWN), SEND],
    )
    feed_grad, d_own, d_send, r_own, r_send = feed_forward(
        [second_in, core_swap(second_in)] + stay(*grads), feed_weights
    )
    d_hidden, branch_low, sums = call(
        second_back_kernel,
        stay(hidden, gain_two, d_own) + [core_swap(d_send)] + stay(cotangent),
        [away(OWN), SEND, f32(8, WIDTH)],
    )
    branch = [branch_low, core_swap(branch_low)]

    feed_grad = lax.psum_scatter(feed_grad, "z", scatter_dimension=0, tiled=True)

    back_state, scaled, shift = attention_call(
        back_state_kernel,
        info,
        [queries, values] + stay(attended, inverse) + branch,
        [STATE, WIDE16, WIDE32],
        [wo],
    )
    back_states = [tensor_shift(back_state, -k) for k in range(1, REACH + 1)]
    d_queries, d_key, d_value = attention_call(
        back_inner_kernel,
        info,
        [queries, keys, values, scaled, shift] + stay(*states),
        [away(WIDE16), WIDE32, WIDE32],
    )
    d_keys, d_values, own, send = attention_call(
        back_join_kernel,
        info,
        [keys, values, d_queries, d_key, d_value] + back_states,
        [away(WIDE16), away(WIDE16), away(OWN), SEND],
        [(wqkv, (4, WIDTH, 384), (0, 0, 0))],
    )
    (gqk,) = call(
        query_grad_kernel,
        stay(*first, d_queries, d_keys),
        [away(bf16(4, WIDTH, 256))],
        limit=32,
    )
    d_values = after(d_values, gqk)
    gqk = trade(gqk, "y")
    gvo = call(
        value_grad_kernel,
        stay(*first, *branch, d_values, low),
        [away(bf16(256, WIDTH))] * 4,
        [where],
        limit=32,
        scratch=[pltpu.VMEM((WIDTH, TOKENS2), BF)] * 2,
    )
    sums = after(sums, gvo)
    gvo = ring_trade(gvo, X)
    grad_inputs, packed = call(
        first_back_kernel,
        stay(inputs, gain_one, d_hidden, own) + [core_swap(send), sums],
        [away(OWN), bf16(16, WIDTH)],
    )
    (norms,) = call(norm_core_kernel, [packed, core_swap(packed)], [bf16(16, WIDTH)])
    norms = spread(after(norms, gqk), "y")

    (cut,) = call(main_cut_kernel, [gqk, norms] + stay(*gvo), [bf16(4, 576, 256)])
    feed_grad = call(
        feed_cut_kernel,
        stay(after(feed_grad, cut)),
        [bf16(64, FF_HALF)] * 4 + [bf16(BLOCK, HALF)] * 4,
        [where],
    )
    cut = after(trade(cut, "z"), feed_grad)
    downs, ups = ring_trade(feed_grad[4:], "y"), ring_trade(feed_grad[:4], X)

    sent = call(
        main_turn_kernel, [cut] + downs, [bf16(96, 768)] * 4 + [bf16(64, WIDTH)], [where]
    )
    turned = [turn_x(sent[k], k, True) for k in range(4)]
    ups = after(ups, turned[:2])
    grad_query, grad_key, grad_down, *norms = call(
        main_end_kernel,
        turned,
        [f32(64, 128)] * 2 + [f32(64, 512)] + [f32(1, WIDTH)] * 4,
        [where],
    )
    sent = call(feed_turn_kernel, ups + [sent[4]], [bf16(64, 768)] * 4, [where])
    grad_up, grad_value, grad_out = call(
        feed_end_kernel,
        [turn_y(sent[k], k) for k in range(4)],
        [f32(64, 512)] + [f32(64, 128)] * 2,
    )
    norms = [v.reshape(WIDTH) for v in norms]
    result = hidden + (r_own + core_swap(after(r_send, gqk)).astype(F32))
    return (
        result,
        grad_inputs,
        norms[0],
        norms[1],
        norms[2],
        norms[3],
        grad_query,
        grad_key,
        grad_value,
        grad_out.T,
        grad_up,
        grad_down.T,
    )


def solution(mesh):
    axes = ("z", "xh", "core", "xl", "y")
    split = Mesh(mesh.devices.reshape(4, 2, 2, 2, 4), axes)
    dp, tensor = ("z", "xh", "core"), ("xl", "y")
    tokens, rows, cols = P(axes, None), P(dp, tensor), P(tensor, dp)
    in_specs = (tokens, P(dp, None), P(), P(), P(), P(), rows, rows, rows, cols, rows, cols, tokens)
    out_specs = (tokens, tokens, P(), P(), P(), P(), rows, rows, rows, cols, rows, cols)
    return jax.shard_map(
        local, mesh=split, in_specs=in_specs, out_specs=out_specs, check_vma=False
    )
```

```python
import jax
import jax.numpy as jnp
from jax import lax
from jax.experimental import pallas as pl
from jax.experimental.pallas import tpu as pltpu
from jax.sharding import Mesh, PartitionSpec as P

BF = jnp.bfloat16
F32 = jnp.float32
EPS = 1e-05
BLOCK = 256
WIDTH = 1024
HALF = 512
FF_HALF = 2048
PAIRS = 4
STATE_ROWS = 80
X = ("xh", "xl")
REACH = 4


def dot(left, right, left_dim=1, right_dim=0):
    return lax.dot_general(
        left, right, (((left_dim,), (right_dim,)), ((), ())), preferred_element_type=F32
    )


def ring_shift(value, axis, step):
    return lax.ppermute(value, axis, [(i, (i + step) % 4) for i in range(4)])


def ring_trade(blocks, axis):
    got = {k: ring_shift(blocks[k], axis, k) for k in (1, 3, 2)}
    return [blocks[0], got[1], got[2], got[3]]


def core_swap(value):
    return lax.ppermute(value, "core", [(0, 1), (1, 0)])


def tensor_shift(value, step):
    return lax.ppermute(
        value, ("xl", "y"), [(i, i + step) for i in range(8) if 0 <= i + step < 8]
    )


def turn_y(value, step):
    pairs = []
    for c in range(2):
        for xl in range(2):
            for y in range(4):
                pairs.append(((c * 2 + xl) * 4 + y, (xl * 2 + c) * 4 + (y + step) % 4))
    return lax.ppermute(value, ("core", "xl", "y"), pairs)


def turn_x(value, step, back=False):
    high, low = step // 2, step % 2
    pairs = []
    for xh in range(2):
        for c in range(2):
            for xl in range(2):
                core, x_low = (xl ^ low, c) if back else (xl, c ^ low)
                pairs.append(((xh * 2 + c) * 2 + xl, ((xh ^ high) * 2 + core) * 2 + x_low))
    return lax.ppermute(value, ("xh", "core", "xl"), pairs)


def after(values, earlier):
    return lax.optimization_barrier((values, earlier))[0]


def place(pieces, positions):
    out = jnp.zeros((4,) + pieces[0].shape, pieces[0].dtype)
    for piece, position in zip(pieces, positions):
        out = lax.dynamic_update_index_in_dim(out, piece, position, 0)
    return out


def trade(blocks, axis):
    return lax.all_to_all(blocks, axis, split_axis=0, concat_axis=0, tiled=True)


def spread(value, axis):
    return trade(jnp.broadcast_to(value, (4,) + value.shape), axis)


def stay(*values):
    return [pltpu.with_memory_space_constraint(v, pltpu.HBM) for v in values]


def away(shape):
    return pltpu.HBM(shape.shape, shape.dtype)


COST = pl.CostEstimate(flops=1000, bytes_accessed=1000, transcendentals=0)


def call(kernel, operands, outs, scalars=(), limit=24, scratch=()):
    def whole(value):
        return pl.BlockSpec(value.shape, lambda i: (0,) * len(value.shape))

    return pl.pallas_call(
        kernel,
        grid=(1,),
        in_specs=[pl.BlockSpec(memory_space=pltpu.SMEM)] * len(scalars)
        + [whole(o) for o in operands],
        out_specs=[whole(o) for o in outs],
        out_shape=list(outs),
        scratch_shapes=list(scratch),
        cost_estimate=COST,
        compiler_params=pltpu.CompilerParams(vmem_limit_bytes=limit * 1024 * 1024),
    )(*scalars, *operands)


def f32(*shape):
    return jax.ShapeDtypeStruct(shape, F32)


def bf16(*shape):
    return jax.ShapeDtypeStruct(shape, BF)


def lanes(shape):
    return lax.broadcasted_iota(jnp.int32, shape, 1)


def head_sums(values):
    left = lanes(values.shape) < 64
    first = jnp.sum(jnp.where(left, values, 0.0), axis=1, keepdims=True)
    second = jnp.sum(jnp.where(left, 0.0, values), axis=1, keepdims=True)
    return jnp.where(left, first, second)


def segments_of(info, group, places):
    return sum((places >= info[group, k]).astype(jnp.int32) for k in range(4))


def column_segments(info, group):
    base = info[group, 4]
    return segments_of(info, group, base + lax.broadcasted_iota(jnp.int32, (BLOCK, 1), 0))


def pair_mask(info, group):
    base = info[group, 4]
    rows = lax.broadcasted_iota(jnp.int32, (BLOCK, 1), 0)
    cols = lax.broadcasted_iota(jnp.int32, (1, BLOCK), 1)
    row_seg = segments_of(info, group, base + rows)
    col_seg = segments_of(info, group, base + cols)
    return (rows >= cols) & (row_seg == col_seg)


def carried_of(info, group):
    return column_segments(info, group) == info[group, 5]


def in_last_of(info, group):
    return column_segments(info, group) == info[group, 6]


def masked_mean(values, keep):
    count = jnp.maximum(jnp.sum(keep.astype(F32), axis=0, keepdims=True), 1.0)
    mean = jnp.sum(jnp.where(keep, values, 0.0), axis=0, keepdims=True) / count
    return mean.astype(BF).astype(F32)


def pack_state(matrix, row, center, out, group, pair):
    left = lanes((64, 128)) < 64
    out[group, pair, :64, :] = jnp.where(left, matrix[:64], matrix[64:]).astype(BF)
    high = row.astype(BF).astype(F32)
    place = lax.broadcasted_iota(jnp.int32, (STATE_ROWS - 64, 128), 0)
    rest = jnp.where(place == 0, high, jnp.where(place == 1, row - high, 0.0))
    out[group, pair, 64:, :] = jnp.where(place == 2, center, rest).astype(BF)


def unpack_states(info, group, states, pair, flags):
    left = lanes((64, 128)) < 64
    parts, rows, centers = [], [], []
    for k, state in enumerate(states, 1):
        keep = info[group, flags + k - 1].astype(F32)
        packed = state[0, pair].astype(F32) * keep
        memory = packed[:64]
        parts.append(
            jnp.concatenate([jnp.where(left, memory, 0.0), jnp.where(left, 0.0, memory)], axis=0)
        )
        rows.append(packed[64:65] + packed[65:66])
        centers.append(packed[66:67])
    return parts, rows, centers


def pair_columns(ref, pair):
    return ref[:, pair * 128 : pair * 128 + 128]


def enter_kernel(info, own, other, wqkv, queries, keys, values, out):
    tokens = jnp.concatenate([own[...], other[...]], axis=0)
    both = jnp.concatenate([wqkv[0, :, 256:], wqkv[1, :, 256:]], axis=1)
    values[...] = dot(tokens, both).astype(BF)
    for pair in range(2):
        feat = dot(tokens, wqkv[pair, :, :256])
        feat = jnp.where(feat > 0.0, feat + 1.0, jnp.exp(jnp.minimum(feat, 0.0))).astype(BF)
        queries[:, pair * 128 : pair * 128 + 128] = feat[:, :128]
        keys[:, pair * 128 : pair * 128 + 128] = feat[:, 128:]
    for group in range(2):
        last = in_last_of(info, group)
        rows = slice(group * BLOCK, group * BLOCK + BLOCK)
        for pair in range(2):
            span = slice(pair * 128, pair * 128 + 128)
            v = values[rows, span].astype(F32)
            kept = jnp.where(last, keys[rows, span].astype(F32), 0.0)
            center = masked_mean(v, last)
            matrix = dot(kept.astype(BF), (v - center).astype(BF), 0, 0)
            row = jnp.sum(kept, axis=0, keepdims=True)
            pack_state(matrix, row, center, out, group, pair)


def enter(info, tokens, wqkv):
    whole = pl.BlockSpec((BLOCK, WIDTH), lambda j: (0, 0))
    columns = pl.BlockSpec((TOKENS2, 256), lambda j: (0, j))
    return pl.pallas_call(
        enter_kernel,
        grid=(2,),
        in_specs=[
            pl.BlockSpec(memory_space=pltpu.SMEM),
            whole,
            whole,
            pl.BlockSpec((2, WIDTH, 384), lambda j: (j, 0, 0)),
        ],
        out_specs=[columns] * 3
        + [pl.BlockSpec((2, 2, STATE_ROWS, 128), lambda j: (0, j, 0, 0))],
        out_shape=[away(WIDE16)] * 3 + [STATE],
        cost_estimate=COST,
        compiler_params=pltpu.CompilerParams(vmem_limit_bytes=24 * 1024 * 1024),
    )(info, *tokens, *stay(wqkv))


def relay_kernel(where, own, far, *outs):
    for k, out in enumerate(outs, 1):
        out[...] = jnp.where(where[2] + k < 4, own[...].astype(F32), far[...].astype(F32)).astype(BF)


def inner_kernel(info, queries, keys, values, numer, denom):
    group = pl.program_id(0)
    allowed = pair_mask(info, group)
    left = lanes((BLOCK, 128)) < 64
    for pair in range(PAIRS):
        q, k = pair_columns(queries, pair), pair_columns(keys, pair)
        v = pair_columns(values, pair)
        zero = jnp.zeros_like(q)
        parts = []
        for side in (left, jnp.logical_not(left)):
            scores = jnp.where(allowed, dot(jnp.where(side, q, zero), k, 1, 1), 0.0)
            parts.append((dot(scores.astype(BF), v), jnp.sum(scores, axis=1, keepdims=True)))
        span = slice(pair * 128, pair * 128 + 128)
        numer[:, span] = jnp.where(left, parts[0][0], parts[1][0])
        denom[:, span] = jnp.where(left, parts[0][1], parts[1][1])


def store_halves(group, partial, own, send):
    @pl.when(group == 0)
    def _():
        own[...] = partial

    @pl.when(group == 1)
    def _():
        send[...] = partial.astype(BF)


def join_kernel(
    info, queries, numer, denom, s1, s2, s3, s4, out_rows, wide, low, inverse, own, send
):
    group = pl.program_id(0)
    carried = carried_of(info, group)
    outs = []
    for pair in range(PAIRS):
        q = pair_columns(queries, pair)
        parts, rows, centers = unpack_states(info, group, (s1, s2, s3, s4), pair, 8)
        num, den = dot(q, sum(parts).astype(BF)), 0.0
        for row, center in zip(rows, centers):
            weight = head_sums(q.astype(F32) * row)
            num, den = num + weight * center, den + weight
        inv = 1.0 / (pair_columns(denom, pair) + jnp.where(carried, den, 0.0))
        out = (pair_columns(numer, pair) + jnp.where(carried, num, 0.0)) * inv
        span = slice(pair * 128, pair * 128 + 128)
        wide[:, span] = out
        inverse[:, span] = inv
        outs.append(out.astype(BF))
        low[:, span] = outs[-1]
    partial = dot(jnp.concatenate(outs, axis=1), out_rows[...], 1, 1)
    store_halves(group, partial, own, send)


def back_state_kernel(
    info, queries, values, attended, inverse, b_own, b_other, out_rows, out, scaled, shift
):
    group = pl.program_id(0)
    carried = carried_of(info, group)
    branch = jnp.where(group == 0, b_own[...], b_other[...])
    grad = dot(branch, out_rows[...]).astype(BF).astype(F32)
    for pair in range(PAIRS):
        span = slice(pair * 128, pair * 128 + 128)
        g = (grad[:, span] * pair_columns(inverse, pair)).astype(BF)
        wide = g.astype(F32)
        e = -head_sums(wide * pair_columns(attended, pair))
        scaled[:, span] = g
        shift[:, span] = e
        center = masked_mean(pair_columns(values, pair).astype(F32), carried)
        kept = jnp.where(carried, pair_columns(queries, pair).astype(F32), 0.0)
        row = jnp.sum(kept * (e + head_sums(wide * center)), axis=0, keepdims=True)
        pack_state(dot(kept.astype(BF), g, 0, 0), row, center, out, 0, pair)


def back_inner_kernel(
    info, queries, keys, values, scaled, shift, s1, s2, s3, s4, d_query, d_key, d_value
):
    group = pl.program_id(0)
    allowed = pair_mask(info, group)
    carried = carried_of(info, group)
    left = lanes((BLOCK, 128)) < 64
    for pair in range(PAIRS):
        q, k = pair_columns(queries, pair), pair_columns(keys, pair)
        v, g, e = [pair_columns(r, pair) for r in (values, scaled, shift)]
        zero = jnp.zeros_like(q)
        parts = []
        for head, side in enumerate((left, jnp.logical_not(left))):
            scores = jnp.where(allowed, dot(jnp.where(side, q, zero), k, 1, 1), 0.0).astype(BF)
            d_scores = dot(jnp.where(side, g, zero), v, 1, 1) + e[:, 64 * head : 64 * head + 1]
            d_scores = jnp.where(allowed, d_scores, 0.0).astype(BF)
            parts.append((dot(d_scores, k), dot(d_scores, q, 0, 0), dot(scores, g, 0, 0)))
        dq, dk, dv = [jnp.where(left, a, b) for a, b in zip(*parts)]
        memories, rows, centers = unpack_states(info, group, (s1, s2, s3, s4), pair, 8)
        more = dot(g, sum(memories).astype(BF), 1, 1)
        for row, center in zip(rows, centers):
            more = more + row * (e + head_sums(g.astype(F32) * center))
        dq = dq + jnp.where(carried, more, 0.0)
        span = slice(pair * 128, pair * 128 + 128)
        d_query[:, span] = (dq * jnp.minimum(q.astype(F32), 1.0)).astype(BF)
        d_key[:, span] = dk
        d_value[:, span] = dv


def back_join_kernel(
    info, keys, values, d_query, d_key, d_value, s1, s2, s3, s4, wqkv,
    key_out, value_out, own, send,
):
    group = pl.program_id(0)
    last = in_last_of(info, group)
    partial = 0.0
    for pair in range(PAIRS):
        k, v = pair_columns(keys, pair), pair_columns(values, pair)
        memories, rows, centers = unpack_states(info, group, (s1, s2, s3, s4), pair, 12)
        memory = sum(memories).astype(BF)
        center, row = centers[0], rows[0]
        for m, r, c in zip(memories[1:], rows[1:], centers[1:]):
            away = jnp.broadcast_to(center - c, (16, 128)).astype(BF)
            row = row + r + dot(away, m.astype(BF), 1, 1)[:1]
        more = dot((v.astype(F32) - center).astype(BF), memory, 1, 1) + row
        dk = pair_columns(d_key, pair) + jnp.where(last, more, 0.0)
        dv = pair_columns(d_value, pair) + jnp.where(last, dot(k, memory), 0.0)
        span = slice(pair * 128, pair * 128 + 128)
        dk = (dk * jnp.minimum(k.astype(F32), 1.0)).astype(BF)
        dv = dv.astype(BF)
        key_out[:, span] = dk
        value_out[:, span] = dv
        d_pair = jnp.concatenate([pair_columns(d_query, pair), dk, dv], axis=1)
        partial = partial + dot(d_pair, wqkv[pair], 1, 1)
    store_halves(group, partial, own, send)


def attention_call(kernel, info, operands, outs, weights=()):
    def spec(shape):
        if len(shape) == 4:
            return pl.BlockSpec((1,) + shape[1:], lambda g: (g, 0, 0, 0))
        if shape[0] == TOKENS2:
            return pl.BlockSpec((BLOCK, shape[1]), lambda g: (g, 0))
        return pl.BlockSpec(shape, lambda g: (0, 0))

    def fixed(shape, index):
        return pl.BlockSpec(shape, lambda g: index)

    return pl.pallas_call(
        kernel,
        grid=(2,),
        in_specs=[pl.BlockSpec(memory_space=pltpu.SMEM)]
        + [spec(a.shape) for a in operands]
        + [fixed(shape, index) for _, shape, index in weights],
        out_specs=[spec(o.shape) for o in outs],
        out_shape=outs,
        cost_estimate=COST,
        compiler_params=pltpu.CompilerParams(vmem_limit_bytes=32 * 1024 * 1024),
    )(info, *operands, *stay(*[w for w, _, _ in weights]))


TOKENS2 = 2 * BLOCK
STATE = bf16(2, PAIRS, STATE_ROWS, 128)
WIDE32 = f32(TOKENS2, HALF)
WIDE16 = bf16(TOKENS2, HALF)
OWN = f32(BLOCK, WIDTH)
SEND = bf16(BLOCK, WIDTH)


def prepare_kernel(w_query, w_key, w_value, w_out, w_up, w_down, main, feed):
    main[:, :128] = w_query[...].astype(BF)
    main[:, 128:256] = w_key[...].astype(BF)
    main[:, 256:] = w_value[...].astype(BF)
    feed[:, :512] = w_up[...].astype(BF)
    feed[:, 512:1024] = w_down[...].astype(BF)
    feed[:, 1024:] = w_out[...].astype(BF)


def unit_of(values):
    centred = values - jnp.mean(values, axis=-1, keepdims=True)
    scale = lax.rsqrt(jnp.mean(centred * centred, axis=-1, keepdims=True) + EPS)
    return centred * scale, scale


def feed_rows_kernel(where, p0, p1, p2, p3, feed, out):
    for k, p in enumerate((p0, p1, p2, p3)):
        feed[:, k * 512 : k * 512 + 512] = p[:, :512]
        feed[:, FF_HALF + k * 512 : FF_HALF + k * 512 + 512] = p[:, 512:1024]
        y = lax.rem(where[2] - k + 4, 4)
        out[:, pl.ds(pl.multiple_of(y * 128, 128), 128)] = p[:, 1024:]


def first_norm_kernel(inputs, cotangent, gain, bias, first_in, grad_low):
    unit, _ = unit_of(inputs[...])
    first_in[...] = (unit * gain[...] + bias[...]).astype(BF)
    grad_low[...] = cotangent[...].astype(BF)


def second_norm_kernel(inputs, gain, bias, own, got, hidden, second_in):
    total = inputs[...] + (own[...] + got[...].astype(F32))
    hidden[...] = total
    unit, _ = unit_of(total)
    second_in[...] = (unit * gain[...] + bias[...]).astype(BF)


def norm_slope(values, gain, own, got):
    unit, scale = unit_of(values[...])
    d_out = own[...] + got[...].astype(F32)
    gh = d_out * gain[...]
    slope = scale * (
        gh
        - jnp.mean(gh, axis=-1, keepdims=True)
        - unit * jnp.mean(gh * unit, axis=-1, keepdims=True)
    )
    gains = jnp.sum(d_out * unit, axis=0, keepdims=True)
    return slope, gains, jnp.sum(d_out, axis=0, keepdims=True)


def second_back_kernel(hidden, gain, own, got, cotangent, d_hidden, low, sums):
    slope, gains, biases = norm_slope(hidden, gain, own, got)
    total = cotangent[...] + slope
    d_hidden[...] = total
    low[...] = total.astype(BF)
    sums[...] = jnp.zeros_like(sums)
    sums[2:3, :] = gains
    sums[3:4, :] = biases


def split_pair(sums):
    high = sums.astype(BF).astype(F32)
    return jnp.concatenate([high, sums - high], axis=0).astype(BF)


def join_pair(packed):
    wide = packed.astype(F32)
    return wide[:8] + wide[8:]


def first_back_kernel(inputs, gain, d_hidden, own, got, sums, grad_inputs, packed):
    slope, gains, biases = norm_slope(inputs, gain, own, got)
    grad_inputs[...] = d_hidden[...] + slope
    place = lax.broadcasted_iota(jnp.int32, sums.shape, 0)
    total = jnp.where(place == 0, gains, jnp.where(place == 1, biases, sums[...]))
    packed[...] = split_pair(total)


def sum_in_order(pieces, position):
    total = 0.0
    for a in range(4):
        k = position(a)
        total = total + sum(jnp.where(k == i, p, 0.0) for i, p in enumerate(pieces))
    return total


FF_STEP = 512
FF_STEPS = FF_HALF // FF_STEP


def gelu_parts(u):
    density = jnp.exp(-0.5 * u * u) * 0.3989422804014327
    return 0.5 * (1.0 + lax.erf(u * 0.7071067811865476)), density


def feed_kernel(
    s_own, s_other, g_own, g_other, up, down,
    grads, act_out, d_own, d_send, second, grad, second_t, grad_t, d_total,
):
    step = pl.program_id(0)

    @pl.when(step == 0)
    def _():
        second[:BLOCK] = s_own[...]
        second[BLOCK:] = s_other[...]
        grad[:BLOCK] = g_own[...]
        grad[BLOCK:] = g_other[...]
        second_t[...] = second[...].T
        grad_t[...] = grad[...].T
        d_total[...] = jnp.zeros_like(d_total)

    u = dot(second[...], up[...])
    d_act = dot(grad[...], down[...])
    below, density = gelu_parts(u)
    act = (u * below).astype(BF)
    d_up = (d_act * (below + u * density)).astype(BF)
    grads[:, :FF_STEP] = dot(second_t[...], d_up).astype(BF)
    grads[:, FF_STEP:] = dot(grad_t[...], act).astype(BF)
    d_total[...] += dot(d_up, up[...], 1, 1)
    act_out[...] = act

    @pl.when(step == FF_STEPS - 1)
    def _():
        d_own[...] = d_total[:BLOCK]
        d_send[...] = d_total[BLOCK:].astype(BF)


def feed_forward(tokens, weights):
    whole = pl.BlockSpec((BLOCK, WIDTH), lambda j: (0, 0))

    def columns(rows, offset=0):
        return pl.BlockSpec((rows, FF_STEP), lambda j: (0, j + offset))

    (weights,) = stay(weights)
    return pl.pallas_call(
        feed_kernel,
        grid=(FF_STEPS,),
        in_specs=[whole] * 4 + [columns(WIDTH), columns(WIDTH, FF_STEPS)],
        out_specs=[pl.BlockSpec((WIDTH, 2 * FF_STEP), lambda j: (0, j)), columns(TOKENS2)]
        + [whole] * 2,
        out_shape=[away(bf16(WIDTH, 2 * FF_HALF)), away(bf16(TOKENS2, FF_HALF))]
        + [away(v) for v in (OWN, SEND)],
        scratch_shapes=[pltpu.VMEM((TOKENS2, WIDTH), BF)] * 2
        + [pltpu.VMEM((WIDTH, TOKENS2), BF)] * 2
        + [pltpu.VMEM((TOKENS2, WIDTH), F32)],
        cost_estimate=COST,
        compiler_params=pltpu.CompilerParams(vmem_limit_bytes=40 * 1024 * 1024),
    )(*tokens, weights, weights)


def result_kernel(act, down, r_own, r_send, total):
    step = pl.program_id(0)
    part = dot(act[...], down[...], 1, 1)

    @pl.when(step == 0)
    def _():
        total[...] = part

    @pl.when(step > 0)
    def _():
        total[...] += part

    @pl.when(step == FF_STEPS - 1)
    def _():
        r_own[...] = total[:BLOCK]
        r_send[...] = total[BLOCK:].astype(BF)


def result_parts(act, weights):
    whole = pl.BlockSpec((BLOCK, WIDTH), lambda j: (0, 0))
    return pl.pallas_call(
        result_kernel,
        grid=(FF_STEPS,),
        in_specs=[
            pl.BlockSpec((TOKENS2, FF_STEP), lambda j: (0, j)),
            pl.BlockSpec((WIDTH, FF_STEP), lambda j: (0, j + FF_STEPS)),
        ],
        out_specs=[whole] * 2,
        out_shape=[away(OWN), away(SEND)],
        scratch_shapes=[pltpu.VMEM((TOKENS2, WIDTH), F32)],
        cost_estimate=COST,
        compiler_params=pltpu.CompilerParams(vmem_limit_bytes=24 * 1024 * 1024),
    )(*stay(act, weights))


def rows_of(ref, index, size):
    return ref[pl.ds(pl.multiple_of(index * size, size), size), :]


def value_grad_kernel(
    where, f_own, f_other, b_own, b_other, d_value, low, v0, v1, v2, v3, first_t, branch_t
):
    first_t[...] = jnp.concatenate([f_own[...], f_other[...]], axis=0).T
    branch_t[...] = jnp.concatenate([b_own[...], b_other[...]], axis=0).T
    for k, part in enumerate((v0, v1, v2, v3)):
        x = lax.rem(where[1] + k, 4)
        for half, (left, right) in enumerate(((first_t, d_value), (branch_t, low))):
            rows = jnp.concatenate([rows_of(left, 4 * z + x, 64) for z in range(4)], axis=0)
            part[:, half * HALF : half * HALF + HALF] = dot(rows, right[...]).astype(BF)


def query_grad_kernel(f_own, f_other, d_query, d_key, out):
    first = jnp.concatenate([f_own[...], f_other[...]], axis=0).T
    for pair in range(PAIRS):
        d_all = [pair_columns(d, pair) for d in (d_query, d_key)]
        out[pair] = dot(first, jnp.concatenate(d_all, axis=1)).astype(BF)


def norm_core_kernel(packed, other, norms):
    norms[...] = split_pair(join_pair(packed[...]) + join_pair(other[...]))


def feed_cut_kernel(where, part, u0, u1, u2, u3, d0, d1, d2, d3):
    for k, (up, down) in enumerate(((u0, d0), (u1, d1), (u2, d2), (u3, d3))):
        rows = pl.ds(pl.multiple_of(lax.rem(where[1] + k, 4) * 64, 64), 64)
        for j in range(4):
            up[:, j * 512 : j * 512 + 512] = part[rows, j * WIDTH : j * WIDTH + 512]
        slot = (-k) % 4
        down[...] = part[:, slot * WIDTH + 512 : slot * WIDTH + WIDTH]


def sum_of(pieces, *index):
    return sum(pieces[(j,) + index].astype(F32) for j in range(4))


def feed_turn_kernel(where, u0, u1, u2, u3, values, *outs):
    for k, out in enumerate(outs):
        slot = (-k) % 4
        span = slice(slot * 512, slot * 512 + 512)
        out[:, :512] = sum(p[:, span].astype(F32) for p in (u0, u1, u2, u3)).astype(BF)
        y = lax.rem(where[2] + k, 4)
        for half in range(2):
            span = pl.ds(pl.multiple_of(half * HALF + y * 128, 128), 128)
            out[:, 512 + half * 128 : 640 + half * 128] = values[:, span]


def feed_end_kernel(p0, p1, p2, p3, up, value, out):
    total = sum(p[...].astype(F32) for p in (p0, p1, p2, p3))
    up[...] = total[:, :512]
    value[...] = total[:, 512:640]
    out[...] = total[:, 640:]


def main_cut_kernel(main, norms, v0, v1, v2, v3, out):
    total = split_pair(sum(join_pair(norms[j]) for j in range(4)))
    for z in range(4):
        rows = slice(z * 256, z * 256 + 256)
        out[z, :256, :] = sum_of(main, rows, slice(None)).astype(BF)
        rows = slice(z * 64, z * 64 + 64)
        for j in range(4):
            span = slice(j * 256, j * 256 + 256)
            out[z, 256 + 16 * j : 272 + 16 * j, :] = total[:, span]
            values = sum(p[rows, span].astype(F32) for p in (v0, v1, v2, v3))
            out[z, 320 + 64 * j : 384 + 64 * j, :] = values.astype(BF)


def main_turn_kernel(where, main, d0, d1, d2, d3, o0, o1, o2, o3, values):
    pieces = []
    for j in range(4):
        rows = [main[j, 256 + 16 * i : 272 + 16 * i, :] for i in range(4)]
        pieces.append(join_pair(jnp.concatenate(rows, axis=1)))
    norms = split_pair(sum(pieces))
    for j in range(4):
        rows = slice(320 + 64 * j, 384 + 64 * j)
        values[:, j * 256 : j * 256 + 256] = sum_of(main, rows, slice(None)).astype(BF)
    for k, out in enumerate((o0, o1, o2, o3)):
        rows = pl.ds(pl.multiple_of((where[1] ^ k) * 64, 64), 64)
        out[:64, :256] = sum_of(main, rows, slice(None)).astype(BF)
        out[:64, 256:] = sum(p[rows, :].astype(F32) for p in (d0, d1, d2, d3)).astype(BF)
        for i in range(2):
            out[64 + 16 * i : 80 + 16 * i, :512] = norms[:, i * 512 : i * 512 + 512]
            out[64 + 16 * i : 80 + 16 * i, 512:] = jnp.zeros((16, 256), BF)


def main_end_kernel(where, p0, p1, p2, p3, query, key, down, n0, n1, n2, n3):
    pieces = (p0, p1, p2, p3)
    total = sum(p[:64, :].astype(F32) for p in pieces)
    query[...] = total[:, :128]
    key[...] = total[:, 128:256]
    down[...] = total[:, 256:]
    parts = []
    for p in pieces:
        rows = [p[64 + 16 * i : 80 + 16 * i, :512] for i in range(2)]
        parts.append(join_pair(jnp.concatenate(rows, axis=1)))
    norms = sum_in_order(parts, lambda a: where[3] ^ a)
    for k, ref in enumerate((n0, n1, n2, n3)):
        ref[...] = norms[k : k + 1, :]


def local(
    inputs,
    lengths,
    ln1_gain,
    ln1_bias,
    ln2_gain,
    ln2_bias,
    w_query,
    w_key,
    w_value,
    w_out,
    w_up,
    w_down,
    cotangent,
):
    x = lax.axis_index(X)
    block = lax.axis_index(("xl", "y"))
    z = lax.axis_index("z")
    where = [z, x, lax.axis_index("y"), lax.axis_index(("xh", "core"))]
    where = jnp.stack(where).astype(jnp.int32)
    gain_one, bias_one, gain_two, bias_two = [
        v.reshape(1, WIDTH) for v in (ln1_gain, ln1_bias, ln2_gain, ln2_bias)
    ]

    main, feed = call(
        prepare_kernel,
        stay(w_query, w_key, w_value, w_out.T, w_up, w_down.T),
        [bf16(64, 384), bf16(64, 1152)],
    )
    main = [turn_x(main, k) for k in range(4)]
    feed = after(feed, main)
    main = place(main, [x ^ k for k in range(4)]).reshape(256, 384)
    main = spread(main, "z").reshape(WIDTH, 384)
    feed = [turn_y(feed, k) for k in range(4)]
    main = jnp.broadcast_to(main, (4, WIDTH, 384))
    gain_one = after(gain_one, main)
    wqkv = trade(main, "y")
    feed_rows, wo = call(
        feed_rows_kernel,
        after(feed, main),
        [away(bf16(64, 2 * FF_HALF)), bf16(64, HALF)],
        [where],
    )
    feed_weights = lax.all_gather(feed_rows, ("z", "xh", "xl"), axis=0, tiled=True)
    wo = place(ring_trade([wo] * 4, X), [lax.rem(x - k + 4, 4) for k in range(4)])
    wo = ring_trade([wo.reshape(256, HALF)] * 4, "z")
    wo = place(wo, [lax.rem(z - k + 4, 4) for k in range(4)]).reshape(WIDTH, HALF)
    wqkv = after(wqkv, wo)
    wo = (wo, (WIDTH, HALF), (0, 0))

    ends = jnp.cumsum(jnp.concatenate([lengths, core_swap(lengths)], axis=0), axis=1)

    def last_segment(which):
        return jnp.sum((which * BLOCK + BLOCK - 1 >= ends).astype(jnp.int32), axis=1)

    here = last_segment(block)
    before = jnp.where(block > 0, last_segment(block - 1), -1)
    zeros = jnp.zeros((2,), jnp.int32)
    flags = [(block >= k) & (last_segment(block - k) == before) for k in range(1, REACH + 1)]
    flags += [
        (block + k < 8) & (last_segment(block + k - 1) == here) for k in range(1, REACH + 1)
    ]
    rest = [zeros + block * BLOCK, before, here, zeros] + [f.astype(jnp.int32) for f in flags]
    info = jnp.concatenate([ends, jnp.stack(rest, axis=1)], axis=1)

    first_in, grad_low = call(
        first_norm_kernel, stay(inputs, cotangent, gain_one, bias_one), [SEND, away(SEND)]
    )
    first = [first_in, core_swap(first_in)]
    grads = [grad_low, core_swap(grad_low)]

    queries, keys, values, state = enter(info, first, wqkv)
    queries, keys, values = stay(queries, keys, values)
    far = tensor_shift(state, 4)
    states = call(relay_kernel, [state, far], [STATE] * 3, [where])
    states = [ring_shift(states[k - 1], "y", k) for k in (1, 2, 3)] + [far]
    numer, denom = attention_call(
        inner_kernel, info, [queries, keys, values], [WIDE32, WIDE32]
    )
    attended, low, inverse, own, send = attention_call(
        join_kernel,
        info,
        [queries, numer, denom] + states,
        [away(WIDE32), away(WIDE16), away(WIDE32), OWN, SEND],
        [wo],
    )
    hidden, second_in = call(
        second_norm_kernel,
        stay(inputs, gain_two, bias_two) + [own, core_swap(send)],
        [away(OWN), SEND],
    )
    feed_grad, act, d_own, d_send = feed_forward(
        [second_in, core_swap(second_in)] + stay(*grads), feed_weights
    )
    d_hidden, branch_low, sums = call(
        second_back_kernel,
        stay(hidden, gain_two, d_own) + [core_swap(d_send)] + stay(cotangent),
        [away(OWN), SEND, f32(8, WIDTH)],
    )
    branch = [branch_low, core_swap(branch_low)]

    feed_grad = lax.psum_scatter(feed_grad, "z", scatter_dimension=0, tiled=True)

    back_state, scaled, shift = attention_call(
        back_state_kernel,
        info,
        [queries, values] + stay(attended, inverse) + branch,
        [STATE, WIDE16, WIDE32],
        [wo],
    )
    back_states = [tensor_shift(back_state, -k) for k in range(1, REACH + 1)]
    d_queries, d_key, d_value = attention_call(
        back_inner_kernel,
        info,
        [queries, keys, values, scaled, shift] + stay(*states),
        [WIDE16, WIDE32, WIDE32],
    )
    d_keys, d_values, own, send = attention_call(
        back_join_kernel,
        info,
        [keys, values, d_queries, d_key, d_value] + back_states,
        [WIDE16, WIDE16, away(OWN), SEND],
        [(wqkv, (4, WIDTH, 384), (0, 0, 0))],
    )
    (gqk,) = call(
        query_grad_kernel,
        stay(*first) + [d_queries, d_keys],
        [away(bf16(4, WIDTH, 256))],
        limit=32,
    )
    d_values = after(d_values, gqk)
    gqk = trade(gqk, "y")
    gvo = call(
        value_grad_kernel,
        stay(*first, *branch) + [d_values] + stay(low),
        [away(bf16(256, WIDTH))] * 4,
        [where],
        limit=32,
        scratch=[pltpu.VMEM((WIDTH, TOKENS2), BF)] * 2,
    )
    sums = after(sums, gvo)
    gvo = ring_trade(gvo, X)
    grad_inputs, packed = call(
        first_back_kernel,
        stay(inputs, gain_one, d_hidden, own) + [core_swap(send), sums],
        [away(OWN), bf16(16, WIDTH)],
    )
    r_own, r_send = result_parts(after(act, packed), feed_weights)
    packed = after(packed, r_own)
    (norms,) = call(norm_core_kernel, [packed, core_swap(packed)], [bf16(16, WIDTH)])
    norms = spread(after(norms, gqk), "y")

    (cut,) = call(main_cut_kernel, [gqk, norms] + stay(*gvo), [bf16(4, 576, 256)])
    feed_grad = call(
        feed_cut_kernel,
        stay(after(feed_grad, cut)),
        [bf16(64, FF_HALF)] * 4 + [bf16(BLOCK, HALF)] * 4,
        [where],
    )
    cut = after(trade(cut, "z"), feed_grad)
    downs, ups = ring_trade(feed_grad[4:], "y"), ring_trade(feed_grad[:4], X)

    sent = call(
        main_turn_kernel, [cut] + downs, [bf16(96, 768)] * 4 + [bf16(64, WIDTH)], [where]
    )
    turned = [turn_x(sent[k], k, True) for k in range(4)]
    ups = after(ups, turned[:2])
    grad_query, grad_key, grad_down, *norms = call(
        main_end_kernel,
        turned,
        [f32(64, 128)] * 2 + [f32(64, 512)] + [f32(1, WIDTH)] * 4,
        [where],
    )
    sent = call(feed_turn_kernel, ups + [sent[4]], [bf16(64, 768)] * 4, [where])
    grad_up, grad_value, grad_out = call(
        feed_end_kernel,
        [turn_y(sent[k], k) for k in range(4)],
        [f32(64, 512)] + [f32(64, 128)] * 2,
    )
    norms = [v.reshape(WIDTH) for v in norms]
    result = hidden + (r_own + core_swap(after(r_send, gqk)).astype(F32))
    return (
        result,
        grad_inputs,
        norms[0],
        norms[1],
        norms[2],
        norms[3],
        grad_query,
        grad_key,
        grad_value,
        grad_out.T,
        grad_up,
        grad_down.T,
    )


def solution(mesh):
    axes = ("z", "xh", "core", "xl", "y")
    split = Mesh(mesh.devices.reshape(4, 2, 2, 2, 4), axes)
    dp, tensor = ("z", "xh", "core"), ("xl", "y")
    tokens, rows, cols = P(axes, None), P(dp, tensor), P(tensor, dp)
    in_specs = (tokens, P(dp, None), P(), P(), P(), P(), rows, rows, rows, cols, rows, cols, tokens)
    out_specs = (tokens, tokens, P(), P(), P(), P(), rows, rows, rows, cols, rows, cols)
    return jax.shard_map(
        local, mesh=split, in_specs=in_specs, out_specs=out_specs, check_vma=False
    )
```

```python
import jax
import jax.numpy as jnp
from jax import lax
from jax.experimental import pallas as pl
from jax.experimental.pallas import tpu as pltpu
from jax.sharding import Mesh, PartitionSpec as P

BF = jnp.bfloat16
F32 = jnp.float32
EPS = 1e-05
BLOCK = 256
WIDTH = 1024
HALF = 512
FF_HALF = 2048
PAIRS = 4
STATE_ROWS = 80
X = ("xh", "xl")
REACH = 4


def dot(left, right, left_dim=1, right_dim=0):
    return lax.dot_general(
        left, right, (((left_dim,), (right_dim,)), ((), ())), preferred_element_type=F32
    )


def ring_shift(value, axis, step):
    return lax.ppermute(value, axis, [(i, (i + step) % 4) for i in range(4)])


def ring_trade(blocks, axis):
    got = {k: ring_shift(blocks[k], axis, k) for k in (1, 3, 2)}
    return [blocks[0], got[1], got[2], got[3]]


def core_swap(value):
    return lax.ppermute(value, "core", [(0, 1), (1, 0)])


def tensor_shift(value, step):
    return lax.ppermute(
        value, ("xl", "y"), [(i, i + step) for i in range(8) if 0 <= i + step < 8]
    )


def turn_y(value, step):
    pairs = []
    for c in range(2):
        for xl in range(2):
            for y in range(4):
                pairs.append(((c * 2 + xl) * 4 + y, (xl * 2 + c) * 4 + (y + step) % 4))
    return lax.ppermute(value, ("core", "xl", "y"), pairs)


def turn_x(value, step, back=False):
    high, low = step // 2, step % 2
    pairs = []
    for xh in range(2):
        for c in range(2):
            for xl in range(2):
                core, x_low = (xl ^ low, c) if back else (xl, c ^ low)
                pairs.append(((xh * 2 + c) * 2 + xl, ((xh ^ high) * 2 + core) * 2 + x_low))
    return lax.ppermute(value, ("xh", "core", "xl"), pairs)


def after(values, earlier):
    return lax.optimization_barrier((values, earlier))[0]


def place(pieces, positions):
    out = jnp.zeros((4,) + pieces[0].shape, pieces[0].dtype)
    for piece, position in zip(pieces, positions):
        out = lax.dynamic_update_index_in_dim(out, piece, position, 0)
    return out


def trade(blocks, axis):
    return lax.all_to_all(blocks, axis, split_axis=0, concat_axis=0, tiled=True)


def spread(value, axis):
    return trade(jnp.broadcast_to(value, (4,) + value.shape), axis)


def stay(*values):
    return [pltpu.with_memory_space_constraint(v, pltpu.HBM) for v in values]


def away(shape):
    return pltpu.HBM(shape.shape, shape.dtype)


COST = pl.CostEstimate(flops=1000, bytes_accessed=1000, transcendentals=0)


def call(kernel, operands, outs, scalars=(), limit=16, scratch=()):
    def whole(value):
        return pl.BlockSpec(value.shape, lambda i: (0,) * len(value.shape))

    return pl.pallas_call(
        kernel,
        grid=(1,),
        in_specs=[pl.BlockSpec(memory_space=pltpu.SMEM)] * len(scalars)
        + [whole(o) for o in operands],
        out_specs=[whole(o) for o in outs],
        out_shape=list(outs),
        scratch_shapes=list(scratch),
        cost_estimate=COST,
        compiler_params=pltpu.CompilerParams(vmem_limit_bytes=limit * 1024 * 1024),
    )(*scalars, *operands)


def f32(*shape):
    return jax.ShapeDtypeStruct(shape, F32)


def bf16(*shape):
    return jax.ShapeDtypeStruct(shape, BF)


def lanes(shape):
    return lax.broadcasted_iota(jnp.int32, shape, 1)


def head_sums(values):
    left = lanes(values.shape) < 64
    first = jnp.sum(jnp.where(left, values, 0.0), axis=1, keepdims=True)
    second = jnp.sum(jnp.where(left, 0.0, values), axis=1, keepdims=True)
    return jnp.where(left, first, second)


def segments_of(info, group, places):
    return sum((places >= info[group, k]).astype(jnp.int32) for k in range(4))


def column_segments(info, group):
    base = info[group, 4]
    return segments_of(info, group, base + lax.broadcasted_iota(jnp.int32, (BLOCK, 1), 0))


def pair_mask(info, group):
    base = info[group, 4]
    rows = lax.broadcasted_iota(jnp.int32, (BLOCK, 1), 0)
    cols = lax.broadcasted_iota(jnp.int32, (1, BLOCK), 1)
    row_seg = segments_of(info, group, base + rows)
    col_seg = segments_of(info, group, base + cols)
    return (rows >= cols) & (row_seg == col_seg)


def carried_of(info, group):
    return column_segments(info, group) == info[group, 5]


def in_last_of(info, group):
    return column_segments(info, group) == info[group, 6]


def masked_mean(values, keep):
    count = jnp.maximum(jnp.sum(keep.astype(F32), axis=0, keepdims=True), 1.0)
    mean = jnp.sum(jnp.where(keep, values, 0.0), axis=0, keepdims=True) / count
    return mean.astype(BF).astype(F32)


def pack_state(matrix, row, center, out, group, pair):
    left = lanes((64, 128)) < 64
    out[group, pair, :64, :] = jnp.where(left, matrix[:64], matrix[64:]).astype(BF)
    high = row.astype(BF).astype(F32)
    place = lax.broadcasted_iota(jnp.int32, (STATE_ROWS - 64, 128), 0)
    rest = jnp.where(place == 0, high, jnp.where(place == 1, row - high, 0.0))
    out[group, pair, 64:, :] = jnp.where(place == 2, center, rest).astype(BF)


def unpack_states(info, group, states, pair, flags):
    left = lanes((64, 128)) < 64
    parts, rows, centers = [], [], []
    for k, state in enumerate(states, 1):
        keep = info[group, flags + k - 1].astype(F32)
        packed = state[0, pair].astype(F32) * keep
        memory = packed[:64]
        parts.append(
            jnp.concatenate([jnp.where(left, memory, 0.0), jnp.where(left, 0.0, memory)], axis=0)
        )
        rows.append(packed[64:65] + packed[65:66])
        centers.append(packed[66:67])
    return parts, rows, centers


def pair_columns(ref, pair):
    return ref[:, pair * 128 : pair * 128 + 128]


def enter_kernel(info, own, other, wqkv, queries, keys, values, out):
    tokens = jnp.concatenate([own[...], other[...]], axis=0)
    both = jnp.concatenate([wqkv[0, :, 256:], wqkv[1, :, 256:]], axis=1)
    values[...] = dot(tokens, both).astype(BF)
    for pair in range(2):
        feat = dot(tokens, wqkv[pair, :, :256])
        feat = jnp.where(feat > 0.0, feat + 1.0, jnp.exp(jnp.minimum(feat, 0.0))).astype(BF)
        queries[:, pair * 128 : pair * 128 + 128] = feat[:, :128]
        keys[:, pair * 128 : pair * 128 + 128] = feat[:, 128:]
    for group in range(2):
        last = in_last_of(info, group)
        rows = slice(group * BLOCK, group * BLOCK + BLOCK)
        for pair in range(2):
            span = slice(pair * 128, pair * 128 + 128)
            v = values[rows, span].astype(F32)
            kept = jnp.where(last, keys[rows, span].astype(F32), 0.0)
            center = masked_mean(v, last)
            matrix = dot(kept.astype(BF), (v - center).astype(BF), 0, 0)
            row = jnp.sum(kept, axis=0, keepdims=True)
            pack_state(matrix, row, center, out, group, pair)


def enter(info, tokens, wqkv):
    whole = pl.BlockSpec((BLOCK, WIDTH), lambda j: (0, 0))
    columns = pl.BlockSpec((TOKENS2, 256), lambda j: (0, j))
    return pl.pallas_call(
        enter_kernel,
        grid=(2,),
        in_specs=[
            pl.BlockSpec(memory_space=pltpu.SMEM),
            whole,
            whole,
            pl.BlockSpec((2, WIDTH, 384), lambda j: (j, 0, 0)),
        ],
        out_specs=[columns] * 3
        + [pl.BlockSpec((2, 2, STATE_ROWS, 128), lambda j: (0, j, 0, 0))],
        out_shape=[away(WIDE16)] * 3 + [STATE],
        cost_estimate=COST,
        compiler_params=pltpu.CompilerParams(vmem_limit_bytes=24 * 1024 * 1024),
    )(info, *tokens, *stay(wqkv))


def relay_kernel(where, own, far, *outs):
    for k, out in enumerate(outs, 1):
        out[...] = jnp.where(where[2] + k < 4, own[...].astype(F32), far[...].astype(F32)).astype(BF)


def inner_kernel(info, queries, keys, values, numer, denom):
    group = pl.program_id(0)
    allowed = pair_mask(info, group)
    left = lanes((BLOCK, 128)) < 64
    for pair in range(PAIRS):
        q, k = pair_columns(queries, pair), pair_columns(keys, pair)
        v = pair_columns(values, pair)
        zero = jnp.zeros_like(q)
        parts = []
        for side in (left, jnp.logical_not(left)):
            scores = jnp.where(allowed, dot(jnp.where(side, q, zero), k, 1, 1), 0.0)
            parts.append((dot(scores.astype(BF), v), jnp.sum(scores, axis=1, keepdims=True)))
        span = slice(pair * 128, pair * 128 + 128)
        numer[:, span] = jnp.where(left, parts[0][0], parts[1][0])
        denom[:, span] = jnp.where(left, parts[0][1], parts[1][1])


def store_halves(group, partial, own, send):
    @pl.when(group == 0)
    def _():
        own[...] = partial

    @pl.when(group == 1)
    def _():
        send[...] = partial.astype(BF)


def join_kernel(
    info, queries, numer, denom, s1, s2, s3, s4, out_rows, wide, low, inverse, own, send
):
    group = pl.program_id(0)
    carried = carried_of(info, group)
    outs = []
    for pair in range(PAIRS):
        q = pair_columns(queries, pair)
        parts, rows, centers = unpack_states(info, group, (s1, s2, s3, s4), pair, 8)
        num, den = dot(q, sum(parts).astype(BF)), 0.0
        for row, center in zip(rows, centers):
            weight = head_sums(q.astype(F32) * row)
            num, den = num + weight * center, den + weight
        inv = 1.0 / (pair_columns(denom, pair) + jnp.where(carried, den, 0.0))
        out = (pair_columns(numer, pair) + jnp.where(carried, num, 0.0)) * inv
        span = slice(pair * 128, pair * 128 + 128)
        wide[:, span] = out
        inverse[:, span] = inv
        outs.append(out.astype(BF))
        low[:, span] = outs[-1]
    partial = dot(jnp.concatenate(outs, axis=1), out_rows[...], 1, 1)
    store_halves(group, partial, own, send)


def back_state_kernel(
    info, queries, values, attended, inverse, b_own, b_other, out_rows, out, scaled, shift
):
    group = pl.program_id(0)
    carried = carried_of(info, group)
    branch = jnp.where(group == 0, b_own[...], b_other[...])
    grad = dot(branch, out_rows[...]).astype(BF).astype(F32)
    for pair in range(PAIRS):
        span = slice(pair * 128, pair * 128 + 128)
        g = (grad[:, span] * pair_columns(inverse, pair)).astype(BF)
        wide = g.astype(F32)
        e = -head_sums(wide * pair_columns(attended, pair))
        scaled[:, span] = g
        shift[:, span] = e
        center = masked_mean(pair_columns(values, pair).astype(F32), carried)
        kept = jnp.where(carried, pair_columns(queries, pair).astype(F32), 0.0)
        row = jnp.sum(kept * (e + head_sums(wide * center)), axis=0, keepdims=True)
        pack_state(dot(kept.astype(BF), g, 0, 0), row, center, out, 0, pair)


def back_inner_kernel(
    info, queries, keys, values, scaled, shift, s1, s2, s3, s4, d_query, d_key, d_value
):
    group = pl.program_id(0)
    allowed = pair_mask(info, group)
    carried = carried_of(info, group)
    left = lanes((BLOCK, 128)) < 64
    for pair in range(PAIRS):
        q, k = pair_columns(queries, pair), pair_columns(keys, pair)
        v, g, e = [pair_columns(r, pair) for r in (values, scaled, shift)]
        zero = jnp.zeros_like(q)
        parts = []
        for head, side in enumerate((left, jnp.logical_not(left))):
            scores = jnp.where(allowed, dot(jnp.where(side, q, zero), k, 1, 1), 0.0).astype(BF)
            d_scores = dot(jnp.where(side, g, zero), v, 1, 1) + e[:, 64 * head : 64 * head + 1]
            d_scores = jnp.where(allowed, d_scores, 0.0).astype(BF)
            parts.append((dot(d_scores, k), dot(d_scores, q, 0, 0), dot(scores, g, 0, 0)))
        dq, dk, dv = [jnp.where(left, a, b) for a, b in zip(*parts)]
        memories, rows, centers = unpack_states(info, group, (s1, s2, s3, s4), pair, 8)
        more = dot(g, sum(memories).astype(BF), 1, 1)
        for row, center in zip(rows, centers):
            more = more + row * (e + head_sums(g.astype(F32) * center))
        dq = dq + jnp.where(carried, more, 0.0)
        span = slice(pair * 128, pair * 128 + 128)
        d_query[:, span] = (dq * jnp.minimum(q.astype(F32), 1.0)).astype(BF)
        d_key[:, span] = dk
        d_value[:, span] = dv


def back_join_kernel(
    info, keys, values, d_query, d_key, d_value, s1, s2, s3, s4, wqkv,
    key_out, value_out, own, send,
):
    group = pl.program_id(0)
    last = in_last_of(info, group)
    partial = 0.0
    for pair in range(PAIRS):
        k, v = pair_columns(keys, pair), pair_columns(values, pair)
        memories, rows, centers = unpack_states(info, group, (s1, s2, s3, s4), pair, 12)
        memory = sum(memories).astype(BF)
        center, row = centers[0], rows[0]
        for m, r, c in zip(memories[1:], rows[1:], centers[1:]):
            away = jnp.broadcast_to(center - c, (16, 128)).astype(BF)
            row = row + r + dot(away, m.astype(BF), 1, 1)[:1]
        more = dot((v.astype(F32) - center).astype(BF), memory, 1, 1) + row
        dk = pair_columns(d_key, pair) + jnp.where(last, more, 0.0)
        dv = pair_columns(d_value, pair) + jnp.where(last, dot(k, memory), 0.0)
        span = slice(pair * 128, pair * 128 + 128)
        dk = (dk * jnp.minimum(k.astype(F32), 1.0)).astype(BF)
        dv = dv.astype(BF)
        key_out[:, span] = dk
        value_out[:, span] = dv
        d_pair = jnp.concatenate([pair_columns(d_query, pair), dk, dv], axis=1)
        partial = partial + dot(d_pair, wqkv[pair], 1, 1)
    store_halves(group, partial, own, send)


def attention_call(kernel, info, operands, outs, weights=()):
    def spec(shape):
        if len(shape) == 4:
            return pl.BlockSpec((1,) + shape[1:], lambda g: (g, 0, 0, 0))
        if shape[0] == TOKENS2:
            return pl.BlockSpec((BLOCK, shape[1]), lambda g: (g, 0))
        return pl.BlockSpec(shape, lambda g: (0, 0))

    def fixed(shape, index):
        return pl.BlockSpec(shape, lambda g: index)

    return pl.pallas_call(
        kernel,
        grid=(2,),
        in_specs=[pl.BlockSpec(memory_space=pltpu.SMEM)]
        + [spec(a.shape) for a in operands]
        + [fixed(shape, index) for _, shape, index in weights],
        out_specs=[spec(o.shape) for o in outs],
        out_shape=outs,
        cost_estimate=COST,
        compiler_params=pltpu.CompilerParams(vmem_limit_bytes=20 * 1024 * 1024),
    )(info, *operands, *stay(*[w for w, _, _ in weights]))


TOKENS2 = 2 * BLOCK
STATE = bf16(2, PAIRS, STATE_ROWS, 128)
WIDE32 = f32(TOKENS2, HALF)
WIDE16 = bf16(TOKENS2, HALF)
OWN = f32(BLOCK, WIDTH)
SEND = bf16(BLOCK, WIDTH)


def prepare_kernel(w_query, w_key, w_value, w_out, w_up, w_down, main, feed):
    main[:, :128] = w_query[...].astype(BF)
    main[:, 128:256] = w_key[...].astype(BF)
    main[:, 256:] = w_value[...].astype(BF)
    feed[:, :512] = w_up[...].astype(BF)
    feed[:, 512:1024] = w_down[...].astype(BF)
    feed[:, 1024:] = w_out[...].astype(BF)


def unit_of(values):
    centred = values - jnp.mean(values, axis=-1, keepdims=True)
    scale = lax.rsqrt(jnp.mean(centred * centred, axis=-1, keepdims=True) + EPS)
    return centred * scale, scale


def feed_rows_kernel(where, p0, p1, p2, p3, feed, out):
    for k, p in enumerate((p0, p1, p2, p3)):
        feed[:, k * 512 : k * 512 + 512] = p[:, :512]
        feed[:, FF_HALF + k * 512 : FF_HALF + k * 512 + 512] = p[:, 512:1024]
        y = lax.rem(where[2] - k + 4, 4)
        out[:, pl.ds(pl.multiple_of(y * 128, 128), 128)] = p[:, 1024:]


def first_norm_kernel(inputs, cotangent, gain, bias, first_in, grad_low):
    unit, _ = unit_of(inputs[...])
    first_in[...] = (unit * gain[...] + bias[...]).astype(BF)
    grad_low[...] = cotangent[...].astype(BF)


def second_norm_kernel(inputs, gain, bias, own, got, hidden, second_in):
    total = inputs[...] + (own[...] + got[...].astype(F32))
    hidden[...] = total
    unit, _ = unit_of(total)
    second_in[...] = (unit * gain[...] + bias[...]).astype(BF)


def norm_slope(values, gain, own, got):
    unit, scale = unit_of(values[...])
    d_out = own[...] + got[...].astype(F32)
    gh = d_out * gain[...]
    slope = scale * (
        gh
        - jnp.mean(gh, axis=-1, keepdims=True)
        - unit * jnp.mean(gh * unit, axis=-1, keepdims=True)
    )
    gains = jnp.sum(d_out * unit, axis=0, keepdims=True)
    return slope, gains, jnp.sum(d_out, axis=0, keepdims=True)


def second_back_kernel(hidden, gain, own, got, cotangent, d_hidden, low, sums):
    slope, gains, biases = norm_slope(hidden, gain, own, got)
    total = cotangent[...] + slope
    d_hidden[...] = total
    low[...] = total.astype(BF)
    sums[...] = jnp.zeros_like(sums)
    sums[2:3, :] = gains
    sums[3:4, :] = biases


def split_pair(sums):
    high = sums.astype(BF).astype(F32)
    return jnp.concatenate([high, sums - high], axis=0).astype(BF)


def join_pair(packed):
    wide = packed.astype(F32)
    return wide[:8] + wide[8:]


def first_back_kernel(inputs, gain, d_hidden, own, got, sums, grad_inputs, packed):
    slope, gains, biases = norm_slope(inputs, gain, own, got)
    grad_inputs[...] = d_hidden[...] + slope
    place = lax.broadcasted_iota(jnp.int32, sums.shape, 0)
    total = jnp.where(place == 0, gains, jnp.where(place == 1, biases, sums[...]))
    packed[...] = split_pair(total)


def sum_in_order(pieces, position):
    total = 0.0
    for a in range(4):
        k = position(a)
        total = total + sum(jnp.where(k == i, p, 0.0) for i, p in enumerate(pieces))
    return total


FF_STEP = 512
FF_STEPS = FF_HALF // FF_STEP


def gelu_parts(u):
    density = jnp.exp(-0.5 * u * u) * 0.3989422804014327
    return 0.5 * (1.0 + lax.erf(u * 0.7071067811865476)), density


def feed_kernel(
    s_own, s_other, g_own, g_other, up, down,
    grads, act_out, d_own, d_send, second, grad, second_t, grad_t, d_total,
):
    step = pl.program_id(0)

    @pl.when(step == 0)
    def _():
        second[:BLOCK] = s_own[...]
        second[BLOCK:] = s_other[...]
        grad[:BLOCK] = g_own[...]
        grad[BLOCK:] = g_other[...]
        second_t[...] = second[...].T
        grad_t[...] = grad[...].T
        d_total[...] = jnp.zeros_like(d_total)

    u = dot(second[...], up[...])
    d_act = dot(grad[...], down[...])
    below, density = gelu_parts(u)
    act = (u * below).astype(BF)
    d_up = (d_act * (below + u * density)).astype(BF)
    grads[:, :FF_STEP] = dot(second_t[...], d_up).astype(BF)
    grads[:, FF_STEP:] = dot(grad_t[...], act).astype(BF)
    d_total[...] += dot(d_up, up[...], 1, 1)
    act_out[...] = act

    @pl.when(step == FF_STEPS - 1)
    def _():
        d_own[...] = d_total[:BLOCK]
        d_send[...] = d_total[BLOCK:].astype(BF)


def feed_forward(tokens, weights):
    whole = pl.BlockSpec((BLOCK, WIDTH), lambda j: (0, 0))

    def columns(rows, offset=0):
        return pl.BlockSpec((rows, FF_STEP), lambda j: (0, j + offset))

    (weights,) = stay(weights)
    return pl.pallas_call(
        feed_kernel,
        grid=(FF_STEPS,),
        in_specs=[whole] * 4 + [columns(WIDTH), columns(WIDTH, FF_STEPS)],
        out_specs=[pl.BlockSpec((WIDTH, 2 * FF_STEP), lambda j: (0, j)), columns(TOKENS2)]
        + [whole] * 2,
        out_shape=[away(bf16(WIDTH, 2 * FF_HALF)), away(bf16(TOKENS2, FF_HALF))]
        + [away(v) for v in (OWN, SEND)],
        scratch_shapes=[pltpu.VMEM((TOKENS2, WIDTH), BF)] * 2
        + [pltpu.VMEM((WIDTH, TOKENS2), BF)] * 2
        + [pltpu.VMEM((TOKENS2, WIDTH), F32)],
        cost_estimate=COST,
        compiler_params=pltpu.CompilerParams(vmem_limit_bytes=34 * 1024 * 1024),
    )(*tokens, weights, weights)


def result_kernel(act, down, r_own, r_send, total):
    step = pl.program_id(0)
    part = dot(act[...], down[...], 1, 1)

    @pl.when(step == 0)
    def _():
        total[...] = part

    @pl.when(step > 0)
    def _():
        total[...] += part

    @pl.when(step == FF_STEPS - 1)
    def _():
        r_own[...] = total[:BLOCK]
        r_send[...] = total[BLOCK:].astype(BF)


def result_parts(act, weights):
    whole = pl.BlockSpec((BLOCK, WIDTH), lambda j: (0, 0))
    return pl.pallas_call(
        result_kernel,
        grid=(FF_STEPS,),
        in_specs=[
            pl.BlockSpec((TOKENS2, FF_STEP), lambda j: (0, j)),
            pl.BlockSpec((WIDTH, FF_STEP), lambda j: (0, j + FF_STEPS)),
        ],
        out_specs=[whole] * 2,
        out_shape=[away(OWN), away(SEND)],
        scratch_shapes=[pltpu.VMEM((TOKENS2, WIDTH), F32)],
        cost_estimate=COST,
        compiler_params=pltpu.CompilerParams(vmem_limit_bytes=24 * 1024 * 1024),
    )(*stay(act, weights))


def rows_of(ref, index, size):
    return ref[pl.ds(pl.multiple_of(index * size, size), size), :]


def value_grad_kernel(
    where, f_own, f_other, b_own, b_other, d_value, low, v0, v1, v2, v3, first_t, branch_t
):
    first_t[...] = jnp.concatenate([f_own[...], f_other[...]], axis=0).T
    branch_t[...] = jnp.concatenate([b_own[...], b_other[...]], axis=0).T
    for k, part in enumerate((v0, v1, v2, v3)):
        x = lax.rem(where[1] + k, 4)
        for half, (left, right) in enumerate(((first_t, d_value), (branch_t, low))):
            rows = jnp.concatenate([rows_of(left, 4 * z + x, 64) for z in range(4)], axis=0)
            part[:, half * HALF : half * HALF + HALF] = dot(rows, right[...]).astype(BF)


def query_grad_kernel(f_own, f_other, d_query, d_key, out):
    first = jnp.concatenate([f_own[...], f_other[...]], axis=0).T
    for pair in range(PAIRS):
        d_all = [pair_columns(d, pair) for d in (d_query, d_key)]
        out[pair] = dot(first, jnp.concatenate(d_all, axis=1)).astype(BF)


def norm_core_kernel(packed, other, norms):
    norms[...] = split_pair(join_pair(packed[...]) + join_pair(other[...]))


def feed_cut_kernel(where, part, u0, u1, u2, u3, d0, d1, d2, d3):
    for k, (up, down) in enumerate(((u0, d0), (u1, d1), (u2, d2), (u3, d3))):
        rows = pl.ds(pl.multiple_of(lax.rem(where[1] + k, 4) * 64, 64), 64)
        for j in range(4):
            up[:, j * 512 : j * 512 + 512] = part[rows, j * WIDTH : j * WIDTH + 512]
        slot = (-k) % 4
        down[...] = part[:, slot * WIDTH + 512 : slot * WIDTH + WIDTH]


def sum_of(pieces, *index):
    return sum(pieces[(j,) + index].astype(F32) for j in range(4))


def feed_turn_kernel(where, u0, u1, u2, u3, values, *outs):
    for k, out in enumerate(outs):
        slot = (-k) % 4
        span = slice(slot * 512, slot * 512 + 512)
        out[:, :512] = sum(p[:, span].astype(F32) for p in (u0, u1, u2, u3)).astype(BF)
        y = lax.rem(where[2] + k, 4)
        for half in range(2):
            span = pl.ds(pl.multiple_of(half * HALF + y * 128, 128), 128)
            out[:, 512 + half * 128 : 640 + half * 128] = values[:, span]


def feed_end_kernel(p0, p1, p2, p3, up, value, out):
    total = sum(p[...].astype(F32) for p in (p0, p1, p2, p3))
    up[...] = total[:, :512]
    value[...] = total[:, 512:640]
    out[...] = total[:, 640:]


def main_cut_kernel(main, norms, v0, v1, v2, v3, out):
    total = split_pair(sum(join_pair(norms[j]) for j in range(4)))
    for z in range(4):
        rows = slice(z * 256, z * 256 + 256)
        out[z, :256, :] = sum_of(main, rows, slice(None)).astype(BF)
        rows = slice(z * 64, z * 64 + 64)
        for j in range(4):
            span = slice(j * 256, j * 256 + 256)
            out[z, 256 + 16 * j : 272 + 16 * j, :] = total[:, span]
            values = sum(p[rows, span].astype(F32) for p in (v0, v1, v2, v3))
            out[z, 320 + 64 * j : 384 + 64 * j, :] = values.astype(BF)


def main_turn_kernel(where, main, d0, d1, d2, d3, o0, o1, o2, o3, values):
    pieces = []
    for j in range(4):
        rows = [main[j, 256 + 16 * i : 272 + 16 * i, :] for i in range(4)]
        pieces.append(join_pair(jnp.concatenate(rows, axis=1)))
    norms = split_pair(sum(pieces))
    for j in range(4):
        rows = slice(320 + 64 * j, 384 + 64 * j)
        values[:, j * 256 : j * 256 + 256] = sum_of(main, rows, slice(None)).astype(BF)
    for k, out in enumerate((o0, o1, o2, o3)):
        rows = pl.ds(pl.multiple_of((where[1] ^ k) * 64, 64), 64)
        out[:64, :256] = sum_of(main, rows, slice(None)).astype(BF)
        out[:64, 256:] = sum(p[rows, :].astype(F32) for p in (d0, d1, d2, d3)).astype(BF)
        for i in range(2):
            out[64 + 16 * i : 80 + 16 * i, :512] = norms[:, i * 512 : i * 512 + 512]
            out[64 + 16 * i : 80 + 16 * i, 512:] = jnp.zeros((16, 256), BF)


def main_end_kernel(where, p0, p1, p2, p3, query, key, down, n0, n1, n2, n3):
    pieces = (p0, p1, p2, p3)
    total = sum(p[:64, :].astype(F32) for p in pieces)
    query[...] = total[:, :128]
    key[...] = total[:, 128:256]
    down[...] = total[:, 256:]
    parts = []
    for p in pieces:
        rows = [p[64 + 16 * i : 80 + 16 * i, :512] for i in range(2)]
        parts.append(join_pair(jnp.concatenate(rows, axis=1)))
    norms = sum_in_order(parts, lambda a: where[3] ^ a)
    for k, ref in enumerate((n0, n1, n2, n3)):
        ref[...] = norms[k : k + 1, :]


def local(
    inputs,
    lengths,
    ln1_gain,
    ln1_bias,
    ln2_gain,
    ln2_bias,
    w_query,
    w_key,
    w_value,
    w_out,
    w_up,
    w_down,
    cotangent,
):
    x = lax.axis_index(X)
    block = lax.axis_index(("xl", "y"))
    z = lax.axis_index("z")
    where = [z, x, lax.axis_index("y"), lax.axis_index(("xh", "core"))]
    where = jnp.stack(where).astype(jnp.int32)
    gain_one, bias_one, gain_two, bias_two = [
        v.reshape(1, WIDTH) for v in (ln1_gain, ln1_bias, ln2_gain, ln2_bias)
    ]

    main, feed = call(
        prepare_kernel,
        stay(w_query, w_key, w_value, w_out.T, w_up, w_down.T),
        [bf16(64, 384), bf16(64, 1152)],
    )
    main = [turn_x(main, k) for k in range(4)]
    feed = after(feed, main)
    main = place(main, [x ^ k for k in range(4)]).reshape(256, 384)
    main = spread(main, "z").reshape(WIDTH, 384)
    feed = [turn_y(feed, k) for k in range(4)]
    main = jnp.broadcast_to(main, (4, WIDTH, 384))
    gain_one = after(gain_one, main)
    wqkv = trade(main, "y")
    feed_rows, wo = call(
        feed_rows_kernel,
        after(feed, main),
        [away(bf16(64, 2 * FF_HALF)), bf16(64, HALF)],
        [where],
    )
    feed_weights = lax.all_gather(feed_rows, ("z", "xh", "xl"), axis=0, tiled=True)
    wo = place(ring_trade([wo] * 4, X), [lax.rem(x - k + 4, 4) for k in range(4)])
    wo = ring_trade([wo.reshape(256, HALF)] * 4, "z")
    wo = place(wo, [lax.rem(z - k + 4, 4) for k in range(4)]).reshape(WIDTH, HALF)
    wqkv = after(wqkv, wo)
    wo = (wo, (WIDTH, HALF), (0, 0))

    ends = jnp.cumsum(jnp.concatenate([lengths, core_swap(lengths)], axis=0), axis=1)

    def last_segment(which):
        return jnp.sum((which * BLOCK + BLOCK - 1 >= ends).astype(jnp.int32), axis=1)

    here = last_segment(block)
    before = jnp.where(block > 0, last_segment(block - 1), -1)
    zeros = jnp.zeros((2,), jnp.int32)
    flags = [(block >= k) & (last_segment(block - k) == before) for k in range(1, REACH + 1)]
    flags += [
        (block + k < 8) & (last_segment(block + k - 1) == here) for k in range(1, REACH + 1)
    ]
    rest = [zeros + block * BLOCK, before, here, zeros] + [f.astype(jnp.int32) for f in flags]
    info = jnp.concatenate([ends, jnp.stack(rest, axis=1)], axis=1)

    first_in, grad_low = call(
        first_norm_kernel, stay(inputs, cotangent, gain_one, bias_one), [SEND, away(SEND)]
    )
    first = [first_in, core_swap(first_in)]
    grads = [grad_low, core_swap(grad_low)]

    queries, keys, values, state = enter(info, first, wqkv)
    queries, keys, values = stay(queries, keys, values)
    far = tensor_shift(state, 4)
    states = call(relay_kernel, [state, far], [STATE] * 3, [where])
    states = [ring_shift(states[k - 1], "y", k) for k in (1, 2, 3)] + [far]
    numer, denom = attention_call(
        inner_kernel, info, [queries, keys, values], [WIDE32, WIDE32]
    )
    attended, low, inverse, own, send = attention_call(
        join_kernel,
        info,
        [queries, numer, denom] + states,
        [away(WIDE32), away(WIDE16), away(WIDE32), OWN, SEND],
        [wo],
    )
    hidden, second_in = call(
        second_norm_kernel,
        stay(inputs, gain_two, bias_two) + [own, core_swap(send)],
        [away(OWN), SEND],
    )
    feed_grad, act, d_own, d_send = feed_forward(
        [second_in, core_swap(second_in)] + stay(*grads), feed_weights
    )
    d_hidden, branch_low, sums = call(
        second_back_kernel,
        stay(hidden, gain_two, d_own) + [core_swap(d_send)] + stay(cotangent),
        [away(OWN), SEND, f32(8, WIDTH)],
    )
    branch = [branch_low, core_swap(branch_low)]

    feed_grad = lax.psum_scatter(feed_grad, "z", scatter_dimension=0, tiled=True)

    back_state, scaled, shift = attention_call(
        back_state_kernel,
        info,
        [queries, values] + stay(attended, inverse) + branch,
        [STATE, WIDE16, WIDE32],
        [wo],
    )
    back_states = [tensor_shift(back_state, -k) for k in range(1, REACH + 1)]
    d_queries, d_key, d_value = attention_call(
        back_inner_kernel,
        info,
        [queries, keys, values, scaled, shift] + stay(*states),
        [WIDE16, WIDE32, WIDE32],
    )
    d_keys, d_values, own, send = attention_call(
        back_join_kernel,
        info,
        [keys, values, d_queries, d_key, d_value] + back_states,
        [WIDE16, WIDE16, away(OWN), SEND],
        [(wqkv, (4, WIDTH, 384), (0, 0, 0))],
    )
    (gqk,) = call(
        query_grad_kernel,
        first + [d_queries, d_keys],
        [away(bf16(4, WIDTH, 256))],
        limit=20,
    )
    d_values = after(d_values, gqk)
    gqk = trade(gqk, "y")
    gvo = call(
        value_grad_kernel,
        first + branch + [d_values] + stay(low),
        [away(bf16(256, WIDTH))] * 4,
        [where],
        limit=20,
        scratch=[pltpu.VMEM((WIDTH, TOKENS2), BF)] * 2,
    )
    sums = after(sums, gvo)
    gvo = ring_trade(gvo, X)
    grad_inputs, packed = call(
        first_back_kernel,
        stay(inputs, gain_one, d_hidden, own) + [core_swap(send), sums],
        [away(OWN), bf16(16, WIDTH)],
    )
    r_own, r_send = result_parts(after(act, packed), feed_weights)
    packed = after(packed, r_own)
    (norms,) = call(norm_core_kernel, [packed, core_swap(packed)], [bf16(16, WIDTH)])
    norms = spread(after(norms, gqk), "y")

    (cut,) = call(main_cut_kernel, [gqk, norms] + stay(*gvo), [bf16(4, 576, 256)])
    feed_grad = call(
        feed_cut_kernel,
        stay(after(feed_grad, cut)),
        [bf16(64, FF_HALF)] * 4 + [bf16(BLOCK, HALF)] * 4,
        [where],
    )
    cut = after(trade(cut, "z"), feed_grad)
    downs, ups = ring_trade(feed_grad[4:], "y"), ring_trade(feed_grad[:4], X)

    sent = call(
        main_turn_kernel, [cut] + downs, [bf16(96, 768)] * 4 + [bf16(64, WIDTH)], [where]
    )
    turned = [turn_x(sent[k], k, True) for k in range(4)]
    ups = after(ups, turned[:2])
    grad_query, grad_key, grad_down, *norms = call(
        main_end_kernel,
        turned,
        [f32(64, 128)] * 2 + [f32(64, 512)] + [f32(1, WIDTH)] * 4,
        [where],
    )
    sent = call(feed_turn_kernel, ups + [sent[4]], [bf16(64, 768)] * 4, [where])
    grad_up, grad_value, grad_out = call(
        feed_end_kernel,
        [turn_y(sent[k], k) for k in range(4)],
        [f32(64, 512)] + [f32(64, 128)] * 2,
    )
    norms = [v.reshape(WIDTH) for v in norms]
    result = hidden + (r_own + core_swap(after(r_send, gqk)).astype(F32))
    return (
        result,
        grad_inputs,
        norms[0],
        norms[1],
        norms[2],
        norms[3],
        grad_query,
        grad_key,
        grad_value,
        grad_out.T,
        grad_up,
        grad_down.T,
    )


def solution(mesh):
    axes = ("z", "xh", "core", "xl", "y")
    split = Mesh(mesh.devices.reshape(4, 2, 2, 2, 4), axes)
    dp, tensor = ("z", "xh", "core"), ("xl", "y")
    tokens, rows, cols = P(axes, None), P(dp, tensor), P(tensor, dp)
    in_specs = (tokens, P(dp, None), P(), P(), P(), P(), rows, rows, rows, cols, rows, cols, tokens)
    out_specs = (tokens, tokens, P(), P(), P(), P(), rows, rows, rows, cols, rows, cols)
    return jax.shard_map(
        local, mesh=split, in_specs=in_specs, out_specs=out_specs, check_vma=False
    )
```
